128 devices in a mesh: dp: 32 (over z, x, y_lo), seq: 4 (over y_hi, core).
Axes of the slice: x: 4, y: 4 (y_hi: 2, y_lo: 2; y = y_hi * 2 + y_lo), z: 4, core: 2. Of those that a mesh axis runs over, the one named last changes fastest.
Arguments:
- clip_rows: bfloat16 [32768, 3072], P(('dp', 'seq')), may hold values from -24 to 24
- velocity_target: bfloat16 [32768, 3072], P(('dp', 'seq')), may hold values from -24 to 24
- plan: int32 [32, 4, 32], replicated, may hold values from 0 to 2, as said below
- segment_ids: int32 [32, 1024], P('dp'), may hold values from 0 to 1, as said below
- reward_levels: int32 [32, 2], P('dp'), may hold values from 1 to 8
- w_qkv: bfloat16 [3072, 4608], P('dp', 'seq'), may hold values from -0.109375 to 0.109375
- w_out: bfloat16 [3072, 1536], P('dp', 'seq'), may hold values from -0.15625 to 0.15625
Outputs:
- grad_qkv: float32 [3072, 4608], P('dp', 'seq')
- grad_out: float32 [3072, 1536], P('dp', 'seq')
The draws below stay inside these ranges and needn't reach their ends.
Inputs may be any that keep to these rules, and one draw needn't show every extreme that they name: `plan`: for every g and s the counts over t sum to 32, and for every t and s the counts over g sum to 32; some count equals 2. `segment_ids`: in each group the rows before a boundary, which lies between 256 and 768, are piece 0 (the tail of an earlier clip) and the rest piece 1 (the start of the next clip).
All inputs are finite; a program needn't handle non-finite values.
Results may differ from the reference program's by a relative error of at most 0.03.
Values may be sent and summed in bfloat16 or wider, within the bound.
A program may use at most 128 MiB of HBM per device.

```python
import math
import jax
import jax.numpy as jnp
from jax import lax

D = 3072
HEADS = 12
HD = 128
SEGS = 2
GROUPS = 32
SHARDS = 4
BLOCK_ROWS = 8
GROUP_ROWS = 1024
TOKENS = 32768


def plan_one(sub_key):
    first, second, third, fourth = jax.random.split(sub_key, 4)
    perm_dest = jax.random.permutation(first, GROUPS).astype(jnp.int32)
    perm_source = jax.random.permutation(second, GROUPS).astype(jnp.int32)
    offset_rank = jax.random.permutation(third, GROUPS).astype(jnp.int32)
    doubled = jax.random.randint(fourth, (), 1, GROUPS // 2 + 1).astype(jnp.int32)
    upper = (offset_rank < doubled).astype(jnp.int32)
    lower = ((offset_rank >= doubled) & (offset_rank < 2 * doubled)).astype(jnp.int32)
    multiple = 1 + upper - lower
    inverse_dest = jnp.zeros((GROUPS,), jnp.int32).at[perm_dest].set(jnp.arange(GROUPS, dtype=jnp.int32))
    offset_index = (inverse_dest[None, :] - perm_source[:, None]) % GROUPS
    return multiple[offset_index]


def draw_plan(key, part):
    key = jax.random.fold_in(key, 11)
    shard_keys = jax.random.split(key, SHARDS)
    plans = jax.vmap(plan_one)(shard_keys)
    return jnp.transpose(plans, (1, 0, 2)).astype(jnp.int32)


def draw_segment_ids(key, part):
    key = jax.random.fold_in(key, 13)
    boundary = jax.random.randint(key, (GROUPS,), GROUP_ROWS // 4, 3 * GROUP_ROWS // 4 + 1).astype(jnp.int32)
    positions = jnp.arange(GROUP_ROWS, dtype=jnp.int32)
    return (positions[None, :] >= boundary[:, None]).astype(jnp.int32)


def plant(result, key, low, largest):
    index_at = [jax.random.randint(jax.random.fold_in(key, axis), (), 0, length) for axis, length in enumerate(result.shape)]
    main_axis = result.shape.index(max(result.shape))
    neighbour = index_at[:main_axis] + [(index_at[main_axis] + 1) % result.shape[main_axis]] + index_at[main_axis + 1:]
    return result.at[tuple(index_at)].set(low).at[tuple(neighbour)].set(largest)


def strengthened(result, rng, source, target, shards_of, factor):
    owner, partner = [(jnp.arange(result.shape[dim]) // (result.shape[dim] // shards_of)).reshape([-1 if axis == dim else 1 for axis in range(result.ndim)]) for dim in (source, target)]
    chosen = jax.random.permutation(rng, shards_of)[partner]
    strong = (owner == chosen) | (owner == (partner + shards_of // 2) % shards_of)
    return jnp.where(strong, factor * result, result)


def shard_levels(rng, dims, pieces, smallest, largest):
    gain = 1.0
    for dim, blocks in pieces:
        draws = jax.random.uniform(jax.random.fold_in(jax.random.fold_in(rng, 6), dim), (blocks,), jnp.float32, smallest / len(pieces), largest / len(pieces))
        gain = gain * jnp.repeat(jnp.exp(draws), dims[dim] // blocks).reshape((-1,) + (1,) * (len(dims) - 1 - dim))
    return gain


def bell_draw(stream_key, extent, scale, bound, pieces=(), held_as=jnp.bfloat16):
    level = shard_levels(stream_key, extent, pieces, -0.22, 0.18) if pieces else 1.0
    array = jax.random.normal(stream_key, extent, jnp.float32) * scale * level
    return jnp.minimum(jnp.maximum(array, -bound), bound).astype(held_as)


def gaussian_with(key, shape, deviation, most, pieces, heavy, kind=jnp.bfloat16):
    values = deviation * jax.random.normal(key, shape, jnp.float32)
    if pieces:
        values = values * shard_levels(key, shape, pieces, -0.22, 0.18)
    return jnp.clip(strengthened(values, jax.random.fold_in(key, 3), *heavy), -most, most).astype(kind)


def setup_inputs(seed: int = 0) -> dict:
    streams_of = jax.random.split(jax.random.key(seed), 8)
    return {
        "clip_rows": gaussian_with(streams_of[0], (TOKENS, D), 1.0, 24.0, ((0, 128),), (0, 1, 128, 5.5)),
        "velocity_target": gaussian_with(streams_of[1], (TOKENS, D), 1.0, 24.0, ((0, 128),), (0, 1, 128, 5.5)),
        "plan": draw_plan(jax.random.fold_in(streams_of[7], 71), 0),
        "segment_ids": draw_segment_ids(jax.random.fold_in(streams_of[7], 71), 0),
        "reward_levels": plant(jax.random.randint(streams_of[4], (GROUPS, SEGS), 1, 9), jax.random.fold_in(streams_of[4], 1), 1, 8).astype(jnp.int32),
        "w_qkv": bell_draw(streams_of[5], (D, HEADS * 3 * HD), D ** -0.5, 0.109375, ((0, 32), (1, 4))),
        "w_out": bell_draw(streams_of[6], (D, HEADS * HD), (HEADS * HD) ** -0.5, 0.15625, ((0, 32), (1, 4))),
    }


epsilon = 1e-06

def rounded(value):
    return lax.optimization_barrier(value.astype(jnp.bfloat16))

def rebalance(source_rows, plan):
    blocks = source_rows.reshape(GROUPS, SHARDS, GROUPS, BLOCK_ROWS, D)
    send_start = (jnp.cumsum(plan, axis=2) - plan).astype(jnp.int32)
    arriving = jnp.transpose(plan, (2, 1, 0))
    arriving_end = jnp.cumsum(arriving, axis=2).astype(jnp.int32)
    slot_ids = jnp.arange(GROUPS, dtype=jnp.int32)
    source_group = lax.optimization_barrier(jnp.sum((arriving_end[:, :, None, :] <= slot_ids[None, None, :, None]).astype(jnp.int32), axis=3)).astype(jnp.int32)
    arriving_start = jnp.take_along_axis((arriving_end - arriving).astype(jnp.int32), source_group, axis=2).astype(jnp.int32)
    shard_ids = jnp.arange(SHARDS, dtype=jnp.int32)[None, :, None]
    group_ids = jnp.arange(GROUPS, dtype=jnp.int32)[:, None, None]
    source_block = (send_start[source_group, shard_ids, group_ids] + slot_ids[None, None, :] - arriving_start).astype(jnp.int32)
    moved = blocks[source_group, shard_ids, source_block]
    return moved.reshape(GROUPS, GROUP_ROWS, D)

def mixdot(form, left, right):
    return jnp.einsum(form, left.astype(jnp.float32), right.astype(jnp.float32), precision=lax.Precision.HIGHEST)

def group_grads(rows_in, target_in, segment_row, level_row, w_qkv, w_out):
    rows = rows_in.shape[0]
    projected = jnp.dot(rows_in, w_qkv, preferred_element_type=jnp.float32).reshape(rows, HEADS, 3, HD)
    query_raw = projected[:, :, 0]
    key_raw = projected[:, :, 1]
    value_raw = projected[:, :, 2]
    query_factor = lax.rsqrt(lax.optimization_barrier(jnp.mean(query_raw * query_raw, axis=-1, keepdims=True)) + epsilon)
    key_factor = lax.rsqrt(lax.optimization_barrier(jnp.mean(key_raw * key_raw, axis=-1, keepdims=True)) + epsilon)
    query_norm = query_raw * query_factor
    key_norm = key_raw * key_factor
    query_half = rounded(query_norm)
    key_half = rounded(key_norm)
    value_half = rounded(value_raw)
    same_segment = segment_row[:, None] == segment_row[None, :]
    scores = mixdot('qhe,khe->hqk', query_half, key_half) / math.sqrt(HD)
    expd = jnp.where(same_segment[None], jnp.exp(scores), jnp.float32(0.0))
    attention_probs = expd / lax.optimization_barrier(jnp.sum(expd, axis=-1, keepdims=True))
    probs_half = rounded(attention_probs)
    mixed = rounded(mixdot('hqk,khe->qhe', probs_half, value_half)).reshape(rows, HEADS * HD)
    per_shard = HEADS * HD // SHARDS
    prediction = rows_in.astype(jnp.float32)
    for shard in range(SHARDS):
        lower = shard * per_shard
        partial_term = jnp.dot(mixed[:, lower:lower + per_shard], w_out[:, lower:lower + per_shard].T, preferred_element_type=jnp.float32)
        prediction = prediction + rounded(partial_term).astype(jnp.float32)
    clip_index = jnp.arange(SEGS, dtype=jnp.int32)
    row_weight = lax.optimization_barrier(jnp.sum(jnp.where(segment_row[:, None] == clip_index[None, :], level_row.astype(jnp.float32)[None, :] / 8.0, jnp.float32(0.0)), axis=1))
    pred_grad = (row_weight[:, None] * (prediction - target_in.astype(jnp.float32)) / math.sqrt(TOKENS)).astype(jnp.bfloat16)
    out_grad = rounded(jnp.dot(pred_grad, w_out, preferred_element_type=jnp.float32)).reshape(rows, HEADS, HD)
    value_grad = mixdot('hqk,qhe->khe', probs_half, out_grad)
    prob_grad = mixdot('qhe,khe->hqk', out_grad, value_half)
    delta = lax.optimization_barrier(jnp.sum(attention_probs * prob_grad, axis=-1, keepdims=True))
    score_grad = rounded(attention_probs * (prob_grad - delta) / math.sqrt(HD))
    query_grad = mixdot('hqk,khe->qhe', score_grad, key_half)
    key_grad = mixdot('hqk,qhe->khe', score_grad, query_half)
    query_raw_grad = query_factor * (query_grad - query_norm * lax.optimization_barrier(jnp.mean(query_grad * query_norm, axis=-1, keepdims=True)))
    key_raw_grad = key_factor * (key_grad - key_norm * lax.optimization_barrier(jnp.mean(key_grad * key_norm, axis=-1, keepdims=True)))
    projected_grad = jnp.stack([query_raw_grad, key_raw_grad, value_grad], axis=2).reshape(rows, HEADS * 3 * HD).astype(jnp.bfloat16)
    qkv_term = jnp.dot(rows_in.T, projected_grad, preferred_element_type=jnp.float32)
    out_term = jnp.dot(pred_grad.T, mixed, preferred_element_type=jnp.float32)
    return (qkv_term, out_term)

def reference(clip_rows, velocity_target, plan, segment_ids, reward_levels, w_qkv, w_out):
    rows_moved = rebalance(clip_rows, plan)
    target_moved = rebalance(velocity_target, plan)

    def accumulate(carry, items):
        qkv_term, out_term = group_grads(items[0], items[1], items[2], items[3], w_qkv, w_out)
        return ((carry[0] + rounded(qkv_term).astype(jnp.float32), carry[1] + rounded(out_term).astype(jnp.float32)), None)
    start = (jnp.zeros((D, HEADS * 3 * HD), jnp.float32), jnp.zeros((D, HEADS * HD), jnp.float32))
    totals, _ = lax.scan(accumulate, start, (rows_moved, target_moved, segment_ids, reward_levels))
    return (totals[0], totals[1])
```

```python
import math

import jax
import jax.numpy as jnp
from jax import lax
from jax.experimental import pallas as pl
from jax.experimental.pallas import tpu as pltpu
from jax.sharding import PartitionSpec as P

HD = 128
CAP = 2
MESH = pl.DeviceIdType.MESH
VMEM_LIMIT = 60 * 1024 * 1024

epsilon = 1e-06


def my_place():
    dp = lax.axis_index("dp")
    seq = lax.axis_index("seq")
    return (dp // 8, (dp // 2) % 4, dp % 2, seq // 2, seq % 2)


def device(place):
    z, x, y, a, c = place
    return {"dp": z * 8 + x * 2 + y, "seq": a * 2 + c}


def moved(place, axis, by):
    place = list(place)
    size = (4, 4, 2, 2, 2)[axis]
    place[axis] = (place[axis] + by + size) % size
    return tuple(place)


Z, X, Y, A, C = range(5)


class Copies:
    def __init__(self, send_sem, recv_sem):
        self.send_sem, self.recv_sem, self.used = send_sem, recv_sem, 0
        self.started = []

    def start(self, src, dst, to):
        copy = pltpu.make_async_remote_copy(
            src_ref=src,
            dst_ref=dst,
            send_sem=self.send_sem.at[self.used],
            recv_sem=self.recv_sem.at[self.used],
            device_id=device(to),
            device_id_type=MESH,
        )
        self.used += 1
        copy.start()
        self.started.append(copy)
        return copy

    def finish(self):
        for copy in self.started:
            copy.wait_send()


def greet(places):
    barrier = pltpu.get_barrier_semaphore()
    for place in places:
        pl.semaphore_signal(barrier, inc=1, device_id=device(place), device_id_type=MESH)
    pl.semaphore_wait(barrier, len(places))


def dp_peer(place, k, sign):
    z, x, y, a, c = place
    dz, dx, dy = k // 8, (k // 2) % 4, k % 2
    return ((z + sign * dz + 4) % 4, (x + sign * dx + 4) % 4, (y + sign * dy + 2) % 2, a, c)


def ring_gather_start(copies, me, axis, part):
    own = me[axis]
    up, down = moved(me, axis, 1), moved(me, axis, -1)
    first_up = copies.start(part(own, 0), part(own, 0), up)
    first_down = copies.start(part(own, 1), part(own, 1), down)
    second_up = copies.start(part(own, 1), part(own, 1), up)
    second_down = copies.start(part(own, 0), part(own, 0), down)
    return first_up, first_down, second_up, second_down


def ring_gather_forward(copies, me, axis, part, sent):
    up, down = moved(me, axis, 1), moved(me, axis, -1)
    below, above = down[axis], up[axis]
    sent[0].wait_recv()
    third_up = copies.start(part(below, 0), part(below, 0), up)
    sent[1].wait_recv()
    third_down = copies.start(part(above, 1), part(above, 1), down)
    return sent[2], sent[3], third_up, third_down


def gather_kernel(packed, shard, chosen, x_full, w_full, received, own_rows, a2a_send, a2a_recv, send_sem, recv_sem, local_sem):
    me = my_place()
    z, x, y, a, c = me
    dp = lax.axis_index("dp")
    seq = lax.axis_index("seq")
    rows = own_rows.shape[0]
    other_chip, other_core = moved(me, A, 1), moved(me, C, 1)
    barrier = pltpu.get_barrier_semaphore()

    @pl.loop(1, 32)
    def _(k):
        pl.semaphore_signal(barrier, inc=1, device_id=device(dp_peer(me, k, 1)), device_id_type=MESH)

    for place in (other_chip, other_core):
        pl.semaphore_signal(barrier, inc=1, device_id=device(place), device_id_type=MESH)
    pl.semaphore_wait(barrier, 33)

    copies = Copies(send_sem, recv_sem)
    own_shard = pltpu.make_async_copy(shard, w_full.at[z, x, y], local_sem.at[0])
    own_shard.start()
    across = copies.start(shard, w_full.at[z, x, y], moved(me, Y, 1))

    def block_copy(k):
        to = dp_peer(me, k, 1)
        return pltpu.make_async_remote_copy(
            src_ref=packed.at[device(to)["dp"]],
            dst_ref=received.at[dp],
            send_sem=a2a_send.at[k],
            recv_sem=a2a_recv.at[k],
            device_id=device(to),
            device_id_type=MESH,
        )

    @pl.loop(1, 32)
    def _(k):
        block_copy(k).start()

    own_block = pltpu.make_async_copy(packed.at[dp], received.at[dp], local_sem.at[1])
    own_block.start()

    own_shard.wait()
    across.wait_recv()

    def near(half):
        if half == 0:
            return lambda at, which: w_full.at[at, x, which, 0]
        return lambda at, which: w_full.at[z, at, which, 1]

    def far(half):
        if half == 0:
            return lambda at, which: w_full.at[pl.ds(2 * which, 2), at, :, 0]
        return lambda at, which: w_full.at[at, pl.ds(2 * which, 2), :, 1]

    near_axis, far_axis = (Z, X), (X, Z)
    sent = [ring_gather_start(copies, me, near_axis[half], near(half)) for half in (0, 1)]
    rest = [ring_gather_forward(copies, me, near_axis[half], near(half), sent[half]) for half in (0, 1)]
    for half in (0, 1):
        for copy in rest[half]:
            copy.wait_recv()
    sent = [ring_gather_start(copies, me, far_axis[half], far(half)) for half in (0, 1)]

    own_block.wait()

    @pl.loop(1, 32)
    def _(k):
        block_copy(k).wait_recv()

    width = own_rows.shape[1]
    tile = 512

    @pl.loop(0, width // tile)
    def _(t):
        columns = pl.ds(pl.multiple_of(t * tile, tile), tile)
        blocks = received[:, :, columns].reshape(rows * CAP, tile)
        own_rows[:, columns] = jnp.dot(chosen[...], blocks, preferred_element_type=jnp.float32).astype(jnp.bfloat16)

    def rows_of(place):
        return pl.ds(pl.multiple_of(device(place)["seq"] * rows, rows), rows)

    to_chip = copies.start(own_rows, x_full.at[rows_of(me)], other_chip)
    to_core = copies.start(own_rows, x_full.at[rows_of(me)], other_core)
    own_place = pltpu.make_async_copy(own_rows, x_full.at[rows_of(me)], local_sem.at[2])
    own_place.start()

    rest = [ring_gather_forward(copies, me, far_axis[half], far(half), sent[half]) for half in (0, 1)]
    to_chip.wait_recv()
    passed = copies.start(x_full.at[rows_of(other_chip)], x_full.at[rows_of(other_chip)], other_core)
    to_core.wait_recv()
    passed.wait_recv()
    for half in (0, 1):
        for copy in rest[half]:
            copy.wait_recv()
    own_place.wait()

    @pl.loop(1, 32)
    def _(k):
        block_copy(k).wait_send()

    copies.finish()


def gather_all(packed, shard, chosen):
    rows = chosen.shape[0]
    width = packed.shape[2]
    w_cols = shard.shape[1]
    x_full, w_full = pl.pallas_call(
        gather_kernel,
        out_shape=(
            jax.ShapeDtypeStruct((rows * 4, width), jnp.bfloat16),
            jax.ShapeDtypeStruct((4, 4, 2, 2, 48, w_cols), jnp.bfloat16),
        ),
        in_specs=[
            pl.BlockSpec(memory_space=pl.ANY),
            pl.BlockSpec(memory_space=pl.ANY),
            pl.BlockSpec(memory_space=pltpu.VMEM),
        ],
        out_specs=(pl.BlockSpec(memory_space=pl.ANY), pl.BlockSpec(memory_space=pl.ANY)),
        scratch_shapes=[
            pltpu.VMEM(packed.shape, jnp.bfloat16),
            pltpu.VMEM((rows, width), jnp.bfloat16),
            pltpu.SemaphoreType.DMA((32,)),
            pltpu.SemaphoreType.DMA((32,)),
            pltpu.SemaphoreType.DMA((28,)),
            pltpu.SemaphoreType.DMA((28,)),
            pltpu.SemaphoreType.DMA((3,)),
        ],
        compiler_params=pltpu.CompilerParams(collective_id=1, has_side_effects=True, vmem_limit_bytes=VMEM_LIMIT),
        name="gather_rows_weights",
    )(packed, shard.reshape(2, 48, w_cols), chosen)
    return x_full, w_full.reshape(3072, w_cols)


CHUNKS = 4


def residual_kernel(packed, chosen, partial, x_own, weight, d_full, received, target, from_core, summed, from_chip, a2a_send, a2a_recv, send_sem, recv_sem, local_sem):
    me = my_place()
    dp = lax.axis_index("dp")
    rows, width = x_own.shape
    other_chip, other_core = moved(me, A, 1), moved(me, C, 1)
    barrier = pltpu.get_barrier_semaphore()

    @pl.loop(1, 32)
    def _(k):
        pl.semaphore_signal(barrier, inc=1, device_id=device(dp_peer(me, k, 1)), device_id_type=MESH)

    for place in (other_chip, other_core):
        pl.semaphore_signal(barrier, inc=1, device_id=device(place), device_id_type=MESH)
    pl.semaphore_wait(barrier, 33)

    copies = Copies(send_sem, recv_sem)
    step = rows // CHUNKS

    def rows_of(place, chunk):
        return pl.ds(pl.multiple_of(device(place)["seq"] * rows + chunk * step, step), step)

    core_first, core_second = [], []
    for chunk in range(CHUNKS):
        core_first.append(copies.start(
            partial.at[rows_of(moved(other_core, A, 1), chunk)], from_core.at[0, pl.ds(chunk * step, step)], other_core))
    for chunk in range(CHUNKS):
        core_second.append(copies.start(
            partial.at[rows_of(other_core, chunk)], from_core.at[1, pl.ds(chunk * step, step)], other_core))

    def block_copy(k):
        to = dp_peer(me, k, 1)
        return pltpu.make_async_remote_copy(
            src_ref=packed.at[device(to)["dp"]],
            dst_ref=received.at[dp],
            send_sem=a2a_send.at[k],
            recv_sem=a2a_recv.at[k],
            device_id=device(to),
            device_id_type=MESH,
        )

    @pl.loop(1, 32)
    def _(k):
        block_copy(k).start()

    own_block = pltpu.make_async_copy(packed.at[dp], received.at[dp], local_sem.at[0])
    own_block.start()

    chip_sums = []
    for chunk in range(CHUNKS):
        core_first[chunk].wait_recv()
        at = pl.ds(chunk * step, step)
        summed[at] = (partial[rows_of(other_chip, chunk)].astype(jnp.float32) + from_core[0, at].astype(jnp.float32)).astype(jnp.bfloat16)
        chip_sums.append(copies.start(summed.at[at], from_chip.at[at], other_chip))

    own_block.wait()

    @pl.loop(1, 32)
    def _(k):
        block_copy(k).wait_recv()

    tile = 512

    @pl.loop(0, width // tile)
    def _(t):
        columns = pl.ds(pl.multiple_of(t * tile, tile), tile)
        blocks = received[:, :, columns].reshape(rows * CAP, tile)
        target[:, columns] = jnp.dot(chosen[...], blocks, preferred_element_type=jnp.float32).astype(jnp.bfloat16)

    to_chip, to_core, passed = [], [], []
    for chunk in range(CHUNKS):
        core_second[chunk].wait_recv()
        chip_sums[chunk].wait_recv()
        at = pl.ds(chunk * step, step)
        mine = rows_of(me, chunk)
        prediction = (
            x_own[at].astype(jnp.float32)
            + (partial[mine].astype(jnp.float32) + from_core[1, at].astype(jnp.float32) + from_chip[at].astype(jnp.float32))
        )
        d_full[mine] = (weight[at] * (prediction - target[at].astype(jnp.float32))).astype(jnp.bfloat16)
        to_chip.append(copies.start(d_full.at[mine], d_full.at[mine], other_chip))
        to_core.append(copies.start(d_full.at[mine], d_full.at[mine], other_core))
    for chunk in range(CHUNKS):
        to_chip[chunk].wait_recv()
        theirs = rows_of(other_chip, chunk)
        passed.append(copies.start(d_full.at[theirs], d_full.at[theirs], other_core))
    for chunk in range(CHUNKS):
        to_core[chunk].wait_recv()
        passed[chunk].wait_recv()

    @pl.loop(1, 32)
    def _(k):
        block_copy(k).wait_send()

    copies.finish()


def residual(packed, chosen, partial, x_own, weight):
    rows, width = x_own.shape
    return pl.pallas_call(
        residual_kernel,
        out_shape=jax.ShapeDtypeStruct(partial.shape, jnp.bfloat16),
        in_specs=[pl.BlockSpec(memory_space=pl.ANY)] + [pl.BlockSpec(memory_space=pltpu.VMEM)] * 4,
        out_specs=pl.BlockSpec(memory_space=pltpu.VMEM),
        scratch_shapes=[
            pltpu.VMEM(packed.shape, jnp.bfloat16),
            pltpu.VMEM((rows, width), jnp.bfloat16),
            pltpu.VMEM((2, rows, width), jnp.bfloat16),
            pltpu.VMEM((rows, width), jnp.bfloat16),
            pltpu.VMEM((rows, width), jnp.bfloat16),
            pltpu.SemaphoreType.DMA((32,)),
            pltpu.SemaphoreType.DMA((32,)),
            pltpu.SemaphoreType.DMA((6 * CHUNKS,)),
            pltpu.SemaphoreType.DMA((6 * CHUNKS,)),
            pltpu.SemaphoreType.DMA((1,)),
        ],
        compiler_params=pltpu.CompilerParams(collective_id=2, has_side_effects=True, vmem_limit_bytes=VMEM_LIMIT),
        name="residual_gradient",
    )(packed, chosen, partial, x_own, weight)


def added(*values):
    total = values[0].astype(jnp.float32)
    for value in values[1:]:
        total = total + value.astype(jnp.float32)
    return total


def reduce_start(copies, me, axis, block, got):
    up, down = moved(me, axis, 1), moved(me, axis, -1)
    opposite = moved(me, axis, 2)[axis]
    far_up = copies.start(block(opposite, 0), got(0), up)
    far_down = copies.start(block(opposite, 1), got(1), down)
    near_up = copies.start(block(up[axis], 1), got(2), up)
    near_down = copies.start(block(down[axis], 0), got(3), down)
    return far_up, far_down, near_up, near_down


def reduce_pass(copies, me, axis, block, got, sums, sent, add):
    up, down = moved(me, axis, 1), moved(me, axis, -1)
    sent[0].wait_recv()
    add(sums(0), [block(up[axis], 0), got(0)])
    sum_up = copies.start(sums(0), got(4), up)
    sent[1].wait_recv()
    add(sums(1), [block(down[axis], 1), got(1)])
    sum_down = copies.start(sums(1), got(5), down)
    return sent[2], sent[3], sum_up, sum_down


def reduce_end(me, axis, block, got, out, sent, add):
    sent[1].wait_recv()
    sent[2].wait_recv()
    add(out(0), [block(me[axis], 0), got(3), got(4)])
    sent[0].wait_recv()
    sent[3].wait_recv()
    add(out(1), [block(me[axis], 1), got(2), got(5)])


def add_rows(out, parts):
    lead = out.shape[:-2]
    count = math.prod(lead)

    @pl.loop(0, count)
    def _(i):
        index, rest = [], i
        for size in reversed(lead):
            index.insert(0, rest % size)
            rest = rest // size
        index = tuple(index)
        out[index] = added(*[part[index] for part in parts]).astype(out.dtype)


def scatter_kernel(grads, sums_out, got_far, sum_far, half_far, got_near, sum_near, half_near, got_last, send_sem, recv_sem):
    me = my_place()
    z, x, y, a, c = me
    greet([moved(me, Z, 1), moved(me, Z, -1), moved(me, X, 1), moved(me, X, -1), moved(me, Y, 1)])
    copies = Copies(send_sem, recv_sem)
    far_axis, near_axis = (X, Z), (Z, X)

    def far_block(half):
        if half == 0:
            return lambda at, which: grads.at[pl.ds(2 * which, 2), at, :, 0]
        return lambda at, which: grads.at[at, pl.ds(2 * which, 2), :, 1]

    def near_block(half):
        return lambda at, which: half_far.at[half, at, which]

    def slots(ref, half):
        return lambda j: ref.at[half, j]

    def far_out(half):
        return lambda which: half_far.at[half, pl.ds(2 * which, 2)]

    def near_out(half):
        return lambda which: half_near.at[half, pl.ds(which, 1)]

    def near_add(out, parts):
        out[...] = added(*[part[...] for part in parts]).astype(out.dtype).reshape(out.shape)

    sent = [reduce_start(copies, me, far_axis[h], far_block(h), slots(got_far, h)) for h in (0, 1)]
    sent = [reduce_pass(copies, me, far_axis[h], far_block(h), slots(got_far, h), slots(sum_far, h), sent[h], add_rows) for h in (0, 1)]
    for h in (0, 1):
        reduce_end(me, far_axis[h], far_block(h), slots(got_far, h), far_out(h), sent[h], add_rows)
    sent = [reduce_start(copies, me, near_axis[h], near_block(h), slots(got_near, h)) for h in (0, 1)]
    sent = [reduce_pass(copies, me, near_axis[h], near_block(h), slots(got_near, h), slots(sum_near, h), sent[h], near_add) for h in (0, 1)]
    for h in (0, 1):
        reduce_end(me, near_axis[h], near_block(h), slots(got_near, h), near_out(h), sent[h], near_add)
    last = [copies.start(half_near.at[h, 1 - y], got_last.at[h], moved(me, Y, 1)) for h in (0, 1)]
    for h in (0, 1):
        last[h].wait_recv()
        sums_out[h] = added(half_near[h, y], got_last[h])
    copies.finish()


def scatter(grads):
    cols = grads.shape[1]
    half = lambda *lead: pltpu.VMEM((2, *lead, 48, cols), jnp.bfloat16)
    sums = pl.pallas_call(
        scatter_kernel,
        out_shape=jax.ShapeDtypeStruct((2, 48, cols), jnp.float32),
        in_specs=[pl.BlockSpec(memory_space=pltpu.VMEM)],
        out_specs=pl.BlockSpec(memory_space=pltpu.VMEM),
        scratch_shapes=[
            half(6, 2, 2),
            half(2, 2, 2),
            half(4, 2),
            half(6),
            half(2),
            half(2),
            half(),
            pltpu.SemaphoreType.DMA((26,)),
            pltpu.SemaphoreType.DMA((26,)),
        ],
        compiler_params=pltpu.CompilerParams(collective_id=3, has_side_effects=True, vmem_limit_bytes=VMEM_LIMIT),
        name="scatter_gradients",
    )(grads.reshape(4, 4, 2, 2, 48, cols))
    return sums.reshape(96, cols)


def row_norm(values):
    factor = lax.rsqrt(jnp.mean(values * values, axis=-1, keepdims=True) + epsilon)
    return (values * factor, factor)


def spread(block_of, rows, columns):
    source = jnp.repeat(block_of, 8) * 8 + jnp.tile(jnp.arange(8, dtype=jnp.int32), rows // 8)
    source = jnp.where(jnp.repeat(block_of, 8) < 0, -1, source)
    return (source[:, None] == jnp.arange(columns, dtype=jnp.int32)[None, :]).astype(jnp.bfloat16)


def per_device(clip_rows, velocity_target, plan, segment_ids, reward_levels, w_qkv, w_out):
    groups = lax.axis_size("dp")
    shards = lax.axis_size("seq")
    group = lax.axis_index("dp")
    shard = lax.axis_index("seq")
    rows_dev, width = clip_rows.shape
    group_rows = rows_dev * shards
    counts = plan[group, shard]
    send_start = jnp.cumsum(counts) - counts
    slot_index = jnp.arange(CAP, dtype=jnp.int32)
    source_block = jnp.where(slot_index[None, :] < counts[:, None], send_start[:, None] + slot_index[None, :], -1).reshape(-1)
    pack = spread(source_block, rows_dev * CAP, rows_dev)

    def packed(source_rows):
        return jnp.dot(pack, source_rows, preferred_element_type=jnp.float32).astype(jnp.bfloat16).reshape(groups, CAP * 8, width)

    arriving = plan[:, shard, group]
    arriving_end = jnp.cumsum(arriving)
    slot_ids = jnp.arange(groups, dtype=jnp.int32)
    source_group = jnp.sum((arriving_end[None, :] <= slot_ids[:, None]).astype(jnp.int32), axis=1)
    arriving_start = (arriving_end - arriving)[source_group]
    flat_slot = source_group * CAP + slot_ids - arriving_start
    chosen = spread(flat_slot, rows_dev, rows_dev * CAP)

    group_x, weights = gather_all(packed(clip_rows), jnp.concatenate([w_qkv, w_out], axis=1), chosen)
    boundary = w_qkv.shape[1]
    qkv_full, out_full = weights[:, :boundary], weights[:, boundary:]
    projected = jnp.dot(group_x, qkv_full, preferred_element_type=jnp.float32)
    projected = projected.reshape(group_rows, -1, 3, HD)
    query_norm, query_factor = row_norm(projected[:, :, 0])
    key_norm, key_factor = row_norm(projected[:, :, 1])
    query_half = query_norm.astype(jnp.bfloat16)
    key_half = key_norm.astype(jnp.bfloat16)
    value_half = projected[:, :, 2].astype(jnp.bfloat16)
    local_heads = projected.shape[1]
    segment_row = segment_ids[0]
    same_segment = segment_row[:, None] == segment_row[None, :]
    scores = jnp.einsum(
        "qhe,khe->hqk", query_half, key_half, preferred_element_type=jnp.float32
    ) / math.sqrt(HD)
    expd = jnp.where(same_segment[None], jnp.exp(scores), jnp.float32(0.0))
    attention_probs = expd / jnp.sum(expd, axis=-1, keepdims=True)
    probs_half = attention_probs.astype(jnp.bfloat16)
    mixed = jnp.einsum("hqk,khe->qhe", probs_half, value_half, preferred_element_type=jnp.float32)
    mixed = mixed.astype(jnp.bfloat16).reshape(group_rows, local_heads * HD)
    partial_term = jnp.einsum("qc,dc->qd", mixed, out_full, preferred_element_type=jnp.float32).astype(jnp.bfloat16)
    clip_index = jnp.arange(reward_levels.shape[1], dtype=jnp.int32)
    levels = reward_levels[0].astype(jnp.float32) / 8.0
    own_segment = lax.dynamic_slice(segment_row, (shard * rows_dev,), (rows_dev,))
    row_weight = jnp.sum(
        jnp.where(own_segment[:, None] == clip_index[None, :], levels[None, :], jnp.float32(0.0)),
        axis=1,
        keepdims=True,
    )
    loss_scale = 1.0 / math.sqrt(rows_dev * groups * shards)
    own_x = lax.dynamic_slice(group_x, (shard * rows_dev, 0), (rows_dev, width))
    pred_grad = residual(packed(velocity_target), chosen, partial_term, own_x, row_weight * loss_scale)
    out_grad = jnp.dot(pred_grad, out_full, preferred_element_type=jnp.float32)
    out_grad = out_grad.astype(jnp.bfloat16).reshape(group_rows, local_heads, HD)
    value_grad = jnp.einsum(
        "hqk,qhe->khe", probs_half, out_grad, preferred_element_type=jnp.float32
    )
    prob_grad = jnp.einsum("qhe,khe->hqk", out_grad, value_half, preferred_element_type=jnp.float32)
    delta = jnp.sum(attention_probs * prob_grad, axis=-1, keepdims=True)
    score_grad = (attention_probs * (prob_grad - delta) / math.sqrt(HD)).astype(jnp.bfloat16)
    query_grad = jnp.einsum(
        "hqk,khe->qhe", score_grad, key_half, preferred_element_type=jnp.float32
    )
    key_grad = jnp.einsum(
        "hqk,qhe->khe", score_grad, query_half, preferred_element_type=jnp.float32
    )
    query_raw_grad = query_factor * (
        query_grad - query_norm * jnp.mean(query_grad * query_norm, axis=-1, keepdims=True)
    )
    key_raw_grad = key_factor * (
        key_grad - key_norm * jnp.mean(key_grad * key_norm, axis=-1, keepdims=True)
    )
    projected_grad = jnp.stack([query_raw_grad, key_raw_grad, value_grad], axis=2)
    projected_grad = projected_grad.reshape(group_rows, local_heads * 3 * HD).astype(jnp.bfloat16)
    qkv_part = jnp.einsum("qd,qc->dc", group_x, projected_grad, preferred_element_type=jnp.float32)
    out_part = jnp.einsum("qd,qc->dc", pred_grad, mixed, preferred_element_type=jnp.float32)
    summed_grads = scatter(jnp.concatenate([qkv_part, out_part], axis=1).astype(jnp.bfloat16))
    return (summed_grads[:, :boundary], summed_grads[:, boundary:])


def solution(mesh):
    return jax.shard_map(
        per_device,
        mesh=mesh,
        in_specs=(
            P(("dp", "seq"), None),
            P(("dp", "seq"), None),
            P(),
            P("dp", None),
            P("dp", None),
            P("dp", "seq"),
            P("dp", "seq"),
        ),
        out_specs=(P("dp", "seq"), P("dp", "seq")),
        check_vma=False,
    )
```

```python
import math

import jax
import jax.numpy as jnp
from jax import lax
from jax.experimental import pallas as pl
from jax.experimental.pallas import tpu as pltpu
from jax.sharding import PartitionSpec as P

HD = 128
CAP = 2
MESH = pl.DeviceIdType.MESH
VMEM_LIMIT = 60 * 1024 * 1024

epsilon = 1e-06


def my_place():
    dp = lax.axis_index("dp")
    seq = lax.axis_index("seq")
    return (dp // 8, (dp // 2) % 4, dp % 2, seq // 2, seq % 2)


def device(place):
    z, x, y, a, c = place
    return {"dp": z * 8 + x * 2 + y, "seq": a * 2 + c}


def moved(place, axis, by):
    place = list(place)
    size = (4, 4, 2, 2, 2)[axis]
    place[axis] = (place[axis] + by + size) % size
    return tuple(place)


Z, X, Y, A, C = range(5)


class Copies:
    def __init__(self, send_sem, recv_sem):
        self.send_sem, self.recv_sem, self.used = send_sem, recv_sem, 0
        self.started = []

    def start(self, src, dst, to):
        copy = pltpu.make_async_remote_copy(
            src_ref=src,
            dst_ref=dst,
            send_sem=self.send_sem.at[self.used],
            recv_sem=self.recv_sem.at[self.used],
            device_id=device(to),
            device_id_type=MESH,
        )
        self.used += 1
        copy.start()
        self.started.append(copy)
        return copy

    def finish(self):
        for copy in self.started:
            copy.wait_send()


def greet(places):
    barrier = pltpu.get_barrier_semaphore()
    for place in places:
        pl.semaphore_signal(barrier, inc=1, device_id=device(place), device_id_type=MESH)
    pl.semaphore_wait(barrier, len(places))


def dp_peer(place, k, sign):
    z, x, y, a, c = place
    dz, dx, dy = k // 8, (k // 2) % 4, k % 2
    return ((z + sign * dz + 4) % 4, (x + sign * dx + 4) % 4, (y + sign * dy + 2) % 2, a, c)


def ring_gather_start(copies, me, axis, part):
    own = me[axis]
    up, down = moved(me, axis, 1), moved(me, axis, -1)
    first_up = copies.start(part(own, 0), part(own, 0), up)
    first_down = copies.start(part(own, 1), part(own, 1), down)
    second_up = copies.start(part(own, 1), part(own, 1), up)
    second_down = copies.start(part(own, 0), part(own, 0), down)
    return first_up, first_down, second_up, second_down


def ring_gather_forward(copies, me, axis, part, sent):
    up, down = moved(me, axis, 1), moved(me, axis, -1)
    below, above = down[axis], up[axis]
    sent[0].wait_recv()
    third_up = copies.start(part(below, 0), part(below, 0), up)
    sent[1].wait_recv()
    third_down = copies.start(part(above, 1), part(above, 1), down)
    return sent[2], sent[3], third_up, third_down


def gather_kernel(packed, shard, chosen, x_full, w_full, received, own_rows, a2a_send, a2a_recv, send_sem, recv_sem, local_sem):
    me = my_place()
    z, x, y, a, c = me
    dp = lax.axis_index("dp")
    seq = lax.axis_index("seq")
    rows = own_rows.shape[0]
    other_chip, other_core = moved(me, A, 1), moved(me, C, 1)
    barrier = pltpu.get_barrier_semaphore()

    @pl.loop(1, 32)
    def _(k):
        pl.semaphore_signal(barrier, inc=1, device_id=device(dp_peer(me, k, 1)), device_id_type=MESH)

    for place in (other_chip, other_core):
        pl.semaphore_signal(barrier, inc=1, device_id=device(place), device_id_type=MESH)
    pl.semaphore_wait(barrier, 33)

    copies = Copies(send_sem, recv_sem)
    own_shard = pltpu.make_async_copy(shard, w_full.at[z, x, y], local_sem.at[0])
    own_shard.start()
    across = copies.start(shard, w_full.at[z, x, y], moved(me, Y, 1))

    def block_copy(k):
        to = dp_peer(me, k, 1)
        return pltpu.make_async_remote_copy(
            src_ref=packed.at[device(to)["dp"]],
            dst_ref=received.at[dp],
            send_sem=a2a_send.at[k],
            recv_sem=a2a_recv.at[k],
            device_id=device(to),
            device_id_type=MESH,
        )

    @pl.loop(1, 32)
    def _(k):
        block_copy(k).start()

    own_block = pltpu.make_async_copy(packed.at[dp], received.at[dp], local_sem.at[1])
    own_block.start()

    own_shard.wait()
    across.wait_recv()

    def near(half):
        if half == 0:
            return lambda at, which: w_full.at[at, x, which, 0]
        return lambda at, which: w_full.at[z, at, which, 1]

    def far(half):
        if half == 0:
            return lambda at, which: w_full.at[pl.ds(2 * which, 2), at, :, 0]
        return lambda at, which: w_full.at[at, pl.ds(2 * which, 2), :, 1]

    near_axis, far_axis = (Z, X), (X, Z)
    sent = [ring_gather_start(copies, me, near_axis[half], near(half)) for half in (0, 1)]
    rest = [ring_gather_forward(copies, me, near_axis[half], near(half), sent[half]) for half in (0, 1)]
    for half in (0, 1):
        for copy in rest[half]:
            copy.wait_recv()
    sent = [ring_gather_start(copies, me, far_axis[half], far(half)) for half in (0, 1)]

    own_block.wait()

    @pl.loop(1, 32)
    def _(k):
        block_copy(k).wait_recv()

    width = own_rows.shape[1]
    tile = 512

    @pl.loop(0, width // tile)
    def _(t):
        columns = pl.ds(pl.multiple_of(t * tile, tile), tile)
        blocks = received[:, :, columns].reshape(rows * CAP, tile)
        own_rows[:, columns] = jnp.dot(chosen[...], blocks, preferred_element_type=jnp.float32).astype(jnp.bfloat16)

    def rows_of(place):
        return pl.ds(pl.multiple_of(device(place)["seq"] * rows, rows), rows)

    to_chip = copies.start(own_rows, x_full.at[rows_of(me)], other_chip)
    to_core = copies.start(own_rows, x_full.at[rows_of(me)], other_core)
    own_place = pltpu.make_async_copy(own_rows, x_full.at[rows_of(me)], local_sem.at[2])
    own_place.start()

    rest = [ring_gather_forward(copies, me, far_axis[half], far(half), sent[half]) for half in (0, 1)]
    to_chip.wait_recv()
    passed = copies.start(x_full.at[rows_of(other_chip)], x_full.at[rows_of(other_chip)], other_core)
    to_core.wait_recv()
    passed.wait_recv()
    for half in (0, 1):
        for copy in rest[half]:
            copy.wait_recv()
    own_place.wait()

    @pl.loop(1, 32)
    def _(k):
        block_copy(k).wait_send()

    copies.finish()


def gather_all(packed, shard, chosen):
    rows = chosen.shape[0]
    width = packed.shape[2]
    w_cols = shard.shape[1]
    x_full, w_full = pl.pallas_call(
        gather_kernel,
        out_shape=(
            jax.ShapeDtypeStruct((rows * 4, width), jnp.bfloat16),
            jax.ShapeDtypeStruct((4, 4, 2, 2, 48, w_cols), jnp.bfloat16),
        ),
        in_specs=[
            pl.BlockSpec(memory_space=pl.ANY),
            pl.BlockSpec(memory_space=pl.ANY),
            pl.BlockSpec(memory_space=pltpu.VMEM),
        ],
        out_specs=(pl.BlockSpec(memory_space=pl.ANY), pl.BlockSpec(memory_space=pl.ANY)),
        scratch_shapes=[
            pltpu.VMEM(packed.shape, jnp.bfloat16),
            pltpu.VMEM((rows, width), jnp.bfloat16),
            pltpu.SemaphoreType.DMA((32,)),
            pltpu.SemaphoreType.DMA((32,)),
            pltpu.SemaphoreType.DMA((28,)),
            pltpu.SemaphoreType.DMA((28,)),
            pltpu.SemaphoreType.DMA((3,)),
        ],
        compiler_params=pltpu.CompilerParams(collective_id=1, has_side_effects=True, vmem_limit_bytes=VMEM_LIMIT),
        name="gather_rows_weights",
    )(packed, shard.reshape(2, 48, w_cols), chosen)
    return x_full, w_full.reshape(3072, w_cols)


CHUNKS = 4
HEADS = 3
QKV = HEADS * 3 * HD
OUT = HEADS * HD
EXP2_SCALE = math.log2(math.e) / math.sqrt(HD)


def nt(left, right):
    return lax.dot_general(left, right, (((1,), (1,)), ((), ())), preferred_element_type=jnp.float32)


def tn(left, right):
    return lax.dot_general(left, right, (((0,), (0,)), ((), ())), preferred_element_type=jnp.float32)


def nn(left, right):
    return jnp.dot(left, right, preferred_element_type=jnp.float32)


def forward_kernel(
    packed, chosen, x_full, w_full, mark_q, mark_k, x_own, weight,
    d_full, q_marked, k_marked, v_half, factors, inverse, mixed,
    projected, v_turned, partial, received, target, from_core, summed, from_chip,
    a2a_send, a2a_recv, send_sem, recv_sem, local_sem,
):
    me = my_place()
    dp = lax.axis_index("dp")
    rows, width = x_own.shape
    group_rows = x_full.shape[0]
    other_chip, other_core = moved(me, A, 1), moved(me, C, 1)
    barrier = pltpu.get_barrier_semaphore()

    @pl.loop(1, 32)
    def _(k):
        pl.semaphore_signal(barrier, inc=1, device_id=device(dp_peer(me, k, 1)), device_id_type=MESH)

    for place in (other_chip, other_core):
        pl.semaphore_signal(barrier, inc=1, device_id=device(place), device_id_type=MESH)
    pl.semaphore_wait(barrier, 33)

    copies = Copies(send_sem, recv_sem)
    step = rows // CHUNKS

    def rows_of(place, chunk):
        return pl.ds(pl.multiple_of(device(place)["seq"] * rows + chunk * step, step), step)

    def block_copy(k):
        to = dp_peer(me, k, 1)
        return pltpu.make_async_remote_copy(
            src_ref=packed.at[device(to)["dp"]],
            dst_ref=received.at[dp],
            send_sem=a2a_send.at[k],
            recv_sem=a2a_recv.at[k],
            device_id=device(to),
            device_id_type=MESH,
        )

    @pl.loop(1, 32)
    def _(k):
        block_copy(k).start()

    own_block = pltpu.make_async_copy(packed.at[dp], received.at[dp], local_sem.at[0])
    own_block.start()

    @pl.loop(0, group_rows // rows)
    def _(i):
        at = pl.ds(pl.multiple_of(i * rows, rows), rows)
        for low in range(0, QKV, 256):
            columns = slice(low, min(low + 256, QKV))
            projected[:, columns] = nn(x_full[at, :], w_full[:, columns])
        for h in range(HEADS):
            for part, marked, mark in ((0, q_marked, mark_q), (1, k_marked, mark_k)):
                raw = projected[:, (h * 3 + part) * HD:(h * 3 + part + 1) * HD]
                factor = lax.rsqrt(jnp.mean(raw * raw, axis=-1, keepdims=True) + epsilon)
                marked[h, at, 0:HD] = (raw * factor).astype(jnp.bfloat16)
                marked[h, at, HD:2 * HD] = mark[at, :]
                factors[part, h, at, :] = jnp.broadcast_to(factor, (rows, HD))
            value = projected[:, (h * 3 + 2) * HD:(h * 3 + 3) * HD]
            v_half[h, at, :] = value.astype(jnp.bfloat16)
            v_turned[h, :, at] = value.T.astype(jnp.bfloat16)

    def block(place):
        at = pl.ds(pl.multiple_of(device(place)["seq"] * rows, rows), rows)

        @pl.loop(0, HEADS)
        def _(h):
            scores = nt(k_marked[h], q_marked[h, at, :])
            raised = jnp.exp2(scores * EXP2_SCALE)
            inverse_sum = 1.0 / jnp.sum(raised, axis=0, keepdims=True)
            turned = nn(v_turned[h], raised.astype(jnp.bfloat16)) * inverse_sum
            mixed[at, pl.ds(pl.multiple_of(h * HD, HD), HD)] = turned.T.astype(jnp.bfloat16)
            inverse[h, at, :] = jnp.broadcast_to(inverse_sum, (HD, rows)).T

        @pl.loop(0, width // 512)
        def _(t):
            columns = pl.ds(pl.multiple_of(t * 512, 512), 512)
            partial[at, columns] = nt(mixed[at, :], w_full[columns, QKV:QKV + OUT]).astype(jnp.bfloat16)

    core_first, core_second, chip_sums = [], [], []
    block(moved(other_core, A, 1))
    for chunk in range(CHUNKS):
        core_first.append(copies.start(
            partial.at[rows_of(moved(other_core, A, 1), chunk)], from_core.at[0, pl.ds(chunk * step, step)], other_core))
    block(other_chip)
    for chunk in range(CHUNKS):
        core_first[chunk].wait_recv()
        at = pl.ds(chunk * step, step)
        summed[at] = (partial[rows_of(other_chip, chunk)].astype(jnp.float32) + from_core[0, at].astype(jnp.float32)).astype(jnp.bfloat16)
        chip_sums.append(copies.start(summed.at[at], from_chip.at[at], other_chip))
    block(other_core)
    for chunk in range(CHUNKS):
        core_second.append(copies.start(
            partial.at[rows_of(other_core, chunk)], from_core.at[1, pl.ds(chunk * step, step)], other_core))
    block(me)

    own_block.wait()

    @pl.loop(1, 32)
    def _(k):
        block_copy(k).wait_recv()

    tile = 512

    @pl.loop(0, width // tile)
    def _(t):
        columns = pl.ds(pl.multiple_of(t * tile, tile), tile)
        blocks = received[:, :, columns].reshape(rows * CAP, tile)
        target[:, columns] = nn(chosen[...], blocks).astype(jnp.bfloat16)

    to_chip, to_core, passed = [], [], []
    for chunk in range(CHUNKS):
        core_second[chunk].wait_recv()
        chip_sums[chunk].wait_recv()
        at = pl.ds(chunk * step, step)
        mine = rows_of(me, chunk)
        prediction = (
            x_own[at].astype(jnp.float32)
            + (partial[mine].astype(jnp.float32) + from_core[1, at].astype(jnp.float32) + from_chip[at].astype(jnp.float32))
        )
        d_full[mine] = (weight[at] * (prediction - target[at].astype(jnp.float32))).astype(jnp.bfloat16)
        to_chip.append(copies.start(d_full.at[mine], d_full.at[mine], other_chip))
        to_core.append(copies.start(d_full.at[mine], d_full.at[mine], other_core))
    for chunk in range(CHUNKS):
        to_chip[chunk].wait_recv()
        theirs = rows_of(other_chip, chunk)
        passed.append(copies.start(d_full.at[theirs], d_full.at[theirs], other_core))
    for chunk in range(CHUNKS):
        to_core[chunk].wait_recv()
        passed[chunk].wait_recv()

    @pl.loop(1, 32)
    def _(k):
        block_copy(k).wait_send()

    copies.finish()


def forward(packed, chosen, x_full, w_full, mark_q, mark_k, x_own, weight):
    rows, width = x_own.shape
    group_rows = x_full.shape[0]
    vmem = pl.BlockSpec(memory_space=pltpu.VMEM)
    half, full = jnp.bfloat16, jnp.float32
    return pl.pallas_call(
        forward_kernel,
        out_shape=(
            jax.ShapeDtypeStruct((group_rows, width), half),
            jax.ShapeDtypeStruct((HEADS, group_rows, 2 * HD), half),
            jax.ShapeDtypeStruct((HEADS, group_rows, 2 * HD), half),
            jax.ShapeDtypeStruct((HEADS, group_rows, HD), half),
            jax.ShapeDtypeStruct((2, HEADS, group_rows, HD), full),
            jax.ShapeDtypeStruct((HEADS, group_rows, HD), full),
            jax.ShapeDtypeStruct((group_rows, OUT), half),
        ),
        in_specs=[pl.BlockSpec(memory_space=pl.ANY)] + [vmem] * 7,
        out_specs=(vmem,) * 7,
        scratch_shapes=[
            pltpu.VMEM((rows, QKV), full),
            pltpu.VMEM((HEADS, HD, group_rows), half),
            pltpu.VMEM((group_rows, width), half),
            pltpu.VMEM(packed.shape, half),
            pltpu.VMEM((rows, width), half),
            pltpu.VMEM((2, rows, width), half),
            pltpu.VMEM((rows, width), half),
            pltpu.VMEM((rows, width), half),
            pltpu.SemaphoreType.DMA((32,)),
            pltpu.SemaphoreType.DMA((32,)),
            pltpu.SemaphoreType.DMA((6 * CHUNKS,)),
            pltpu.SemaphoreType.DMA((6 * CHUNKS,)),
            pltpu.SemaphoreType.DMA((1,)),
        ],
        compiler_params=pltpu.CompilerParams(collective_id=2, has_side_effects=True, vmem_limit_bytes=VMEM_LIMIT),
        name="forward_residual_gradient",
    )(packed, chosen, x_full, w_full, mark_q, mark_k, x_own, weight)


def added(*values):
    total = values[0].astype(jnp.float32)
    for value in values[1:]:
        total = total + value.astype(jnp.float32)
    return total


def reduce_start(copies, me, axis, block, got):
    up, down = moved(me, axis, 1), moved(me, axis, -1)
    opposite = moved(me, axis, 2)[axis]
    far_up = copies.start(block(opposite, 0), got(0), up)
    far_down = copies.start(block(opposite, 1), got(1), down)
    near_up = copies.start(block(up[axis], 1), got(2), up)
    near_down = copies.start(block(down[axis], 0), got(3), down)
    return far_up, far_down, near_up, near_down


def reduce_pass(copies, me, axis, block, got, sums, sent, add):
    up, down = moved(me, axis, 1), moved(me, axis, -1)
    sent[0].wait_recv()
    add(sums(0), [block(up[axis], 0), got(0)])
    sum_up = copies.start(sums(0), got(4), up)
    sent[1].wait_recv()
    add(sums(1), [block(down[axis], 1), got(1)])
    sum_down = copies.start(sums(1), got(5), down)
    return sent[2], sent[3], sum_up, sum_down


def reduce_end(me, axis, block, got, out, sent, add):
    sent[1].wait_recv()
    sent[2].wait_recv()
    add(out(0), [block(me[axis], 0), got(3), got(4)])
    sent[0].wait_recv()
    sent[3].wait_recv()
    add(out(1), [block(me[axis], 1), got(2), got(5)])


def add_rows(out, parts):
    lead = out.shape[:-2]
    count = math.prod(lead)

    @pl.loop(0, count)
    def _(i):
        index, rest = [], i
        for size in reversed(lead):
            index.insert(0, rest % size)
            rest = rest // size
        index = tuple(index)
        out[index] = added(*[part[index] for part in parts]).astype(out.dtype)


SLABS = HEADS + 1


def backward_kernel(
    d_full, x_full, w_out, q_marked, k_marked, v_half, factors, inverse, mixed,
    qkv_sums, out_sums,
    d_out, k_turned, dq, dk, dv, d_proj,
    grads, got_far, sum_far, half_far, got_near, sum_near, half_near, got_last, send_sem, recv_sem,
):
    me = my_place()
    z, x, y, a, c = me
    greet([moved(me, Z, 1), moved(me, Z, -1), moved(me, X, 1), moved(me, X, -1), moved(me, Y, 1)])
    copies = Copies(send_sem, recv_sem)
    far_axis, near_axis = (X, Z), (Z, X)
    group_rows, width = x_full.shape
    rows = group_rows // 4
    scale = 1.0 / math.sqrt(HD)

    class Slab:
        def __init__(self, s):
            self.s = s

        def far_block(self, half):
            if half == 0:
                return lambda at, which: grads.at[self.s, pl.ds(2 * which, 2), at, :, 0]
            return lambda at, which: grads.at[self.s, at, pl.ds(2 * which, 2), :, 1]

        def near_block(self, half):
            return lambda at, which: half_far.at[self.s, half, at, which]

        def slots(self, ref, half):
            return lambda j: ref.at[self.s, half, j]

        def far_out(self, half):
            return lambda which: half_far.at[self.s, half, pl.ds(2 * which, 2)]

        def near_out(self, half):
            return lambda which: half_near.at[self.s, half, pl.ds(which, 1)]

        def far_start(self):
            self.sent = [
                reduce_start(copies, me, far_axis[h], self.far_block(h), self.slots(got_far, h)) for h in (0, 1)]

        def far_pass(self):
            self.sent = [
                reduce_pass(copies, me, far_axis[h], self.far_block(h), self.slots(got_far, h),
                            self.slots(sum_far, h), self.sent[h], add_rows)
                for h in (0, 1)]

        def near_start(self):
            for h in (0, 1):
                reduce_end(me, far_axis[h], self.far_block(h), self.slots(got_far, h), self.far_out(h), self.sent[h], add_rows)
            self.sent = [
                reduce_start(copies, me, near_axis[h], self.near_block(h), self.slots(got_near, h)) for h in (0, 1)]

        def near_pass(self):
            self.sent = [
                reduce_pass(copies, me, near_axis[h], self.near_block(h), self.slots(got_near, h),
                            self.slots(sum_near, h), self.sent[h], near_add)
                for h in (0, 1)]

        def last_start(self):
            for h in (0, 1):
                reduce_end(me, near_axis[h], self.near_block(h), self.slots(got_near, h), self.near_out(h), self.sent[h], near_add)
            self.sent = [
                copies.start(half_near.at[self.s, h, 1 - y], got_last.at[self.s, h], moved(me, Y, 1)) for h in (0, 1)]

        def end(self):
            for h in (0, 1):
                self.sent[h].wait_recv()
                total = added(half_near[self.s, h, y], got_last[self.s, h])
                if self.s == HEADS:
                    out_sums[h] = total
                else:
                    qkv_sums[h, :, self.s * 3 * HD:(self.s + 1) * 3 * HD] = total

    def near_add(out, parts):
        out[...] = added(*[part[...] for part in parts]).astype(out.dtype).reshape(out.shape)

    def weight_grads(s, left, right):
        @pl.loop(0, 8)
        def _(t):
            columns = pl.ds(pl.multiple_of(t * 384, 384), 384)
            term = tn(left[:, columns], right[...]).astype(jnp.bfloat16)
            grads[s, t // 2, pl.ds(t % 2 * 2, 2)] = term.reshape(2, 2, 2, 48, 384)

    def head(h):
        head_columns = slice(h * HD, (h + 1) * HD)

        @pl.loop(0, 4)
        def _(i):
            at = pl.ds(pl.multiple_of(i * rows, rows), rows)
            k_turned[:, at] = k_marked[h, at, 0:HD].astype(jnp.float32).T.astype(jnp.bfloat16)

        dk[...] = jnp.zeros_like(dk)
        dv[...] = jnp.zeros_like(dv)

        @pl.loop(0, 4)
        def _(i):
            at = pl.ds(pl.multiple_of(i * rows, rows), rows)
            raised = jnp.exp2(nt(k_marked[h], q_marked[h, at, :]) * EXP2_SCALE)
            d_here = d_out[at, head_columns]
            delta = jnp.sum((d_here.astype(jnp.float32) * mixed[at, head_columns].astype(jnp.float32)).T, axis=0, keepdims=True)
            d_scores = (raised * (nt(v_half[h], d_here) - delta)).astype(jnp.bfloat16)
            dv[...] += nn(raised.astype(jnp.bfloat16), d_here)
            dk[...] += nn(d_scores, q_marked[h, at, 0:HD])
            dq[at, :] = nn(k_turned[...], d_scores).T

        @pl.loop(0, 4)
        def _(i):
            at = pl.ds(pl.multiple_of(i * rows, rows), rows)
            for part, grad, marked in ((0, dq, q_marked), (1, dk, k_marked)):
                normed = marked[h, at, 0:HD].astype(jnp.float32)
                got = grad[at, :]
                inner = jnp.mean(got * normed, axis=-1, keepdims=True)
                d_proj[at, part * HD:(part + 1) * HD] = (
                    (factors[part, h, at, :] * scale) * (got - normed * inner)).astype(jnp.bfloat16)
            d_proj[at, 2 * HD:3 * HD] = dv[at, :].astype(jnp.bfloat16)

    out_slab = Slab(HEADS)
    slabs = [Slab(h) for h in range(HEADS)]
    weight_grads(HEADS, d_full, mixed)
    out_slab.far_start()

    @pl.loop(0, 4)
    def _(i):
        at = pl.ds(pl.multiple_of(i * rows, rows), rows)
        got = nn(d_full[at, :], w_out[...])
        for h in range(HEADS):
            d_out[at, h * HD:(h + 1) * HD] = (got[:, h * HD:(h + 1) * HD] * inverse[h, at, :]).astype(jnp.bfloat16)

    head(0)
    out_slab.far_pass()
    weight_grads(0, x_full, d_proj)
    slabs[0].far_start()
    out_slab.near_start()
    head(1)
    slabs[0].far_pass()
    out_slab.near_pass()
    weight_grads(1, x_full, d_proj)
    slabs[1].far_start()
    slabs[0].near_start()
    out_slab.last_start()
    head(2)
    slabs[1].far_pass()
    slabs[0].near_pass()
    out_slab.end()
    weight_grads(2, x_full, d_proj)
    slabs[2].far_start()
    slabs[1].near_start()
    slabs[0].last_start()
    slabs[2].far_pass()
    slabs[1].near_pass()
    slabs[0].end()
    slabs[2].near_start()
    slabs[1].last_start()
    slabs[2].near_pass()
    slabs[1].end()
    slabs[2].last_start()
    slabs[2].end()
    copies.finish()


def backward(d_full, x_full, w_out, q_marked, k_marked, v_half, factors, inverse, mixed):
    group_rows = x_full.shape[0]
    half = lambda *lead: pltpu.VMEM((SLABS, 2, *lead, 48, 3 * HD), jnp.bfloat16)
    vmem = pl.BlockSpec(memory_space=pltpu.VMEM)
    qkv_sums, out_sums = pl.pallas_call(
        backward_kernel,
        out_shape=(
            jax.ShapeDtypeStruct((2, 48, QKV), jnp.float32),
            jax.ShapeDtypeStruct((2, 48, OUT), jnp.float32),
        ),
        in_specs=[vmem] * 9,
        out_specs=(vmem, vmem),
        scratch_shapes=[
            pltpu.VMEM((group_rows, OUT), jnp.bfloat16),
            pltpu.VMEM((HD, group_rows), jnp.bfloat16),
            pltpu.VMEM((group_rows, HD), jnp.float32),
            pltpu.VMEM((group_rows, HD), jnp.float32),
            pltpu.VMEM((group_rows, HD), jnp.float32),
            pltpu.VMEM((group_rows, 3 * HD), jnp.bfloat16),
            pltpu.VMEM((SLABS, 4, 4, 2, 2, 48, 3 * HD), jnp.bfloat16),
            half(6, 2, 2),
            half(2, 2, 2),
            half(4, 2),
            half(6),
            half(2),
            half(2),
            half(),
            pltpu.SemaphoreType.DMA((26 * SLABS,)),
            pltpu.SemaphoreType.DMA((26 * SLABS,)),
        ],
        compiler_params=pltpu.CompilerParams(collective_id=3, has_side_effects=True, vmem_limit_bytes=VMEM_LIMIT),
        name="backward_scatter",
    )(d_full, x_full, w_out, q_marked, k_marked, v_half, factors, inverse, mixed)
    return qkv_sums.reshape(96, QKV), out_sums.reshape(96, OUT)


def spread(block_of, rows, columns):
    source = jnp.repeat(block_of, 8) * 8 + jnp.tile(jnp.arange(8, dtype=jnp.int32), rows // 8)
    source = jnp.where(jnp.repeat(block_of, 8) < 0, -1, source)
    return (source[:, None] == jnp.arange(columns, dtype=jnp.int32)[None, :]).astype(jnp.bfloat16)


def per_device(clip_rows, velocity_target, plan, segment_ids, reward_levels, w_qkv, w_out):
    groups = lax.axis_size("dp")
    shards = lax.axis_size("seq")
    group = lax.axis_index("dp")
    shard = lax.axis_index("seq")
    rows_dev, width = clip_rows.shape
    group_rows = rows_dev * shards
    counts = plan[group, shard]
    send_start = jnp.cumsum(counts) - counts
    slot_index = jnp.arange(CAP, dtype=jnp.int32)
    source_block = jnp.where(slot_index[None, :] < counts[:, None], send_start[:, None] + slot_index[None, :], -1).reshape(-1)
    pack = spread(source_block, rows_dev * CAP, rows_dev)

    def packed(source_rows):
        return jnp.dot(pack, source_rows, preferred_element_type=jnp.float32).astype(jnp.bfloat16).reshape(groups, CAP * 8, width)

    arriving = plan[:, shard, group]
    arriving_end = jnp.cumsum(arriving)
    slot_ids = jnp.arange(groups, dtype=jnp.int32)
    source_group = jnp.sum((arriving_end[None, :] <= slot_ids[:, None]).astype(jnp.int32), axis=1)
    arriving_start = (arriving_end - arriving)[source_group]
    flat_slot = source_group * CAP + slot_ids - arriving_start
    chosen = spread(flat_slot, rows_dev, rows_dev * CAP)

    group_x, weights = gather_all(packed(clip_rows), jnp.concatenate([w_qkv, w_out], axis=1), chosen)
    segment_row = segment_ids[0]
    clip_index = jnp.arange(reward_levels.shape[1], dtype=jnp.int32)
    levels = reward_levels[0].astype(jnp.float32) / 8.0
    own_segment = lax.dynamic_slice(segment_row, (shard * rows_dev,), (rows_dev,))
    row_weight = jnp.sum(
        jnp.where(own_segment[:, None] == clip_index[None, :], levels[None, :], jnp.float32(0.0)),
        axis=1,
        keepdims=True,
    )
    loss_scale = 1.0 / math.sqrt(rows_dev * groups * shards)
    own_x = lax.dynamic_slice(group_x, (shard * rows_dev, 0), (rows_dev, width))

    sign = (2 * segment_row - 1)[:, None]
    lane = jnp.arange(HD, dtype=jnp.int32)[None, :]
    mark_q = jnp.where(lane == 0, 64 * sign, jnp.where(lane == 1, -64, 0)).astype(jnp.bfloat16)
    mark_k = jnp.where(lane == 0, 32 * sign, jnp.where(lane == 1, 32, 0)).astype(jnp.bfloat16)

    pred_grad, *saved = forward(
        packed(velocity_target), chosen, group_x, weights, mark_q, mark_k, own_x, row_weight * loss_scale)
    return backward(pred_grad, group_x, weights[:, QKV:], *saved)


def solution(mesh):
    return jax.shard_map(
        per_device,
        mesh=mesh,
        in_specs=(
            P(("dp", "seq"), None),
            P(("dp", "seq"), None),
            P(),
            P("dp", None),
            P("dp", None),
            P("dp", "seq"),
            P("dp", "seq"),
        ),
        out_specs=(P("dp", "seq"), P("dp", "seq")),
        check_vma=False,
    )
```

```python
import math

import jax
import jax.numpy as jnp
from jax import lax
from jax.experimental import pallas as pl
from jax.experimental.pallas import tpu as pltpu
from jax.sharding import PartitionSpec as P

HD = 128
CAP = 2
MESH = pl.DeviceIdType.MESH
VMEM_LIMIT = 60 * 1024 * 1024

epsilon = 1e-06


def my_place():
    dp = lax.axis_index("dp")
    seq = lax.axis_index("seq")
    return (dp // 8, (dp // 2) % 4, dp % 2, seq // 2, seq % 2)


def device(place):
    z, x, y, a, c = place
    return {"dp": z * 8 + x * 2 + y, "seq": a * 2 + c}


def moved(place, axis, by):
    place = list(place)
    size = (4, 4, 2, 2, 2)[axis]
    place[axis] = (place[axis] + by + size) % size
    return tuple(place)


Z, X, Y, A, C = range(5)


def chip_partner(place):
    return moved(moved(place, Y, 1), A, 1)


class Copies:
    def __init__(self, send_sem, recv_sem):
        self.send_sem, self.recv_sem, self.used = send_sem, recv_sem, 0
        self.started = []

    def start(self, src, dst, to):
        copy = pltpu.make_async_remote_copy(
            src_ref=src,
            dst_ref=dst,
            send_sem=self.send_sem.at[self.used],
            recv_sem=self.recv_sem.at[self.used],
            device_id=device(to),
            device_id_type=MESH,
        )
        self.used += 1
        copy.start()
        self.started.append(copy)
        return copy

    def finish(self):
        for copy in self.started:
            copy.wait_send()


def greet(places):
    barrier = pltpu.get_barrier_semaphore()
    for place in places:
        pl.semaphore_signal(barrier, inc=1, device_id=device(place), device_id_type=MESH)
    pl.semaphore_wait(barrier, len(places))


def dp_peer(place, k, sign):
    z, x, y, a, c = place
    dz, dx, dy = k // 8, (k // 2) % 4, k % 2
    return ((z + sign * dz + 4) % 4, (x + sign * dx + 4) % 4, (y + sign * dy + 2) % 2, a, c)


def ring_gather_start(copies, me, axis, part):
    own = me[axis]
    up, down = moved(me, axis, 1), moved(me, axis, -1)
    first_up = copies.start(part(own, 0), part(own, 0), up)
    first_down = copies.start(part(own, 1), part(own, 1), down)
    second_up = copies.start(part(own, 1), part(own, 1), up)
    second_down = copies.start(part(own, 0), part(own, 0), down)
    return first_up, first_down, second_up, second_down


def ring_gather_forward(copies, me, axis, part, sent):
    up, down = moved(me, axis, 1), moved(me, axis, -1)
    below, above = down[axis], up[axis]
    sent[0].wait_recv()
    third_up = copies.start(part(below, 0), part(below, 0), up)
    sent[1].wait_recv()
    third_down = copies.start(part(above, 1), part(above, 1), down)
    return sent[2], sent[3], third_up, third_down


def gather_kernel(packed, shard, chosen, labels, x_full, w_full, labels_there, received, own_rows, a2a_send, a2a_recv, send_sem, recv_sem, local_sem):
    me = my_place()
    z, x, y, a, c = me
    dp = lax.axis_index("dp")
    seq = lax.axis_index("seq")
    rows = own_rows.shape[0]
    other_chip, other_core = chip_partner(me), moved(me, C, 1)
    barrier = pltpu.get_barrier_semaphore()

    @pl.loop(1, 32)
    def _(k):
        pl.semaphore_signal(barrier, inc=1, device_id=device(dp_peer(me, k, 1)), device_id_type=MESH)

    for place in (other_chip, other_core):
        pl.semaphore_signal(barrier, inc=1, device_id=device(place), device_id_type=MESH)
    pl.semaphore_wait(barrier, 33)

    copies = Copies(send_sem, recv_sem)
    own_shard = pltpu.make_async_copy(shard, w_full.at[z, x, y], local_sem.at[0])
    own_shard.start()
    across = copies.start(shard, w_full.at[z, x, y], moved(me, Y, 1))
    labels_across = copies.start(labels, labels_there, moved(me, Y, 1))

    def block_copy(k):
        to = dp_peer(me, k, 1)
        return pltpu.make_async_remote_copy(
            src_ref=packed.at[device(to)["dp"]],
            dst_ref=received.at[dp],
            send_sem=a2a_send.at[k],
            recv_sem=a2a_recv.at[k],
            device_id=device(to),
            device_id_type=MESH,
        )

    @pl.loop(1, 32)
    def _(k):
        block_copy(k).start()

    own_block = pltpu.make_async_copy(packed.at[dp], received.at[dp], local_sem.at[1])
    own_block.start()

    own_shard.wait()
    across.wait_recv()

    def near(half):
        if half == 0:
            return lambda at, which: w_full.at[at, x, which, 0]
        return lambda at, which: w_full.at[z, at, which, 1]

    def far(half):
        if half == 0:
            return lambda at, which: w_full.at[pl.ds(2 * which, 2), at, :, 0]
        return lambda at, which: w_full.at[at, pl.ds(2 * which, 2), :, 1]

    near_axis, far_axis = (Z, X), (X, Z)
    sent = [ring_gather_start(copies, me, near_axis[half], near(half)) for half in (0, 1)]
    rest = [ring_gather_forward(copies, me, near_axis[half], near(half), sent[half]) for half in (0, 1)]
    for half in (0, 1):
        for copy in rest[half]:
            copy.wait_recv()
    sent = [ring_gather_start(copies, me, far_axis[half], far(half)) for half in (0, 1)]

    own_block.wait()

    @pl.loop(1, 32)
    def _(k):
        block_copy(k).wait_recv()

    width = own_rows.shape[1]
    tile = 512

    @pl.loop(0, width // tile)
    def _(t):
        columns = pl.ds(pl.multiple_of(t * tile, tile), tile)
        blocks = received[:, :, columns].reshape(rows * CAP, tile)
        own_rows[:, columns] = jnp.dot(chosen[...], blocks, preferred_element_type=jnp.float32).astype(jnp.bfloat16)

    def rows_of(place):
        return pl.ds(pl.multiple_of(device(place)["seq"] * rows, rows), rows)

    to_chip = copies.start(own_rows, x_full.at[rows_of(me)], other_chip)
    to_core = copies.start(own_rows, x_full.at[rows_of(me)], other_core)
    own_place = pltpu.make_async_copy(own_rows, x_full.at[rows_of(me)], local_sem.at[2])
    own_place.start()

    rest = [ring_gather_forward(copies, me, far_axis[half], far(half), sent[half]) for half in (0, 1)]
    to_chip.wait_recv()
    passed = copies.start(x_full.at[rows_of(other_chip)], x_full.at[rows_of(other_chip)], other_core)
    to_core.wait_recv()
    passed.wait_recv()
    for half in (0, 1):
        for copy in rest[half]:
            copy.wait_recv()
    own_place.wait()
    labels_across.wait_recv()

    @pl.loop(1, 32)
    def _(k):
        block_copy(k).wait_send()

    copies.finish()


def gather_all(packed, shard, chosen, labels):
    rows = chosen.shape[0]
    width = packed.shape[2]
    w_cols = shard.shape[1]
    x_full, w_full, labels_there = pl.pallas_call(
        gather_kernel,
        out_shape=(
            jax.ShapeDtypeStruct((rows * 4, width), jnp.bfloat16),
            jax.ShapeDtypeStruct((4, 4, 2, 2, 48, w_cols), jnp.bfloat16),
            jax.ShapeDtypeStruct(labels.shape, labels.dtype),
        ),
        in_specs=[
            pl.BlockSpec(memory_space=pl.ANY),
            pl.BlockSpec(memory_space=pl.ANY),
            pl.BlockSpec(memory_space=pltpu.VMEM),
            pl.BlockSpec(memory_space=pl.ANY),
        ],
        out_specs=(pl.BlockSpec(memory_space=pl.ANY),) * 3,
        scratch_shapes=[
            pltpu.VMEM(packed.shape, jnp.bfloat16),
            pltpu.VMEM((rows, width), jnp.bfloat16),
            pltpu.SemaphoreType.DMA((32,)),
            pltpu.SemaphoreType.DMA((32,)),
            pltpu.SemaphoreType.DMA((29,)),
            pltpu.SemaphoreType.DMA((29,)),
            pltpu.SemaphoreType.DMA((3,)),
        ],
        compiler_params=pltpu.CompilerParams(collective_id=1, has_side_effects=True, vmem_limit_bytes=VMEM_LIMIT),
        name="gather_rows_weights",
    )(packed, shard.reshape(2, 48, w_cols), chosen, labels)
    return x_full, w_full.reshape(3072, w_cols), labels_there


CHUNKS = 4
HEADS = 3
QKV = HEADS * 3 * HD
OUT = HEADS * HD
EXP2_SCALE = math.log2(math.e) / math.sqrt(HD)


def nt(left, right):
    return lax.dot_general(left, right, (((1,), (1,)), ((), ())), preferred_element_type=jnp.float32)


def tn(left, right):
    return lax.dot_general(left, right, (((0,), (0,)), ((), ())), preferred_element_type=jnp.float32)


def nn(left, right):
    return jnp.dot(left, right, preferred_element_type=jnp.float32)


def forward_kernel(
    packed, chosen, x_full, w_full, mark_q, mark_k, weight,
    d_full, q_marked, k_marked, v_half, factors, inverse, mixed,
    projected, v_turned, partial, received, target, from_core, summed, from_chip,
    a2a_send, a2a_recv, send_sem, recv_sem, local_sem,
):
    me = my_place()
    dp = lax.axis_index("dp")
    rows = weight.shape[0]
    group_rows, width = x_full.shape
    other_chip, other_core = chip_partner(me), moved(me, C, 1)
    barrier = pltpu.get_barrier_semaphore()

    @pl.loop(1, 32)
    def _(k):
        pl.semaphore_signal(barrier, inc=1, device_id=device(dp_peer(me, k, 1)), device_id_type=MESH)

    for place in (other_chip, other_core):
        pl.semaphore_signal(barrier, inc=1, device_id=device(place), device_id_type=MESH)
    pl.semaphore_wait(barrier, 33)

    copies = Copies(send_sem, recv_sem)
    step = rows // CHUNKS

    def rows_of(place, chunk):
        return pl.ds(pl.multiple_of(device(place)["seq"] * rows + chunk * step, step), step)

    def block_copy(k):
        to = dp_peer(me, k, 1)
        return pltpu.make_async_remote_copy(
            src_ref=packed.at[device(to)["dp"]],
            dst_ref=received.at[dp],
            send_sem=a2a_send.at[k],
            recv_sem=a2a_recv.at[k],
            device_id=device(to),
            device_id_type=MESH,
        )

    @pl.loop(1, 32)
    def _(k):
        block_copy(k).start()

    own_block = pltpu.make_async_copy(packed.at[dp], received.at[dp], local_sem.at[0])
    own_block.start()

    @pl.loop(0, group_rows // rows)
    def _(i):
        at = pl.ds(pl.multiple_of(i * rows, rows), rows)
        for low in range(0, QKV, 256):
            columns = slice(low, min(low + 256, QKV))
            projected[:, columns] = nn(x_full[at, :], w_full[:, columns])
        for h in range(HEADS):
            for part, marked, mark in ((0, q_marked, mark_q), (1, k_marked, mark_k)):
                raw = projected[:, (h * 3 + part) * HD:(h * 3 + part + 1) * HD]
                factor = lax.rsqrt(jnp.mean(raw * raw, axis=-1, keepdims=True) + epsilon)
                marked[h, at, 0:HD] = (raw * factor).astype(jnp.bfloat16)
                marked[h, at, HD:2 * HD] = mark[at, :]
                factors[part, h, at, :] = jnp.broadcast_to(factor, (rows, HD))
            value = projected[:, (h * 3 + 2) * HD:(h * 3 + 3) * HD]
            v_half[h, at, :] = value.astype(jnp.bfloat16)
            v_turned[h, :, at] = value.T.astype(jnp.bfloat16)

    def block(place):
        at = pl.ds(pl.multiple_of(device(place)["seq"] * rows, rows), rows)

        @pl.loop(0, HEADS)
        def _(h):
            scores = nt(k_marked[h], q_marked[h, at, :])
            raised = jnp.exp2(scores * EXP2_SCALE)
            inverse_sum = 1.0 / jnp.sum(raised, axis=0, keepdims=True)
            turned = nn(v_turned[h], raised.astype(jnp.bfloat16)) * inverse_sum
            mixed[at, pl.ds(pl.multiple_of(h * HD, HD), HD)] = turned.T.astype(jnp.bfloat16)
            inverse[h, at, :] = jnp.broadcast_to(inverse_sum, (HD, rows)).T

        @pl.loop(0, width // 512)
        def _(t):
            columns = pl.ds(pl.multiple_of(t * 512, 512), 512)
            partial[at, columns] = nt(mixed[at, :], w_full[columns, QKV:QKV + OUT]).astype(jnp.bfloat16)

    core_first, core_second, chip_sums = [], [], []
    block(moved(other_core, A, 1))
    for chunk in range(CHUNKS):
        core_first.append(copies.start(
            partial.at[rows_of(moved(other_core, A, 1), chunk)], from_core.at[0, pl.ds(chunk * step, step)], other_core))
    block(other_chip)
    for chunk in range(CHUNKS):
        core_first[chunk].wait_recv()
        at = pl.ds(chunk * step, step)
        summed[at] = (partial[rows_of(other_chip, chunk)].astype(jnp.float32) + from_core[0, at].astype(jnp.float32)).astype(jnp.bfloat16)
        chip_sums.append(copies.start(summed.at[at], from_chip.at[at], other_chip))
    block(other_core)
    for chunk in range(CHUNKS):
        core_second.append(copies.start(
            partial.at[rows_of(other_core, chunk)], from_core.at[1, pl.ds(chunk * step, step)], other_core))
    block(me)

    own_block.wait()

    @pl.loop(1, 32)
    def _(k):
        block_copy(k).wait_recv()

    tile = 512

    @pl.loop(0, width // tile)
    def _(t):
        columns = pl.ds(pl.multiple_of(t * tile, tile), tile)
        blocks = received[:, :, columns].reshape(rows * CAP, tile)
        target[:, columns] = nn(chosen[...], blocks).astype(jnp.bfloat16)

    to_chip, to_core, passed = [], [], []
    for chunk in range(CHUNKS):
        core_second[chunk].wait_recv()
        chip_sums[chunk].wait_recv()
        at = pl.ds(chunk * step, step)
        mine = rows_of(me, chunk)
        prediction = (
            x_full[mine].astype(jnp.float32)
            + (partial[mine].astype(jnp.float32) + from_core[1, at].astype(jnp.float32) + from_chip[at].astype(jnp.float32))
        )
        d_full[mine] = (weight[at] * (prediction - target[at].astype(jnp.float32))).astype(jnp.bfloat16)
        to_chip.append(copies.start(d_full.at[mine], d_full.at[mine], other_chip))
        to_core.append(copies.start(d_full.at[mine], d_full.at[mine], other_core))
    for chunk in range(CHUNKS):
        to_chip[chunk].wait_recv()
        theirs = rows_of(other_chip, chunk)
        passed.append(copies.start(d_full.at[theirs], d_full.at[theirs], other_core))
    for chunk in range(CHUNKS):
        to_core[chunk].wait_recv()
        passed[chunk].wait_recv()

    @pl.loop(1, 32)
    def _(k):
        block_copy(k).wait_send()

    copies.finish()


def forward(packed, chosen, x_full, w_full, mark_q, mark_k, weight):
    rows = weight.shape[0]
    group_rows, width = x_full.shape
    vmem = pl.BlockSpec(memory_space=pltpu.VMEM)
    half, full = jnp.bfloat16, jnp.float32
    return pl.pallas_call(
        forward_kernel,
        out_shape=(
            jax.ShapeDtypeStruct((group_rows, width), half),
            jax.ShapeDtypeStruct((HEADS, group_rows, 2 * HD), half),
            jax.ShapeDtypeStruct((HEADS, group_rows, 2 * HD), half),
            jax.ShapeDtypeStruct((HEADS, group_rows, HD), half),
            jax.ShapeDtypeStruct((2, HEADS, group_rows, HD), full),
            jax.ShapeDtypeStruct((HEADS, group_rows, HD), full),
            jax.ShapeDtypeStruct((group_rows, OUT), half),
        ),
        in_specs=[pl.BlockSpec(memory_space=pl.ANY)] + [vmem] * 6,
        out_specs=(vmem,) * 7,
        scratch_shapes=[
            pltpu.VMEM((rows, QKV), full),
            pltpu.VMEM((HEADS, HD, group_rows), half),
            pltpu.VMEM((group_rows, width), half),
            pltpu.VMEM(packed.shape, half),
            pltpu.VMEM((rows, width), half),
            pltpu.VMEM((2, rows, width), half),
            pltpu.VMEM((rows, width), half),
            pltpu.VMEM((rows, width), half),
            pltpu.SemaphoreType.DMA((32,)),
            pltpu.SemaphoreType.DMA((32,)),
            pltpu.SemaphoreType.DMA((6 * CHUNKS,)),
            pltpu.SemaphoreType.DMA((6 * CHUNKS,)),
            pltpu.SemaphoreType.DMA((1,)),
        ],
        compiler_params=pltpu.CompilerParams(collective_id=2, has_side_effects=True, vmem_limit_bytes=VMEM_LIMIT),
        name="forward_residual_gradient",
    )(packed, chosen, x_full, w_full, mark_q, mark_k, weight)


def added(*values):
    total = values[0].astype(jnp.float32)
    for value in values[1:]:
        total = total + value.astype(jnp.float32)
    return total


def reduce_start(copies, me, axis, block, got):
    up, down = moved(me, axis, 1), moved(me, axis, -1)
    opposite = moved(me, axis, 2)[axis]
    far_up = copies.start(block(opposite, 0), got(0), up)
    far_down = copies.start(block(opposite, 1), got(1), down)
    near_up = copies.start(block(up[axis], 1), got(2), up)
    near_down = copies.start(block(down[axis], 0), got(3), down)
    return far_up, far_down, near_up, near_down


def reduce_pass(copies, me, axis, block, got, sums, sent, add):
    up, down = moved(me, axis, 1), moved(me, axis, -1)
    sent[0].wait_recv()
    add(sums(0), [block(up[axis], 0), got(0)])
    sum_up = copies.start(sums(0), got(4), up)
    sent[1].wait_recv()
    add(sums(1), [block(down[axis], 1), got(1)])
    sum_down = copies.start(sums(1), got(5), down)
    return sent[2], sent[3], sum_up, sum_down


def reduce_end(me, axis, block, got, out, sent, add):
    sent[1].wait_recv()
    sent[2].wait_recv()
    add(out(0), [block(me[axis], 0), got(3), got(4)])
    sent[0].wait_recv()
    sent[3].wait_recv()
    add(out(1), [block(me[axis], 1), got(2), got(5)])


def add_rows(out, parts):
    lead = out.shape[:-2]
    count = math.prod(lead)

    @pl.loop(0, count)
    def _(i):
        index, rest = [], i
        for size in reversed(lead):
            index.insert(0, rest % size)
            rest = rest // size
        index = tuple(index)
        out[index] = added(*[part[index] for part in parts]).astype(out.dtype)


SLABS = HEADS + 1


def backward_kernel(
    d_full, x_full, weights, q_marked, k_marked, v_half, factors, inverse, mixed,
    qkv_sums, out_sums,
    d_out, k_turned, dq, dk, dv, d_proj,
    grads, got_far, sum_far, half_far, got_near, sum_near, half_near, got_last, w_out, send_sem, recv_sem, local_sem,
):
    me = my_place()
    z, x, y, a, c = me
    w_copy = pltpu.make_async_copy(weights.at[:, QKV:QKV + OUT], w_out, local_sem.at[0])
    w_copy.start()
    greet([moved(me, Z, 1), moved(me, Z, -1), moved(me, X, 1), moved(me, X, -1), moved(me, Y, 1)])
    copies = Copies(send_sem, recv_sem)
    far_axis, near_axis = (X, Z), (Z, X)
    group_rows, width = x_full.shape
    rows = group_rows // 4
    scale = 1.0 / math.sqrt(HD)

    class Slab:
        def __init__(self, s):
            self.s = s

        def far_block(self, half):
            if half == 0:
                return lambda at, which: grads.at[self.s, pl.ds(2 * which, 2), at, :, 0]
            return lambda at, which: grads.at[self.s, at, pl.ds(2 * which, 2), :, 1]

        def near_block(self, half):
            return lambda at, which: half_far.at[self.s, half, at, which]

        def slots(self, ref, half):
            return lambda j: ref.at[self.s, half, j]

        def far_out(self, half):
            return lambda which: half_far.at[self.s, half, pl.ds(2 * which, 2)]

        def near_out(self, half):
            return lambda which: half_near.at[self.s, half, pl.ds(which, 1)]

        def far_start(self):
            self.sent = [
                reduce_start(copies, me, far_axis[h], self.far_block(h), self.slots(got_far, h)) for h in (0, 1)]

        def far_pass(self):
            self.sent = [
                reduce_pass(copies, me, far_axis[h], self.far_block(h), self.slots(got_far, h),
                            self.slots(sum_far, h), self.sent[h], add_rows)
                for h in (0, 1)]

        def near_start(self):
            for h in (0, 1):
                reduce_end(me, far_axis[h], self.far_block(h), self.slots(got_far, h), self.far_out(h), self.sent[h], add_rows)
            self.sent = [
                reduce_start(copies, me, near_axis[h], self.near_block(h), self.slots(got_near, h)) for h in (0, 1)]

        def near_pass(self):
            self.sent = [
                reduce_pass(copies, me, near_axis[h], self.near_block(h), self.slots(got_near, h),
                            self.slots(sum_near, h), self.sent[h], near_add)
                for h in (0, 1)]

        def last_start(self):
            for h in (0, 1):
                reduce_end(me, near_axis[h], self.near_block(h), self.slots(got_near, h), self.near_out(h), self.sent[h], near_add)
            self.sent = [
                copies.start(half_near.at[self.s, h, 1 - y], got_last.at[self.s, h], moved(me, Y, 1)) for h in (0, 1)]

        def end(self):
            for h in (0, 1):
                self.sent[h].wait_recv()
                total = added(half_near[self.s, h, y], got_last[self.s, h])
                if self.s == HEADS:
                    out_sums[h] = total
                else:
                    qkv_sums[h, :, self.s * 3 * HD:(self.s + 1) * 3 * HD] = total

    def near_add(out, parts):
        out[...] = added(*[part[...] for part in parts]).astype(out.dtype).reshape(out.shape)

    def weight_grads(s, left, right):
        @pl.loop(0, 8)
        def _(t):
            columns = pl.ds(pl.multiple_of(t * 384, 384), 384)
            term = tn(left[:, columns], right[...]).astype(jnp.bfloat16)
            grads[s, t // 2, pl.ds(t % 2 * 2, 2)] = term.reshape(2, 2, 2, 48, 384)

    def head(h):
        head_columns = slice(h * HD, (h + 1) * HD)

        @pl.loop(0, 4)
        def _(i):
            at = pl.ds(pl.multiple_of(i * rows, rows), rows)
            k_turned[:, at] = k_marked[h, at, 0:HD].astype(jnp.float32).T.astype(jnp.bfloat16)

        dk[...] = jnp.zeros_like(dk)
        dv[...] = jnp.zeros_like(dv)

        @pl.loop(0, 4)
        def _(i):
            at = pl.ds(pl.multiple_of(i * rows, rows), rows)
            raised = jnp.exp2(nt(k_marked[h], q_marked[h, at, :]) * EXP2_SCALE)
            d_here = d_out[at, head_columns]
            delta = jnp.sum((d_here.astype(jnp.float32) * mixed[at, head_columns].astype(jnp.float32)).T, axis=0, keepdims=True)
            d_scores = (raised * (nt(v_half[h], d_here) - delta)).astype(jnp.bfloat16)
            dv[...] += nn(raised.astype(jnp.bfloat16), d_here)
            dk[...] += nn(d_scores, q_marked[h, at, 0:HD])
            dq[at, :] = nn(k_turned[...], d_scores).T

        @pl.loop(0, 4)
        def _(i):
            at = pl.ds(pl.multiple_of(i * rows, rows), rows)
            for part, grad, marked in ((0, dq, q_marked), (1, dk, k_marked)):
                normed = marked[h, at, 0:HD].astype(jnp.float32)
                got = grad[at, :]
                inner = jnp.mean(got * normed, axis=-1, keepdims=True)
                d_proj[at, part * HD:(part + 1) * HD] = (
                    (factors[part, h, at, :] * scale) * (got - normed * inner)).astype(jnp.bfloat16)
            d_proj[at, 2 * HD:3 * HD] = dv[at, :].astype(jnp.bfloat16)

    out_slab = Slab(HEADS)
    slabs = [Slab(h) for h in range(HEADS)]
    weight_grads(HEADS, d_full, mixed)
    out_slab.far_start()
    w_copy.wait()

    @pl.loop(0, 4)
    def _(i):
        at = pl.ds(pl.multiple_of(i * rows, rows), rows)
        got = nn(d_full[at, :], w_out[...])
        for h in range(HEADS):
            d_out[at, h * HD:(h + 1) * HD] = (got[:, h * HD:(h + 1) * HD] * inverse[h, at, :]).astype(jnp.bfloat16)

    head(0)
    out_slab.far_pass()
    weight_grads(0, x_full, d_proj)
    slabs[0].far_start()
    out_slab.near_start()
    head(1)
    slabs[0].far_pass()
    out_slab.near_pass()
    weight_grads(1, x_full, d_proj)
    slabs[1].far_start()
    slabs[0].near_start()
    out_slab.last_start()
    head(2)
    slabs[1].far_pass()
    slabs[0].near_pass()
    out_slab.end()
    weight_grads(2, x_full, d_proj)
    slabs[2].far_start()
    slabs[1].near_start()
    slabs[0].last_start()
    slabs[2].far_pass()
    slabs[1].near_pass()
    slabs[0].end()
    slabs[2].near_start()
    slabs[1].last_start()
    slabs[2].near_pass()
    slabs[1].end()
    slabs[2].last_start()
    slabs[2].end()
    copies.finish()


def backward(d_full, x_full, weights, q_marked, k_marked, v_half, factors, inverse, mixed):
    group_rows, width = x_full.shape
    half = lambda *lead: pltpu.VMEM((SLABS, 2, *lead, 48, 3 * HD), jnp.bfloat16)
    vmem = pl.BlockSpec(memory_space=pltpu.VMEM)
    qkv_sums, out_sums = pl.pallas_call(
        backward_kernel,
        out_shape=(
            jax.ShapeDtypeStruct((2, 48, QKV), jnp.float32),
            jax.ShapeDtypeStruct((2, 48, OUT), jnp.float32),
        ),
        in_specs=[vmem] * 2 + [pl.BlockSpec(memory_space=pl.ANY)] + [vmem] * 6,
        out_specs=(vmem, vmem),
        scratch_shapes=[
            pltpu.VMEM((group_rows, OUT), jnp.bfloat16),
            pltpu.VMEM((HD, group_rows), jnp.bfloat16),
            pltpu.VMEM((group_rows, HD), jnp.float32),
            pltpu.VMEM((group_rows, HD), jnp.float32),
            pltpu.VMEM((group_rows, HD), jnp.float32),
            pltpu.VMEM((group_rows, 3 * HD), jnp.bfloat16),
            pltpu.VMEM((SLABS, 4, 4, 2, 2, 48, 3 * HD), jnp.bfloat16),
            half(6, 2, 2),
            half(2, 2, 2),
            half(4, 2),
            half(6),
            half(2),
            half(2),
            half(),
            pltpu.VMEM((width, OUT), jnp.bfloat16),
            pltpu.SemaphoreType.DMA((26 * SLABS,)),
            pltpu.SemaphoreType.DMA((26 * SLABS,)),
            pltpu.SemaphoreType.DMA((1,)),
        ],
        compiler_params=pltpu.CompilerParams(collective_id=3, has_side_effects=True, vmem_limit_bytes=VMEM_LIMIT),
        name="backward_scatter",
    )(d_full, x_full, weights, q_marked, k_marked, v_half, factors, inverse, mixed)
    return qkv_sums.reshape(96, QKV), out_sums.reshape(96, OUT)


def spread(block_of, rows, columns):
    source = jnp.repeat(block_of, 8) * 8 + jnp.tile(jnp.arange(8, dtype=jnp.int32), rows // 8)
    source = jnp.where(jnp.repeat(block_of, 8) < 0, -1, source)
    return (source[:, None] == jnp.arange(columns, dtype=jnp.int32)[None, :]).astype(jnp.bfloat16)


def per_device(clip_rows, velocity_target, plan, segment_ids, reward_levels, w_qkv, w_out):
    groups = lax.axis_size("dp")
    shards = lax.axis_size("seq")
    place = lax.axis_index("dp")
    shard = lax.axis_index("seq")
    crossed = shard // 2
    group = place ^ crossed
    rows_dev, width = clip_rows.shape
    counts = plan[place, shard]
    send_start = jnp.cumsum(counts) - counts

    def by_device(values):
        return jnp.where(crossed == 1, values.reshape(-1, 2)[:, ::-1].reshape(-1), values)

    counts, send_start = by_device(counts), by_device(send_start)
    slot_index = jnp.arange(CAP, dtype=jnp.int32)
    source_block = jnp.where(slot_index[None, :] < counts[:, None], send_start[:, None] + slot_index[None, :], -1).reshape(-1)
    pack = spread(source_block, rows_dev * CAP, rows_dev)

    def packed(source_rows):
        return jnp.dot(pack, source_rows, preferred_element_type=jnp.float32).astype(jnp.bfloat16).reshape(groups, CAP * 8, width)

    arriving = plan[:, shard, group]
    arriving_end = jnp.cumsum(arriving)
    slot_ids = jnp.arange(groups, dtype=jnp.int32)
    source_group = jnp.sum((arriving_end[None, :] <= slot_ids[:, None]).astype(jnp.int32), axis=1)
    arriving_start = (arriving_end - arriving)[source_group]
    flat_slot = source_group * CAP + slot_ids - arriving_start
    chosen = spread(flat_slot, rows_dev, rows_dev * CAP)

    segments = segment_ids.shape[1]
    labels = jnp.concatenate([segment_ids, jnp.pad(reward_levels, ((0, 0), (0, HD - reward_levels.shape[1])))], axis=1)
    labels = jnp.broadcast_to(labels, (8, segments + HD))
    group_x, weights, labels_there = gather_all(
        packed(clip_rows), jnp.concatenate([w_qkv, w_out], axis=1), chosen, labels)
    labels = jnp.where(crossed == 1, labels_there, labels)[0]
    segment_row = labels[:segments]
    clip_index = jnp.arange(reward_levels.shape[1], dtype=jnp.int32)
    levels = labels[segments:segments + reward_levels.shape[1]].astype(jnp.float32) / 8.0
    own_segment = lax.dynamic_slice(segment_row, (shard * rows_dev,), (rows_dev,))
    row_weight = jnp.sum(
        jnp.where(own_segment[:, None] == clip_index[None, :], levels[None, :], jnp.float32(0.0)),
        axis=1,
        keepdims=True,
    )
    loss_scale = 1.0 / math.sqrt(rows_dev * groups * shards)

    sign = (2 * segment_row - 1)[:, None]
    lane = jnp.arange(HD, dtype=jnp.int32)[None, :]
    mark_q = jnp.where(lane == 0, 64 * sign, jnp.where(lane == 1, -64, 0)).astype(jnp.bfloat16)
    mark_k = jnp.where(lane == 0, 32 * sign, jnp.where(lane == 1, 32, 0)).astype(jnp.bfloat16)

    pred_grad, *saved = forward(
        packed(velocity_target), chosen, group_x, weights, mark_q, mark_k, row_weight * loss_scale)
    return backward(pred_grad, group_x, weights, *saved)


def solution(mesh):
    return jax.shard_map(
        per_device,
        mesh=mesh,
        in_specs=(
            P(("dp", "seq"), None),
            P(("dp", "seq"), None),
            P(),
            P("dp", None),
            P("dp", None),
            P("dp", "seq"),
            P("dp", "seq"),
        ),
        out_specs=(P("dp", "seq"), P("dp", "seq")),
        check_vma=False,
    )
```

```python
import math

import jax
import jax.numpy as jnp
from jax import lax
from jax.experimental import pallas as pl
from jax.experimental.pallas import tpu as pltpu
from jax.sharding import PartitionSpec as P

HD = 128
CAP = 2
MESH = pl.DeviceIdType.MESH
VMEM_LIMIT = 60 * 1024 * 1024

epsilon = 1e-06


def my_place():
    dp = lax.axis_index("dp")
    seq = lax.axis_index("seq")
    return (dp // 8, (dp // 2) % 4, dp % 2, seq // 2, seq % 2)


def device(place):
    z, x, y, a, c = place
    return {"dp": z * 8 + x * 2 + y, "seq": a * 2 + c}


def moved(place, axis, by):
    place = list(place)
    size = (4, 4, 2, 2, 2)[axis]
    place[axis] = (place[axis] + by + size) % size
    return tuple(place)


Z, X, Y, A, C = range(5)


def chip_partner(place):
    return moved(moved(place, Y, 1), A, 1)


class Copies:
    def __init__(self, send_sem, recv_sem):
        self.send_sem, self.recv_sem, self.used = send_sem, recv_sem, 0
        self.started = []

    def start(self, src, dst, to):
        copy = pltpu.make_async_remote_copy(
            src_ref=src,
            dst_ref=dst,
            send_sem=self.send_sem.at[self.used],
            recv_sem=self.recv_sem.at[self.used],
            device_id=device(to),
            device_id_type=MESH,
        )
        self.used += 1
        copy.start()
        self.started.append(copy)
        return copy

    def finish(self):
        for copy in self.started:
            copy.wait_send()


def greet(places):
    barrier = pltpu.get_barrier_semaphore()
    for place in places:
        pl.semaphore_signal(barrier, inc=1, device_id=device(place), device_id_type=MESH)
    pl.semaphore_wait(barrier, len(places))


def dp_peer(place, k, sign):
    z, x, y, a, c = place
    dz, dx, dy = k // 8, (k // 2) % 4, k % 2
    return ((z + sign * dz + 4) % 4, (x + sign * dx + 4) % 4, (y + sign * dy + 2) % 2, a, c)


def ring_gather_start(copies, me, axis, part):
    own = me[axis]
    up, down = moved(me, axis, 1), moved(me, axis, -1)
    first_up = copies.start(part(own, 0), part(own, 0), up)
    first_down = copies.start(part(own, 1), part(own, 1), down)
    second_up = copies.start(part(own, 1), part(own, 1), up)
    second_down = copies.start(part(own, 0), part(own, 0), down)
    return first_up, first_down, second_up, second_down


def ring_gather_forward(copies, me, axis, part, sent):
    up, down = moved(me, axis, 1), moved(me, axis, -1)
    below, above = down[axis], up[axis]
    sent[0].wait_recv()
    third_up = copies.start(part(below, 0), part(below, 0), up)
    sent[1].wait_recv()
    third_down = copies.start(part(above, 1), part(above, 1), down)
    return sent[2], sent[3], third_up, third_down


CHUNKS = 4
HEADS = 3
QKV = HEADS * 3 * HD
OUT = HEADS * HD
SLABS = HEADS + 1
EXP2_SCALE = math.log2(math.e) / math.sqrt(HD)


def nt(left, right):
    return lax.dot_general(left, right, (((1,), (1,)), ((), ())), preferred_element_type=jnp.float32)


def tn(left, right):
    return lax.dot_general(left, right, (((0,), (0,)), ((), ())), preferred_element_type=jnp.float32)


def nn(left, right):
    return jnp.dot(left, right, preferred_element_type=jnp.float32)


MOVES = 2


def forward_kernel(
    packed, shard_qkv, shard_out, labels, chosen, pack, own_target,
    d_full, x_out, w_out, q_out, k_out, v_out, factors_out, inverse_out, mixed_out,
    w_full, x_full, received, packed_target, received_target, labels_there,
    q_marked, k_marked, v_half, v_turned, factors, inverse, mixed,
    partial, target, from_core, from_chip, d_own,
    a2a_send, a2a_recv, send_sem, recv_sem, local_sem,
):
    me = my_place()
    z, x, y, a, c = me
    dp = lax.axis_index("dp")
    rows, width = own_target.shape
    group_rows = x_full.shape[0]
    other_chip, other_core = chip_partner(me), moved(me, C, 1)
    barrier = pltpu.get_barrier_semaphore()

    @pl.loop(1, 32)
    def _(k):
        pl.semaphore_signal(barrier, inc=1, device_id=device(dp_peer(me, k, 1)), device_id_type=MESH)

    for place in (other_chip, other_core):
        pl.semaphore_signal(barrier, inc=1, device_id=device(place), device_id_type=MESH)

    locals_started = []

    def local_copy(src, dst):
        copy = pltpu.make_async_copy(src, dst, local_sem.at[len(locals_started)])
        copy.start()
        locals_started.append(copy)
        return copy

    shards = [
        local_copy(shard_qkv.at[:, :, h * 3 * HD:(h + 1) * 3 * HD], w_full.at[h, z, x, y]) for h in range(HEADS)
    ] + [local_copy(shard_out, w_full.at[HEADS, z, x, y])]
    own_block = local_copy(packed.at[dp], received.at[dp])
    for copy in shards:
        copy.wait()
    pl.semaphore_wait(barrier, 33)

    copies = Copies(send_sem, recv_sem)
    across = copies.start(w_full.at[:, z, x, y], w_full.at[:, z, x, y], moved(me, Y, 1))
    labels_across = copies.start(labels, labels_there, moved(me, Y, 1))

    def block_copy(which, src, dst, k):
        to = dp_peer(me, k, 1)
        return pltpu.make_async_remote_copy(
            src_ref=src.at[device(to)["dp"]],
            dst_ref=dst.at[dp],
            send_sem=a2a_send.at[which, k],
            recv_sem=a2a_recv.at[which, k],
            device_id=device(to),
            device_id_type=MESH,
        )

    @pl.loop(1, 32)
    def _(k):
        block_copy(0, packed, received, k).start()

    tile = 512

    @pl.loop(0, width // tile)
    def _(t):
        columns = pl.ds(pl.multiple_of(t * tile, tile), tile)
        blocks = nn(pack[...], own_target[:, columns]).astype(jnp.bfloat16)
        packed_target[:, :, columns] = blocks.reshape(packed_target.shape[0], packed_target.shape[1], tile)

    def select(src, dst):
        @pl.loop(0, width // tile)
        def _(t):
            columns = pl.ds(pl.multiple_of(t * tile, tile), tile)
            blocks = src[:, :, columns].reshape(rows * CAP, tile)
            dst[:, columns] = nn(chosen[...], blocks).astype(jnp.bfloat16)

    def near(half):
        if half == 0:
            return lambda at, which: w_full.at[:, at, x, which, 0]
        return lambda at, which: w_full.at[:, z, at, which, 1]

    def far(s, half):
        if half == 0:
            return lambda at, which: w_full.at[s, pl.ds(2 * which, 2), at, :, 0]
        return lambda at, which: w_full.at[s, at, pl.ds(2 * which, 2), :, 1]

    near_axis, far_axis = (Z, X), (X, Z)
    across.wait_recv()
    sent = [ring_gather_start(copies, me, near_axis[half], near(half)) for half in (0, 1)]
    rest = [ring_gather_forward(copies, me, near_axis[half], near(half), sent[half]) for half in (0, 1)]
    for half in (0, 1):
        for copy in rest[half]:
            copy.wait_recv()

    far_sent = {}

    def far_start(s):
        far_sent[s] = [ring_gather_start(copies, me, far_axis[half], far(s, half)) for half in (0, 1)]

    def far_forward(s):
        far_sent[s] = [ring_gather_forward(copies, me, far_axis[half], far(s, half), far_sent[s][half]) for half in (0, 1)]

    def far_wait(s):
        for half in (0, 1):
            for copy in far_sent[s][half]:
                copy.wait_recv()

    far_start(0)

    def rows_of(place, chunk=0, chunks=1):
        step = rows // chunks
        return pl.ds(pl.multiple_of(device(place)["seq"] * rows + chunk * step, step), step)

    own_block.wait()

    @pl.loop(1, 32)
    def _(k):
        block_copy(0, packed, received, k).wait_recv()

    select(received, x_full.at[rows_of(me)])
    x_chip = []
    for chunk in range(MOVES):
        at = rows_of(me, chunk, MOVES)
        x_chip.append(copies.start(x_full.at[at], x_full.at[at], other_chip))
    x_core = copies.start(x_full.at[rows_of(me)], x_full.at[rows_of(me)], other_core)
    far_start(1)

    labels_across.wait_recv()
    lane = lax.broadcasted_iota(jnp.int32, (rows, HD), 1)
    for i in range(group_rows // rows):
        at = slice(i * rows, (i + 1) * rows)
        segment = jnp.where(a == 1, labels_there[0:1, at], labels[0:1, at]).astype(jnp.float32)
        sign = jnp.broadcast_to(2.0 * segment - 1.0, (HD, rows)).T
        mark_q = jnp.where(lane == 0, 64.0 * sign, jnp.where(lane == 1, -64.0, 0.0)).astype(jnp.bfloat16)
        mark_k = jnp.where(lane == 0, 32.0 * sign, jnp.where(lane == 1, 32.0, 0.0)).astype(jnp.bfloat16)
        for h in range(HEADS):
            q_marked[h, at, HD:2 * HD] = mark_q
            k_marked[h, at, HD:2 * HD] = mark_k

    def project(h, chip):
        @pl.loop(0, 2)
        def _(i):
            at = pl.ds(pl.multiple_of((chip * 2 + i) * rows, rows), rows)
            raw = nn(x_full[at, :], w_full[h].reshape(width, 3 * HD))
            for part, marked in ((0, q_marked), (1, k_marked)):
                values = raw[:, part * HD:(part + 1) * HD]
                factor = lax.rsqrt(jnp.mean(values * values, axis=-1, keepdims=True) + epsilon)
                marked[h, at, 0:HD] = (values * factor).astype(jnp.bfloat16)
                factors[part, h, at, :] = jnp.broadcast_to(factor, (rows, HD))
            values = raw[:, 2 * HD:3 * HD]
            v_half[h, at, :] = values.astype(jnp.bfloat16)
            v_turned[h, :, at] = values.T.astype(jnp.bfloat16)

    def attend(h, at):
        scores = nt(k_marked[h], q_marked[h, at, :])
        raised = jnp.exp2(scores * EXP2_SCALE)
        inverse_sum = 1.0 / jnp.sum(raised, axis=0, keepdims=True)
        turned = nn(v_turned[h], raised.astype(jnp.bfloat16)) * inverse_sum
        mixed[at, h * HD:(h + 1) * HD] = turned.T.astype(jnp.bfloat16)
        inverse[h, at, :] = jnp.broadcast_to(inverse_sum, (HD, rows)).T

    def attend_all(h):
        @pl.loop(0, group_rows // rows)
        def _(i):
            attend(h, pl.ds(pl.multiple_of(i * rows, rows), rows))

    x_passed = []

    def x_pass(chunk):
        x_chip[chunk].wait_recv()
        at = rows_of(other_chip, chunk, MOVES)
        x_passed.append(copies.start(x_full.at[at], x_full.at[at], other_core))

    far_forward(0)
    x_core.wait_recv()
    far_wait(0)
    far_start(2)
    project(0, a)
    x_pass(0)
    far_forward(1)
    far_wait(1)
    far_start(3)
    project(1, a)
    far_forward(2)
    x_pass(1)
    far_wait(2)
    project(2, a)
    far_forward(3)

    @pl.loop(1, 32)
    def _(k):
        block_copy(1, packed_target, received_target, k).start()

    own_block = local_copy(packed_target.at[dp], received_target.at[dp])
    for copy in x_passed:
        copy.wait_recv()
    outs = [local_copy(x_full, x_out)]
    project(0, 1 - a)
    attend_all(0)
    project(1, 1 - a)
    attend_all(1)
    project(2, 1 - a)
    for src, dst in ((q_marked, q_out), (k_marked, k_out), (v_half, v_out), (factors, factors_out)):
        outs.append(local_copy(src, dst))
    far_wait(3)
    outs.append(local_copy(w_full.at[HEADS], w_out))

    def block(place):
        at = rows_of(place)
        attend(HEADS - 1, at)

        @pl.loop(0, 8)
        def _(t):
            weights = w_full[HEADS, t // 2, pl.ds(t % 2 * 2, 2)].reshape(3 * HD, OUT)
            columns = pl.ds(pl.multiple_of(t * 3 * HD, 3 * HD), 3 * HD)
            partial[at, columns] = nt(mixed[at, :], weights).astype(jnp.bfloat16)

    core_first, core_second, chip_sums = [], [], []
    step = rows // CHUNKS
    far_core = moved(other_chip, C, 1)
    block(far_core)
    for chunk in range(CHUNKS):
        core_first.append(copies.start(
            partial.at[rows_of(far_core, chunk, CHUNKS)], from_core.at[0, pl.ds(chunk * step, step)], other_core))
    block(other_chip)
    for chunk in range(CHUNKS):
        core_first[chunk].wait_recv()
        at = pl.ds(chunk * step, step)
        from_core[0, at] = (
            partial[rows_of(other_chip, chunk, CHUNKS)].astype(jnp.float32) + from_core[0, at].astype(jnp.float32)
        ).astype(jnp.bfloat16)
        chip_sums.append(copies.start(from_core.at[0, at], from_chip.at[at], other_chip))
    block(other_core)
    for chunk in range(CHUNKS):
        core_second.append(copies.start(
            partial.at[rows_of(other_core, chunk, CHUNKS)], from_core.at[1, pl.ds(chunk * step, step)], other_core))
    block(me)
    for src, dst in ((inverse, inverse_out), (mixed, mixed_out)):
        outs.append(local_copy(src, dst))

    own_block.wait()

    @pl.loop(1, 32)
    def _(k):
        block_copy(1, packed_target, received_target, k).wait_recv()

    select(received_target, target)
    own_lanes = rows_of(me)
    segment = jnp.where(a == 1, labels_there[0:1, own_lanes], labels[0:1, own_lanes]).astype(jnp.float32)
    first, second = (
        jnp.where(a == 1, labels_there[0:1, at:at + 1], labels[0:1, at:at + 1]).astype(jnp.float32)
        for at in (group_rows, group_rows + 1))
    loss_scale = 1.0 / math.sqrt(group_rows * 32)
    weight = (jnp.where(segment == 0.0, first, second) / 8.0) * loss_scale
    weight = jnp.broadcast_to(weight, (HD, rows)).T[:, 0:1]

    to_chip, to_core, passed = [], [], []
    for chunk in range(CHUNKS):
        core_second[chunk].wait_recv()
        chip_sums[chunk].wait_recv()
        at = slice(chunk * step, (chunk + 1) * step)
        mine = rows_of(me, chunk, CHUNKS)
        prediction = (
            x_full[mine].astype(jnp.float32)
            + (partial[mine].astype(jnp.float32) + from_core[1, at].astype(jnp.float32) + from_chip[at].astype(jnp.float32))
        )
        d_own[at] = (weight[at] * (prediction - target[at].astype(jnp.float32))).astype(jnp.bfloat16)
        to_chip.append(copies.start(d_own.at[at], d_full.at[mine], other_chip))
        to_core.append(copies.start(d_own.at[at], d_full.at[mine], other_core))
    outs.append(local_copy(d_own, d_full.at[rows_of(me)]))
    for chunk in range(CHUNKS):
        to_chip[chunk].wait_recv()
        theirs = rows_of(other_chip, chunk, CHUNKS)
        passed.append(copies.start(d_full.at[theirs], d_full.at[theirs], other_core))
    for chunk in range(CHUNKS):
        to_core[chunk].wait_recv()
        passed[chunk].wait_recv()

    @pl.loop(1, 32)
    def _(k):
        block_copy(0, packed, received, k).wait_send()
        block_copy(1, packed_target, received_target, k).wait_send()

    for copy in outs:
        copy.wait()
    copies.finish()


def forward(packed, shard_qkv, shard_out, labels, chosen, pack, own_target):
    rows, width = own_target.shape
    group_rows = rows * 4
    vmem = pl.BlockSpec(memory_space=pltpu.VMEM)
    hbm = pl.BlockSpec(memory_space=pl.ANY)
    half, full = jnp.bfloat16, jnp.float32
    saved = [
        ((HEADS, group_rows, 2 * HD), half),
        ((HEADS, group_rows, 2 * HD), half),
        ((HEADS, group_rows, HD), half),
        ((2, HEADS, group_rows, HD), full),
        ((HEADS, group_rows, HD), full),
        ((group_rows, OUT), half),
    ]
    q_shape, k_shape, v_shape, factors_shape, inverse_shape, mixed_shape = saved
    scratch = [
        ((SLABS, 4, 4, 2, 2, 48, 3 * HD), half),
        ((group_rows, width), half),
        (packed.shape, half),
        (packed.shape, half),
        (packed.shape, half),
        (labels.shape, labels.dtype),
        q_shape,
        k_shape,
        v_shape,
        ((HEADS, HD, group_rows), half),
        factors_shape,
        inverse_shape,
        mixed_shape,
        ((group_rows, width), half),
        ((rows, width), half),
        ((2, rows, width), half),
        ((rows, width), half),
        ((rows, width), half),
    ]
    sems = 6 + 12 + 12 * SLABS + 2 * MOVES + 1 + 6 * CHUNKS
    return pl.pallas_call(
        forward_kernel,
        out_shape=tuple(
            jax.ShapeDtypeStruct(*shape)
            for shape in [((group_rows, width), half), ((group_rows, width), half), ((4, 4, 2, 2, 48, OUT), half)] + saved
        ),
        in_specs=[hbm] * 3 + [vmem] * 4,
        out_specs=(hbm,) * 9,
        scratch_shapes=[pltpu.VMEM(*shape) for shape in scratch] + [
            pltpu.SemaphoreType.DMA((2, 32)),
            pltpu.SemaphoreType.DMA((2, 32)),
            pltpu.SemaphoreType.DMA((sems,)),
            pltpu.SemaphoreType.DMA((sems,)),
            pltpu.SemaphoreType.DMA((16,)),
        ],
        compiler_params=pltpu.CompilerParams(collective_id=2, has_side_effects=True, vmem_limit_bytes=VMEM_LIMIT),
        name="forward_residual_gradient",
    )(packed, shard_qkv.reshape(2, 48, QKV), shard_out.reshape(2, 48, OUT), labels, chosen, pack, own_target)


def added(*values):
    total = values[0].astype(jnp.float32)
    for value in values[1:]:
        total = total + value.astype(jnp.float32)
    return total


def reduce_start(copies, me, axis, block, got):
    up, down = moved(me, axis, 1), moved(me, axis, -1)
    opposite = moved(me, axis, 2)[axis]
    far_up = copies.start(block(opposite, 0), got(0), up)
    far_down = copies.start(block(opposite, 1), got(1), down)
    near_up = copies.start(block(up[axis], 1), got(2), up)
    near_down = copies.start(block(down[axis], 0), got(3), down)
    return far_up, far_down, near_up, near_down


def reduce_pass(copies, me, axis, block, got, sums, sent, add):
    up, down = moved(me, axis, 1), moved(me, axis, -1)
    sent[0].wait_recv()
    add(sums(0), [block(up[axis], 0), got(0)])
    sum_up = copies.start(sums(0), got(4), up)
    sent[1].wait_recv()
    add(sums(1), [block(down[axis], 1), got(1)])
    sum_down = copies.start(sums(1), got(5), down)
    return sent[2], sent[3], sum_up, sum_down


def reduce_end(me, axis, block, got, out, sent, add):
    sent[1].wait_recv()
    sent[2].wait_recv()
    add(out(0), [block(me[axis], 0), got(3), got(4)])
    sent[0].wait_recv()
    sent[3].wait_recv()
    add(out(1), [block(me[axis], 1), got(2), got(5)])


def add_rows(out, parts):
    lead = out.shape[:-2]
    count = math.prod(lead)

    @pl.loop(0, count)
    def _(i):
        index, rest = [], i
        for size in reversed(lead):
            index.insert(0, rest % size)
            rest = rest // size
        index = tuple(index)
        out[index] = added(*[part[index] for part in parts]).astype(out.dtype)


def backward_kernel(
    d_full, x_full, w_out, q_marked, k_marked, v_half, factors, inverse, mixed,
    qkv_sums, out_sums,
    d_out, k_turned, dq, dk, dv, d_proj,
    grads, got_far, sum_far, half_far, got_near, sum_near, half_near, got_last, send_sem, recv_sem,
):
    me = my_place()
    z, x, y, a, c = me
    greet([moved(me, Z, 1), moved(me, Z, -1), moved(me, X, 1), moved(me, X, -1), moved(me, Y, 1)])
    copies = Copies(send_sem, recv_sem)
    far_axis, near_axis = (X, Z), (Z, X)
    group_rows, width = x_full.shape
    rows = group_rows // 4
    scale = 1.0 / math.sqrt(HD)

    class Slab:
        def __init__(self, s):
            self.s = s

        def far_block(self, half):
            if half == 0:
                return lambda at, which: grads.at[self.s, pl.ds(2 * which, 2), at, :, 0]
            return lambda at, which: grads.at[self.s, at, pl.ds(2 * which, 2), :, 1]

        def near_block(self, half):
            return lambda at, which: half_far.at[self.s, half, at, which]

        def slots(self, ref, half):
            return lambda j: ref.at[self.s, half, j]

        def far_out(self, half):
            return lambda which: half_far.at[self.s, half, pl.ds(2 * which, 2)]

        def near_out(self, half):
            return lambda which: half_near.at[self.s, half, pl.ds(which, 1)]

        def far_start(self):
            self.sent = [
                reduce_start(copies, me, far_axis[h], self.far_block(h), self.slots(got_far, h)) for h in (0, 1)]

        def far_pass(self):
            self.sent = [
                reduce_pass(copies, me, far_axis[h], self.far_block(h), self.slots(got_far, h),
                            self.slots(sum_far, h), self.sent[h], add_rows)
                for h in (0, 1)]

        def near_start(self):
            for h in (0, 1):
                reduce_end(me, far_axis[h], self.far_block(h), self.slots(got_far, h), self.far_out(h), self.sent[h], add_rows)
            self.sent = [
                reduce_start(copies, me, near_axis[h], self.near_block(h), self.slots(got_near, h)) for h in (0, 1)]

        def near_pass(self):
            self.sent = [
                reduce_pass(copies, me, near_axis[h], self.near_block(h), self.slots(got_near, h),
                            self.slots(sum_near, h), self.sent[h], near_add)
                for h in (0, 1)]

        def last_start(self):
            for h in (0, 1):
                reduce_end(me, near_axis[h], self.near_block(h), self.slots(got_near, h), self.near_out(h), self.sent[h], near_add)
            self.sent = [
                copies.start(half_near.at[self.s, h, 1 - y], got_last.at[self.s, h], moved(me, Y, 1)) for h in (0, 1)]

        def end(self):
            for h in (0, 1):
                self.sent[h].wait_recv()
                total = added(half_near[self.s, h, y], got_last[self.s, h])
                if self.s == HEADS:
                    out_sums[h] = total
                else:
                    qkv_sums[h, :, self.s * 3 * HD:(self.s + 1) * 3 * HD] = total

    def near_add(out, parts):
        out[...] = added(*[part[...] for part in parts]).astype(out.dtype).reshape(out.shape)

    def weight_grads(s, left, right):
        @pl.loop(0, 8)
        def _(t):
            columns = pl.ds(pl.multiple_of(t * 384, 384), 384)
            term = tn(left[:, columns], right[...]).astype(jnp.bfloat16)
            grads[s, t // 2, pl.ds(t % 2 * 2, 2)] = term.reshape(2, 2, 2, 48, 384)

    def head(h):
        head_columns = slice(h * HD, (h + 1) * HD)

        @pl.loop(0, 4)
        def _(i):
            at = pl.ds(pl.multiple_of(i * rows, rows), rows)
            k_turned[:, at] = k_marked[h, at, 0:HD].astype(jnp.float32).T.astype(jnp.bfloat16)

        dk[...] = jnp.zeros_like(dk)
        dv[...] = jnp.zeros_like(dv)

        @pl.loop(0, 4)
        def _(i):
            at = pl.ds(pl.multiple_of(i * rows, rows), rows)
            raised = jnp.exp2(nt(k_marked[h], q_marked[h, at, :]) * EXP2_SCALE)
            d_here = d_out[at, head_columns]
            delta = jnp.sum((d_here.astype(jnp.float32) * mixed[at, head_columns].astype(jnp.float32)).T, axis=0, keepdims=True)
            d_scores = (raised * (nt(v_half[h], d_here) - delta)).astype(jnp.bfloat16)
            dv[...] += nn(raised.astype(jnp.bfloat16), d_here)
            dk[...] += nn(d_scores, q_marked[h, at, 0:HD])
            dq[at, :] = nn(k_turned[...], d_scores).T

        @pl.loop(0, 4)
        def _(i):
            at = pl.ds(pl.multiple_of(i * rows, rows), rows)
            for part, grad, marked in ((0, dq, q_marked), (1, dk, k_marked)):
                normed = marked[h, at, 0:HD].astype(jnp.float32)
                got = grad[at, :]
                inner = jnp.mean(got * normed, axis=-1, keepdims=True)
                d_proj[at, part * HD:(part + 1) * HD] = (
                    (factors[part, h, at, :] * scale) * (got - normed * inner)).astype(jnp.bfloat16)
            d_proj[at, 2 * HD:3 * HD] = dv[at, :].astype(jnp.bfloat16)

    out_slab = Slab(HEADS)
    slabs = [Slab(h) for h in range(HEADS)]
    weight_grads(HEADS, d_full, mixed)
    out_slab.far_start()

    @pl.loop(0, 4)
    def _(i):
        at = pl.ds(pl.multiple_of(i * rows, rows), rows)
        got = nn(d_full[at, :], w_out[...])
        for h in range(HEADS):
            d_out[at, h * HD:(h + 1) * HD] = (got[:, h * HD:(h + 1) * HD] * inverse[h, at, :]).astype(jnp.bfloat16)

    head(0)
    out_slab.far_pass()
    weight_grads(0, x_full, d_proj)
    slabs[0].far_start()
    out_slab.near_start()
    head(1)
    slabs[0].far_pass()
    out_slab.near_pass()
    weight_grads(1, x_full, d_proj)
    slabs[1].far_start()
    slabs[0].near_start()
    out_slab.last_start()
    head(2)
    slabs[1].far_pass()
    slabs[0].near_pass()
    out_slab.end()
    weight_grads(2, x_full, d_proj)
    slabs[2].far_start()
    slabs[1].near_start()
    slabs[0].last_start()
    slabs[2].far_pass()
    slabs[1].near_pass()
    slabs[0].end()
    slabs[2].near_start()
    slabs[1].last_start()
    slabs[2].near_pass()
    slabs[1].end()
    slabs[2].last_start()
    slabs[2].end()
    copies.finish()


def backward(d_full, x_full, w_out, q_marked, k_marked, v_half, factors, inverse, mixed):
    group_rows, width = x_full.shape
    half = lambda *lead: pltpu.VMEM((SLABS, 2, *lead, 48, 3 * HD), jnp.bfloat16)
    vmem = pl.BlockSpec(memory_space=pltpu.VMEM)
    qkv_sums, out_sums = pl.pallas_call(
        backward_kernel,
        out_shape=(
            jax.ShapeDtypeStruct((2, 48, QKV), jnp.float32),
            jax.ShapeDtypeStruct((2, 48, OUT), jnp.float32),
        ),
        in_specs=[vmem] * 9,
        out_specs=(vmem, vmem),
        scratch_shapes=[
            pltpu.VMEM((group_rows, OUT), jnp.bfloat16),
            pltpu.VMEM((HD, group_rows), jnp.bfloat16),
            pltpu.VMEM((group_rows, HD), jnp.float32),
            pltpu.VMEM((group_rows, HD), jnp.float32),
            pltpu.VMEM((group_rows, HD), jnp.float32),
            pltpu.VMEM((group_rows, 3 * HD), jnp.bfloat16),
            pltpu.VMEM((SLABS, 4, 4, 2, 2, 48, 3 * HD), jnp.bfloat16),
            half(6, 2, 2),
            half(2, 2, 2),
            half(4, 2),
            half(6),
            half(2),
            half(2),
            half(),
            pltpu.SemaphoreType.DMA((26 * SLABS,)),
            pltpu.SemaphoreType.DMA((26 * SLABS,)),
        ],
        compiler_params=pltpu.CompilerParams(collective_id=3, has_side_effects=True, vmem_limit_bytes=VMEM_LIMIT),
        name="backward_scatter",
    )(d_full, x_full, w_out.reshape(width, OUT), q_marked, k_marked, v_half, factors, inverse, mixed)
    return qkv_sums.reshape(96, QKV), out_sums.reshape(96, OUT)


def spread(block_of, rows, columns):
    source = jnp.repeat(block_of, 8) * 8 + jnp.tile(jnp.arange(8, dtype=jnp.int32), rows // 8)
    source = jnp.where(jnp.repeat(block_of, 8) < 0, -1, source)
    return (source[:, None] == jnp.arange(columns, dtype=jnp.int32)[None, :]).astype(jnp.bfloat16)


def per_device(clip_rows, velocity_target, plan, segment_ids, reward_levels, w_qkv, w_out):
    groups = lax.axis_size("dp")
    shards = lax.axis_size("seq")
    place = lax.axis_index("dp")
    shard = lax.axis_index("seq")
    crossed = shard // 2
    group = place ^ crossed
    rows_dev, width = clip_rows.shape
    counts = plan[place, shard]
    send_start = jnp.cumsum(counts) - counts

    def by_device(values):
        return jnp.where(crossed == 1, values.reshape(-1, 2)[:, ::-1].reshape(-1), values)

    counts, send_start = by_device(counts), by_device(send_start)
    slot_index = jnp.arange(CAP, dtype=jnp.int32)
    source_block = jnp.where(slot_index[None, :] < counts[:, None], send_start[:, None] + slot_index[None, :], -1).reshape(-1)
    pack = spread(source_block, rows_dev * CAP, rows_dev)

    def packed(source_rows):
        return jnp.dot(pack, source_rows, preferred_element_type=jnp.float32).astype(jnp.bfloat16).reshape(groups, CAP * 8, width)

    arriving = plan[:, shard, group]
    arriving_end = jnp.cumsum(arriving)
    slot_ids = jnp.arange(groups, dtype=jnp.int32)
    source_group = jnp.sum((arriving_end[None, :] <= slot_ids[:, None]).astype(jnp.int32), axis=1)
    arriving_start = (arriving_end - arriving)[source_group]
    flat_slot = source_group * CAP + slot_ids - arriving_start
    chosen = spread(flat_slot, rows_dev, rows_dev * CAP)

    segments = segment_ids.shape[1]
    labels = jnp.concatenate([segment_ids, jnp.pad(reward_levels, ((0, 0), (0, HD - reward_levels.shape[1])))], axis=1)
    labels = jnp.broadcast_to(labels, (8, segments + HD))
    return backward(*forward(packed(clip_rows), w_qkv, w_out, labels, chosen, pack, velocity_target))


def solution(mesh):
    return jax.shard_map(
        per_device,
        mesh=mesh,
        in_specs=(
            P(("dp", "seq"), None),
            P(("dp", "seq"), None),
            P(),
            P("dp", None),
            P("dp", None),
            P("dp", "seq"),
            P("dp", "seq"),
        ),
        out_specs=(P("dp", "seq"), P("dp", "seq")),
        check_vma=False,
    )
```

```python
import math

import jax
import jax.numpy as jnp
from jax import lax
from jax.experimental import pallas as pl
from jax.experimental.pallas import tpu as pltpu
from jax.sharding import PartitionSpec as P

HD = 128
CAP = 2
MESH = pl.DeviceIdType.MESH
VMEM_LIMIT = 60 * 1024 * 1024

epsilon = 1e-06


def my_place():
    dp = lax.axis_index("dp")
    seq = lax.axis_index("seq")
    return (dp // 8, (dp // 2) % 4, dp % 2, seq // 2, seq % 2)


def device(place):
    z, x, y, a, c = place
    return {"dp": z * 8 + x * 2 + y, "seq": a * 2 + c}


def moved(place, axis, by):
    place = list(place)
    size = (4, 4, 2, 2, 2)[axis]
    place[axis] = (place[axis] + by + size) % size
    return tuple(place)


Z, X, Y, A, C = range(5)


def chip_partner(place):
    return moved(moved(place, Y, 1), A, 1)


class Copies:
    def __init__(self, send_sem, recv_sem):
        self.send_sem, self.recv_sem, self.used = send_sem, recv_sem, 0
        self.started = []

    def start(self, src, dst, to):
        copy = pltpu.make_async_remote_copy(
            src_ref=src,
            dst_ref=dst,
            send_sem=self.send_sem.at[self.used],
            recv_sem=self.recv_sem.at[self.used],
            device_id=device(to),
            device_id_type=MESH,
        )
        self.used += 1
        copy.start()
        self.started.append(copy)
        return copy

    def finish(self):
        for copy in self.started:
            copy.wait_send()


def greet(places):
    barrier = pltpu.get_barrier_semaphore()
    for place in places:
        pl.semaphore_signal(barrier, inc=1, device_id=device(place), device_id_type=MESH)
    pl.semaphore_wait(barrier, len(places))


def dp_peer(place, k, sign):
    z, x, y, a, c = place
    k = (k * 13) % 32
    sign = sign * (1 - 2 * c)
    dz, dx, dy = k // 8, (k // 2) % 4, k % 2
    return ((z + sign * dz + 4) % 4, (x + sign * dx + 4) % 4, (y + sign * dy + 2) % 2, a, c)


def ring_gather_start(copies, me, axis, part):
    own = me[axis]
    up, down = moved(me, axis, 1), moved(me, axis, -1)
    first_up = copies.start(part(own, 0), part(own, 0), up)
    first_down = copies.start(part(own, 1), part(own, 1), down)
    second_up = copies.start(part(own, 1), part(own, 1), up)
    second_down = copies.start(part(own, 0), part(own, 0), down)
    return first_up, first_down, second_up, second_down


def ring_gather_forward(copies, me, axis, part, sent):
    up, down = moved(me, axis, 1), moved(me, axis, -1)
    below, above = down[axis], up[axis]
    sent[0].wait_recv()
    third_up = copies.start(part(below, 0), part(below, 0), up)
    sent[1].wait_recv()
    third_down = copies.start(part(above, 1), part(above, 1), down)
    return sent[2], sent[3], third_up, third_down


CHUNKS = 4
HEADS = 3
QKV = HEADS * 3 * HD
OUT = HEADS * HD
SLABS = HEADS + 1
EXP2_SCALE = math.log2(math.e) / math.sqrt(HD)


def nt(left, right):
    return lax.dot_general(left, right, (((1,), (1,)), ((), ())), preferred_element_type=jnp.float32)


def tn(left, right):
    return lax.dot_general(left, right, (((0,), (0,)), ((), ())), preferred_element_type=jnp.float32)


def nn(left, right):
    return jnp.dot(left, right, preferred_element_type=jnp.float32)


MOVES = 3


def forward_kernel(
    plan, shard_qkv, shard_out, segments, levels, own_rows, own_target,
    d_full, x_out, w_out, q_out, k_out, v_out, factors_out, inverse_out, mixed_out,
    w_full, x_full, packed, received, received_target, labels, labels_there, pack, chosen,
    q_marked, k_marked, v_half, v_turned, factors, inverse, mixed,
    partial, target, from_core, from_chip, d_own,
    a2a_send, a2a_recv, send_sem, recv_sem, local_sem,
):
    me = my_place()
    z, x, y, a, c = me
    dp = lax.axis_index("dp")
    rows, width = own_target.shape
    group_rows = x_full.shape[0]
    other_chip, other_core = chip_partner(me), moved(me, C, 1)
    barrier = pltpu.get_barrier_semaphore()

    @pl.loop(1, 32)
    def _(k):
        pl.semaphore_signal(barrier, inc=1, device_id=device(dp_peer(me, k, 1)), device_id_type=MESH)

    for place in (other_chip, other_core):
        pl.semaphore_signal(barrier, inc=1, device_id=device(place), device_id_type=MESH)

    locals_started = []

    def local_copy(src, dst):
        copy = pltpu.make_async_copy(src, dst, local_sem.at[len(locals_started)])
        copy.start()
        locals_started.append(copy)
        return copy

    shards = [
        local_copy(shard_qkv.at[:, :, h * 3 * HD:(h + 1) * 3 * HD], w_full.at[h, z, x, y]) for h in range(HEADS)
    ] + [local_copy(shard_out, w_full.at[HEADS, z, x, y])]
    tile = width // MOVES

    def iota(shape, axis):
        return lax.broadcasted_iota(jnp.int32, shape, axis)

    def one_where(condition):
        return jnp.where(condition, 1.0, 0.0).astype(jnp.bfloat16)

    shards_of, groups = 4, 32
    group = dp + a * (1 - 2 * y)
    plan_half = plan[...].astype(jnp.float32).astype(jnp.bfloat16)
    before = one_where(iota((groups, groups), 0) < iota((groups, groups), 1))
    counts = nn(one_where(iota((8, groups * shards_of), 1) == dp * shards_of + a * 2 + c), plan_half).astype(jnp.bfloat16)
    starts = nn(counts, before).astype(jnp.bfloat16)
    to_group = iota((rows * CAP, groups), 1)
    to_group = to_group + a * (1 - 2 * (to_group & 1))
    here = one_where((iota((rows * CAP, groups), 0) >> 4) == to_group)
    of_row = iota((rows * CAP, 1), 0)
    which = ((of_row >> 3) & 1).astype(jnp.float32)
    source = (nt(here, starts)[:, 0:1] + which) * 8.0 + (of_row & 7).astype(jnp.float32)
    source = jnp.where(which < nt(here, counts)[:, 0:1], source, -1.0)
    pack[...] = one_where(iota((rows * CAP, rows), 1).astype(jnp.float32) == source)
    arriving = nn(
        one_where(iota((groups, groups * shards_of), 1) == iota((groups, groups * shards_of), 0) * shards_of + a * 2 + c), plan_half)
    arriving = jnp.where(iota((groups, groups), 1) == group, arriving, 0.0).astype(jnp.bfloat16)
    counts = nt(jnp.ones((8, groups), jnp.bfloat16), arriving).astype(jnp.bfloat16)
    starts = nn(counts, before).astype(jnp.bfloat16)
    there = one_where((iota((groups, rows * CAP), 1) >> 4) == iota((groups, rows * CAP), 0))
    of_column = iota((1, rows * CAP), 1)
    which = ((of_column >> 3) & 1).astype(jnp.float32)
    slot = nn(starts, there)[0:1, :] + which
    slot = jnp.where(which < nn(counts, there)[0:1, :], slot, -1.0)
    place = slot * 8.0 + (of_column & 7).astype(jnp.float32)
    chosen[...] = one_where(iota((rows, rows * CAP), 0).astype(jnp.float32) == place)

    labels[:, 0:group_rows] = jnp.broadcast_to(segments[...], (8, group_rows))
    lane = iota((8, HD), 1)
    labels[:, group_rows:group_rows + HD] = jnp.where(lane == 0, levels[0:1, 0:1], jnp.where(lane == 1, levels[0:1, 1:2], 0))

    def fill(src, chunk):
        for low in range(chunk * tile, (chunk + 1) * tile, 512):
            blocks = nn(pack[...], src[:, low:low + 512]).astype(jnp.bfloat16)
            packed[:, :, low:low + 512] = blocks.reshape(packed.shape[0], packed.shape[1], 512)

    def block_copy(chunk, k):
        to = dp_peer(me, k, 1)
        dst = received_target if chunk == MOVES else received
        columns = slice(None) if chunk == MOVES else slice(chunk * tile, (chunk + 1) * tile)
        return pltpu.make_async_remote_copy(
            src_ref=packed.at[device(to)["dp"], :, columns],
            dst_ref=dst.at[dp, :, columns],
            send_sem=a2a_send.at[chunk, k],
            recv_sem=a2a_recv.at[chunk, k],
            device_id=device(to),
            device_id_type=MESH,
        )

    def own_block_copy(chunk):
        dst = received_target if chunk == MOVES else received
        columns = slice(None) if chunk == MOVES else slice(chunk * tile, (chunk + 1) * tile)
        return local_copy(packed.at[dp, :, columns], dst.at[dp, :, columns])

    fill(own_rows, 0)
    for copy in shards:
        copy.wait()
    pl.semaphore_wait(barrier, 33)

    copies = Copies(send_sem, recv_sem)
    across = copies.start(w_full.at[:, z, x, y], w_full.at[:, z, x, y], moved(me, Y, 1))
    labels_across = copies.start(labels, labels_there, moved(me, Y, 1))
    own_blocks = []
    for chunk in range(MOVES):
        if chunk:
            fill(own_rows, chunk)

        @pl.loop(1, 32)
        def _(k):
            block_copy(chunk, k).start()

        own_blocks.append(own_block_copy(chunk))

    def select(src, dst, at, chunk):
        for low in range(chunk * tile, (chunk + 1) * tile, 512):
            blocks = src[:, :, low:low + 512].reshape(rows * CAP, 512)
            dst[at, low:low + 512] = nn(chosen[...], blocks).astype(jnp.bfloat16)

    def near(half):
        if half == 0:
            return lambda at, which: w_full.at[:, at, x, which, 0]
        return lambda at, which: w_full.at[:, z, at, which, 1]

    def far(s, half):
        if half == 0:
            return lambda at, which: w_full.at[s, pl.ds(2 * which, 2), at, :, 0]
        return lambda at, which: w_full.at[s, at, pl.ds(2 * which, 2), :, 1]

    near_axis, far_axis = (Z, X), (X, Z)
    across.wait_recv()
    sent = [ring_gather_start(copies, me, near_axis[half], near(half)) for half in (0, 1)]
    rest = [ring_gather_forward(copies, me, near_axis[half], near(half), sent[half]) for half in (0, 1)]
    for half in (0, 1):
        for copy in rest[half]:
            copy.wait_recv()

    far_sent = {}

    def far_start(s):
        far_sent[s] = [ring_gather_start(copies, me, far_axis[half], far(s, half)) for half in (0, 1)]

    def far_forward(s):
        far_sent[s] = [ring_gather_forward(copies, me, far_axis[half], far(s, half), far_sent[s][half]) for half in (0, 1)]

    def far_wait(s):
        for half in (0, 1):
            for copy in far_sent[s][half]:
                copy.wait_recv()

    far_start(0)

    def rows_of(place, chunk=0, chunks=1):
        step = rows // chunks
        return pl.ds(pl.multiple_of(device(place)["seq"] * rows + chunk * step, step), step)

    x_chip, x_core, x_passed = [], [], []

    def x_arrive(chunk):
        own_blocks[chunk].wait()

        @pl.loop(1, 32)
        def _(k):
            block_copy(chunk, k).wait_recv()

        at = rows_of(me)
        select(received, x_full, at, chunk)
        part = x_full.at[at, chunk * tile:(chunk + 1) * tile]
        x_chip.append(copies.start(part, part, other_chip))
        x_core.append(copies.start(part, part, other_core))

    def x_pass(chunk):
        x_chip[chunk].wait_recv()
        part = x_full.at[rows_of(other_chip), chunk * tile:(chunk + 1) * tile]
        x_passed.append(copies.start(part, part, other_core))

    x_arrive(0)
    far_start(1)

    labels_across.wait_recv()
    lane = iota((rows, HD), 1)
    for i in range(group_rows // rows):
        at = slice(i * rows, (i + 1) * rows)
        segment = jnp.where(a == 1, labels_there[0:1, at], labels[0:1, at]).astype(jnp.float32)
        sign = jnp.broadcast_to(2.0 * segment - 1.0, (HD, rows)).T
        mark_q = jnp.where(lane == 0, 64.0 * sign, jnp.where(lane == 1, -64.0, 0.0)).astype(jnp.bfloat16)
        mark_k = jnp.where(lane == 0, 32.0 * sign, jnp.where(lane == 1, 32.0, 0.0)).astype(jnp.bfloat16)
        for h in range(HEADS):
            q_marked[h, at, HD:2 * HD] = mark_q
            k_marked[h, at, HD:2 * HD] = mark_k

    def project(h, chip):
        @pl.loop(0, 2)
        def _(i):
            at = pl.ds(pl.multiple_of((chip * 2 + i) * rows, rows), rows)
            raw = nn(x_full[at, :], w_full[h].reshape(width, 3 * HD))
            for part, marked in ((0, q_marked), (1, k_marked)):
                values = raw[:, part * HD:(part + 1) * HD]
                factor = lax.rsqrt(jnp.mean(values * values, axis=-1, keepdims=True) + epsilon)
                marked[h, at, 0:HD] = (values * factor).astype(jnp.bfloat16)
                factors[part, h, at, :] = jnp.broadcast_to(factor, (rows, HD))
            values = raw[:, 2 * HD:3 * HD]
            v_half[h, at, :] = values.astype(jnp.bfloat16)
            v_turned[h, :, at] = values.T.astype(jnp.bfloat16)

    def attend(h, at):
        scores = nt(k_marked[h], q_marked[h, at, :])
        raised = jnp.exp2(scores * EXP2_SCALE)
        inverse_sum = 1.0 / jnp.sum(raised, axis=0, keepdims=True)
        turned = nn(v_turned[h], raised.astype(jnp.bfloat16)) * inverse_sum
        mixed[at, h * HD:(h + 1) * HD] = turned.T.astype(jnp.bfloat16)
        inverse[h, at, :] = jnp.broadcast_to(inverse_sum, (HD, rows)).T

    def attend_all(h):
        @pl.loop(0, group_rows // rows)
        def _(i):
            attend(h, pl.ds(pl.multiple_of(i * rows, rows), rows))

    x_arrive(1)
    x_pass(0)
    far_forward(0)
    x_arrive(2)
    far_wait(0)
    far_start(2)
    far_forward(1)
    x_pass(1)
    for copy in x_core:
        copy.wait_recv()
    project(0, a)
    far_wait(1)
    far_start(3)
    project(1, a)
    far_forward(2)
    x_pass(2)
    for copy in x_passed:
        copy.wait_recv()
    outs = [local_copy(x_full, x_out)]
    project(0, 1 - a)
    far_forward(3)
    attend_all(0)
    for chunk in range(MOVES):
        @pl.loop(1, 32)
        def _(k):
            block_copy(chunk, k).wait_send()

    for chunk in range(MOVES):
        fill(own_target, chunk)

    @pl.loop(1, 32)
    def _(k):
        block_copy(MOVES, k).start()

    own_block = own_block_copy(MOVES)
    project(1, 1 - a)
    attend_all(1)
    far_wait(2)
    project(2, a)
    project(2, 1 - a)
    for src, dst in ((q_marked, q_out), (k_marked, k_out), (v_half, v_out), (factors, factors_out)):
        outs.append(local_copy(src, dst))
    far_wait(3)
    outs.append(local_copy(w_full.at[HEADS], w_out))

    def block(place):
        at = rows_of(place)
        attend(HEADS - 1, at)

        @pl.loop(0, 8)
        def _(t):
            weights = w_full[HEADS, t // 2, pl.ds(t % 2 * 2, 2)].reshape(3 * HD, OUT)
            columns = pl.ds(pl.multiple_of(t * 3 * HD, 3 * HD), 3 * HD)
            partial[at, columns] = nt(mixed[at, :], weights).astype(jnp.bfloat16)

    core_first, core_second, chip_sums = [], [], []
    step = rows // CHUNKS
    far_core = moved(other_chip, C, 1)
    block(far_core)
    for chunk in range(CHUNKS):
        core_first.append(copies.start(
            partial.at[rows_of(far_core, chunk, CHUNKS)], from_core.at[0, pl.ds(chunk * step, step)], other_core))
    block(other_chip)
    for chunk in range(CHUNKS):
        core_first[chunk].wait_recv()
        at = pl.ds(chunk * step, step)
        from_core[0, at] = (
            partial[rows_of(other_chip, chunk, CHUNKS)].astype(jnp.float32) + from_core[0, at].astype(jnp.float32)
        ).astype(jnp.bfloat16)
        chip_sums.append(copies.start(from_core.at[0, at], from_chip.at[at], other_chip))
    block(other_core)
    for chunk in range(CHUNKS):
        core_second.append(copies.start(
            partial.at[rows_of(other_core, chunk, CHUNKS)], from_core.at[1, pl.ds(chunk * step, step)], other_core))
    block(me)
    for src, dst in ((inverse, inverse_out), (mixed, mixed_out)):
        outs.append(local_copy(src, dst))

    own_block.wait()

    @pl.loop(1, 32)
    def _(k):
        block_copy(MOVES, k).wait_recv()

    for chunk in range(MOVES):
        select(received_target, target, slice(None), chunk)
    own_lanes = rows_of(me)
    segment = jnp.where(a == 1, labels_there[0:1, own_lanes], labels[0:1, own_lanes]).astype(jnp.float32)
    first, second = (
        jnp.where(a == 1, labels_there[0:1, at:at + 1], labels[0:1, at:at + 1]).astype(jnp.float32)
        for at in (group_rows, group_rows + 1))
    loss_scale = 1.0 / math.sqrt(group_rows * 32)
    weight = (jnp.where(segment == 0.0, first, second) / 8.0) * loss_scale
    weight = jnp.broadcast_to(weight, (HD, rows)).T[:, 0:1]

    to_chip, to_core, passed = [], [], []
    for chunk in range(CHUNKS):
        core_second[chunk].wait_recv()
        chip_sums[chunk].wait_recv()
        at = slice(chunk * step, (chunk + 1) * step)
        mine = rows_of(me, chunk, CHUNKS)
        prediction = (
            x_full[mine].astype(jnp.float32)
            + (partial[mine].astype(jnp.float32) + from_core[1, at].astype(jnp.float32) + from_chip[at].astype(jnp.float32))
        )
        d_own[at] = (weight[at] * (prediction - target[at].astype(jnp.float32))).astype(jnp.bfloat16)
        to_chip.append(copies.start(d_own.at[at], d_full.at[mine], other_chip))
        to_core.append(copies.start(d_own.at[at], d_full.at[mine], other_core))
    outs.append(local_copy(d_own, d_full.at[rows_of(me)]))
    for chunk in range(CHUNKS):
        to_chip[chunk].wait_recv()
        theirs = rows_of(other_chip, chunk, CHUNKS)
        passed.append(copies.start(d_full.at[theirs], d_full.at[theirs], other_core))
    for chunk in range(CHUNKS):
        to_core[chunk].wait_recv()
        passed[chunk].wait_recv()

    @pl.loop(1, 32)
    def _(k):
        block_copy(MOVES, k).wait_send()

    for copy in outs:
        copy.wait()
    copies.finish()


def forward(plan, shard_qkv, shard_out, segments, levels, own_rows, own_target):
    rows, width = own_target.shape
    group_rows = rows * 4
    blocks = (32, CAP * 8, width)
    vmem = pl.BlockSpec(memory_space=pltpu.VMEM)
    hbm = pl.BlockSpec(memory_space=pl.ANY)
    half, full = jnp.bfloat16, jnp.float32
    saved = [
        ((HEADS, group_rows, 2 * HD), half),
        ((HEADS, group_rows, 2 * HD), half),
        ((HEADS, group_rows, HD), half),
        ((2, HEADS, group_rows, HD), full),
        ((HEADS, group_rows, HD), full),
        ((group_rows, OUT), half),
    ]
    q_shape, k_shape, v_shape, factors_shape, inverse_shape, mixed_shape = saved
    scratch = [
        ((SLABS, 4, 4, 2, 2, 48, 3 * HD), half),
        ((group_rows, width), half),
        (blocks, half),
        (blocks, half),
        (blocks, half),
        ((8, group_rows + HD), jnp.int32),
        ((8, group_rows + HD), jnp.int32),
        ((rows * CAP, rows), half),
        ((rows, rows * CAP), half),
        q_shape,
        k_shape,
        v_shape,
        ((HEADS, HD, group_rows), half),
        factors_shape,
        inverse_shape,
        mixed_shape,
        ((group_rows, width), half),
        ((rows, width), half),
        ((2, rows, width), half),
        ((rows, width), half),
        ((rows, width), half),
    ]
    sems = 2 + 12 + 12 * SLABS + 3 * MOVES + 6 * CHUNKS
    return pl.pallas_call(
        forward_kernel,
        out_shape=tuple(
            jax.ShapeDtypeStruct(*shape)
            for shape in [((group_rows, width), half), ((group_rows, width), half), ((4, 4, 2, 2, 48, OUT), half)] + saved
        ),
        in_specs=[vmem] + [hbm] * 2 + [vmem] * 4,
        out_specs=(hbm,) * 9,
        scratch_shapes=[pltpu.VMEM(*shape) for shape in scratch] + [
            pltpu.SemaphoreType.DMA((MOVES + 1, 32)),
            pltpu.SemaphoreType.DMA((MOVES + 1, 32)),
            pltpu.SemaphoreType.DMA((sems,)),
            pltpu.SemaphoreType.DMA((sems,)),
            pltpu.SemaphoreType.DMA((20,)),
        ],
        compiler_params=pltpu.CompilerParams(collective_id=2, has_side_effects=True, vmem_limit_bytes=VMEM_LIMIT),
        name="forward_residual_gradient",
    )(
        plan.reshape(-1, plan.shape[2]), shard_qkv.reshape(2, 48, QKV), shard_out.reshape(2, 48, OUT),
        segments, levels, own_rows, own_target)


def added(*values):
    total = values[0].astype(jnp.float32)
    for value in values[1:]:
        total = total + value.astype(jnp.float32)
    return total


def reduce_start(copies, me, axis, block, got):
    up, down = moved(me, axis, 1), moved(me, axis, -1)
    opposite = moved(me, axis, 2)[axis]
    far_up = copies.start(block(opposite, 0), got(0), up)
    far_down = copies.start(block(opposite, 1), got(1), down)
    near_up = copies.start(block(up[axis], 1), got(2), up)
    near_down = copies.start(block(down[axis], 0), got(3), down)
    return far_up, far_down, near_up, near_down


def reduce_pass(copies, me, axis, block, got, sums, sent, add):
    up, down = moved(me, axis, 1), moved(me, axis, -1)
    sent[0].wait_recv()
    add(sums(0), [block(up[axis], 0), got(0)])
    sum_up = copies.start(sums(0), got(4), up)
    sent[1].wait_recv()
    add(sums(1), [block(down[axis], 1), got(1)])
    sum_down = copies.start(sums(1), got(5), down)
    return sent[2], sent[3], sum_up, sum_down


def reduce_end(me, axis, block, got, out, sent, add):
    sent[1].wait_recv()
    sent[2].wait_recv()
    add(out(0), [block(me[axis], 0), got(3), got(4)])
    sent[0].wait_recv()
    sent[3].wait_recv()
    add(out(1), [block(me[axis], 1), got(2), got(5)])


def add_rows(out, parts):
    lead = out.shape[:-2]
    count = math.prod(lead)

    @pl.loop(0, count)
    def _(i):
        index, rest = [], i
        for size in reversed(lead):
            index.insert(0, rest % size)
            rest = rest // size
        index = tuple(index)
        out[index] = added(*[part[index] for part in parts]).astype(out.dtype)


def backward_kernel(*refs):
    inputs, (qkv_sums, out_sums), held = refs[:9], refs[9:11], refs[11:20]
    d_full, x_full, w_out, q_marked, k_marked, v_half, factors, inverse, mixed = held
    (
        d_out, k_turned, dq, dk, dv, d_proj,
        grads, got_far, sum_far, half_far, got_near, sum_near, half_near, got_last, send_sem, recv_sem, local_sem,
    ) = refs[20:]
    loads = [pltpu.make_async_copy(inputs[i], held[i], local_sem.at[i]) for i in range(9)]
    for i in (0, 8, 2, 7, 4, 3, 5, 1, 6):
        loads[i].start()
    me = my_place()
    z, x, y, a, c = me
    greet([moved(me, Z, 1), moved(me, Z, -1), moved(me, X, 1), moved(me, X, -1), moved(me, Y, 1)])
    copies = Copies(send_sem, recv_sem)
    far_axis, near_axis = (X, Z), (Z, X)
    group_rows, width = x_full.shape
    rows = group_rows // 4
    scale = 1.0 / math.sqrt(HD)

    class Slab:
        def __init__(self, s):
            self.s = s

        def far_block(self, half):
            if half == 0:
                return lambda at, which: grads.at[self.s, pl.ds(2 * which, 2), at, :, 0]
            return lambda at, which: grads.at[self.s, at, pl.ds(2 * which, 2), :, 1]

        def near_block(self, half):
            return lambda at, which: half_far.at[self.s, half, at, which]

        def slots(self, ref, half):
            return lambda j: ref.at[self.s, half, j]

        def far_out(self, half):
            return lambda which: half_far.at[self.s, half, pl.ds(2 * which, 2)]

        def near_out(self, half):
            return lambda which: half_near.at[self.s, half, pl.ds(which, 1)]

        def far_start(self):
            self.sent = [
                reduce_start(copies, me, far_axis[h], self.far_block(h), self.slots(got_far, h)) for h in (0, 1)]

        def far_pass(self):
            self.sent = [
                reduce_pass(copies, me, far_axis[h], self.far_block(h), self.slots(got_far, h),
                            self.slots(sum_far, h), self.sent[h], add_rows)
                for h in (0, 1)]

        def near_start(self):
            for h in (0, 1):
                reduce_end(me, far_axis[h], self.far_block(h), self.slots(got_far, h), self.far_out(h), self.sent[h], add_rows)
            self.sent = [
                reduce_start(copies, me, near_axis[h], self.near_block(h), self.slots(got_near, h)) for h in (0, 1)]

        def near_pass(self):
            self.sent = [
                reduce_pass(copies, me, near_axis[h], self.near_block(h), self.slots(got_near, h),
                            self.slots(sum_near, h), self.sent[h], near_add)
                for h in (0, 1)]

        def last_start(self):
            for h in (0, 1):
                reduce_end(me, near_axis[h], self.near_block(h), self.slots(got_near, h), self.near_out(h), self.sent[h], near_add)
            self.sent = [
                copies.start(half_near.at[self.s, h, 1 - y], got_last.at[self.s, h], moved(me, Y, 1)) for h in (0, 1)]

        def end(self):
            for h in (0, 1):
                self.sent[h].wait_recv()
                total = added(half_near[self.s, h, y], got_last[self.s, h])
                if self.s == HEADS:
                    out_sums[h] = total
                else:
                    qkv_sums[h, :, self.s * 3 * HD:(self.s + 1) * 3 * HD] = total

    def near_add(out, parts):
        out[...] = added(*[part[...] for part in parts]).astype(out.dtype).reshape(out.shape)

    def weight_grads(s, left, right):
        @pl.loop(0, 8)
        def _(t):
            columns = pl.ds(pl.multiple_of(t * 384, 384), 384)
            term = tn(left[:, columns], right[...]).astype(jnp.bfloat16)
            grads[s, t // 2, pl.ds(t % 2 * 2, 2)] = term.reshape(2, 2, 2, 48, 384)

    def head(h):
        head_columns = slice(h * HD, (h + 1) * HD)

        @pl.loop(0, 4)
        def _(i):
            at = pl.ds(pl.multiple_of(i * rows, rows), rows)
            k_turned[:, at] = k_marked[h, at, 0:HD].astype(jnp.float32).T.astype(jnp.bfloat16)

        dk[...] = jnp.zeros_like(dk)
        dv[...] = jnp.zeros_like(dv)

        @pl.loop(0, 4)
        def _(i):
            at = pl.ds(pl.multiple_of(i * rows, rows), rows)
            raised = jnp.exp2(nt(k_marked[h], q_marked[h, at, :]) * EXP2_SCALE)
            d_here = d_out[at, head_columns]
            delta = jnp.sum((d_here.astype(jnp.float32) * mixed[at, head_columns].astype(jnp.float32)).T, axis=0, keepdims=True)
            d_scores = (raised * (nt(v_half[h], d_here) - delta)).astype(jnp.bfloat16)
            dv[...] += nn(raised.astype(jnp.bfloat16), d_here)
            dk[...] += nn(d_scores, q_marked[h, at, 0:HD])
            dq[at, :] = nn(k_turned[...], d_scores).T

        @pl.loop(0, 4)
        def _(i):
            at = pl.ds(pl.multiple_of(i * rows, rows), rows)
            for part, grad, marked in ((0, dq, q_marked), (1, dk, k_marked)):
                normed = marked[h, at, 0:HD].astype(jnp.float32)
                got = grad[at, :]
                inner = jnp.mean(got * normed, axis=-1, keepdims=True)
                d_proj[at, part * HD:(part + 1) * HD] = (
                    (factors[part, h, at, :] * scale) * (got - normed * inner)).astype(jnp.bfloat16)
            d_proj[at, 2 * HD:3 * HD] = dv[at, :].astype(jnp.bfloat16)

    out_slab = Slab(HEADS)
    slabs = [Slab(h) for h in range(HEADS)]
    loads[0].wait()
    loads[8].wait()
    weight_grads(HEADS, d_full, mixed)
    out_slab.far_start()
    for i in range(1, 8):
        loads[i].wait()

    @pl.loop(0, 4)
    def _(i):
        at = pl.ds(pl.multiple_of(i * rows, rows), rows)
        got = nn(d_full[at, :], w_out[...])
        for h in range(HEADS):
            d_out[at, h * HD:(h + 1) * HD] = (got[:, h * HD:(h + 1) * HD] * inverse[h, at, :]).astype(jnp.bfloat16)

    head(0)
    out_slab.far_pass()
    weight_grads(0, x_full, d_proj)
    slabs[0].far_start()
    out_slab.near_start()
    head(1)
    slabs[0].far_pass()
    out_slab.near_pass()
    weight_grads(1, x_full, d_proj)
    slabs[1].far_start()
    slabs[0].near_start()
    out_slab.last_start()
    head(2)
    slabs[1].far_pass()
    slabs[0].near_pass()
    out_slab.end()
    weight_grads(2, x_full, d_proj)
    slabs[2].far_start()
    slabs[1].near_start()
    slabs[0].last_start()
    slabs[2].far_pass()
    slabs[1].near_pass()
    slabs[0].end()
    slabs[2].near_start()
    slabs[1].last_start()
    slabs[2].near_pass()
    slabs[1].end()
    slabs[2].last_start()
    slabs[2].end()
    copies.finish()


def backward(d_full, x_full, w_out, q_marked, k_marked, v_half, factors, inverse, mixed):
    group_rows, width = x_full.shape
    inputs = (d_full, x_full, w_out.reshape(width, OUT), q_marked, k_marked, v_half, factors, inverse, mixed)
    half = lambda *lead: pltpu.VMEM((SLABS, 2, *lead, 48, 3 * HD), jnp.bfloat16)
    vmem = pl.BlockSpec(memory_space=pltpu.VMEM)
    qkv_sums, out_sums = pl.pallas_call(
        backward_kernel,
        out_shape=(
            jax.ShapeDtypeStruct((2, 48, QKV), jnp.float32),
            jax.ShapeDtypeStruct((2, 48, OUT), jnp.float32),
        ),
        in_specs=[pl.BlockSpec(memory_space=pl.ANY)] * 9,
        out_specs=(vmem, vmem),
        scratch_shapes=[pltpu.VMEM(value.shape, value.dtype) for value in inputs] + [
            pltpu.VMEM((group_rows, OUT), jnp.bfloat16),
            pltpu.VMEM((HD, group_rows), jnp.bfloat16),
            pltpu.VMEM((group_rows, HD), jnp.float32),
            pltpu.VMEM((group_rows, HD), jnp.float32),
            pltpu.VMEM((group_rows, HD), jnp.float32),
            pltpu.VMEM((group_rows, 3 * HD), jnp.bfloat16),
            pltpu.VMEM((SLABS, 4, 4, 2, 2, 48, 3 * HD), jnp.bfloat16),
            half(6, 2, 2),
            half(2, 2, 2),
            half(4, 2),
            half(6),
            half(2),
            half(2),
            half(),
            pltpu.SemaphoreType.DMA((26 * SLABS,)),
            pltpu.SemaphoreType.DMA((26 * SLABS,)),
            pltpu.SemaphoreType.DMA((9,)),
        ],
        compiler_params=pltpu.CompilerParams(collective_id=3, has_side_effects=True, vmem_limit_bytes=VMEM_LIMIT),
        name="backward_scatter",
    )(*inputs)
    return qkv_sums.reshape(96, QKV), out_sums.reshape(96, OUT)


def per_device(clip_rows, velocity_target, plan, segment_ids, reward_levels, w_qkv, w_out):
    return backward(*forward(plan, w_qkv, w_out, segment_ids, reward_levels, clip_rows, velocity_target))


def solution(mesh):
    return jax.shard_map(
        per_device,
        mesh=mesh,
        in_specs=(
            P(("dp", "seq"), None),
            P(("dp", "seq"), None),
            P(),
            P("dp", None),
            P("dp", None),
            P("dp", "seq"),
            P("dp", "seq"),
        ),
        out_specs=(P("dp", "seq"), P("dp", "seq")),
        check_vma=False,
    )
```

```python
import math

import jax
import jax.numpy as jnp
from jax import lax
from jax.experimental import pallas as pl
from jax.experimental.pallas import tpu as pltpu
from jax.sharding import PartitionSpec as P

HD = 128
CAP = 2
MESH = pl.DeviceIdType.MESH
VMEM_LIMIT = 60 * 1024 * 1024

epsilon = 1e-06


def my_place():
    dp = lax.axis_index("dp")
    seq = lax.axis_index("seq")
    return (dp // 8, (dp // 2) % 4, dp % 2, seq // 2, seq % 2)


def device(place):
    z, x, y, a, c = place
    return {"dp": z * 8 + x * 2 + y, "seq": a * 2 + c}


def moved(place, axis, by):
    place = list(place)
    size = (4, 4, 2, 2, 2)[axis]
    place[axis] = (place[axis] + by + size) % size
    return tuple(place)


Z, X, Y, A, C = range(5)


def chip_partner(place):
    return moved(moved(place, Y, 1), A, 1)


class Copies:
    def __init__(self, send_sem, recv_sem):
        self.send_sem, self.recv_sem, self.used = send_sem, recv_sem, 0
        self.started = []

    def start(self, src, dst, to):
        copy = pltpu.make_async_remote_copy(
            src_ref=src,
            dst_ref=dst,
            send_sem=self.send_sem.at[self.used],
            recv_sem=self.recv_sem.at[self.used],
            device_id=device(to),
            device_id_type=MESH,
        )
        self.used += 1
        copy.start()
        self.started.append(copy)
        return copy

    def finish(self):
        for copy in self.started:
            copy.wait_send()


def greet(places):
    barrier = pltpu.get_barrier_semaphore()
    for place in places:
        pl.semaphore_signal(barrier, inc=1, device_id=device(place), device_id_type=MESH)
    pl.semaphore_wait(barrier, len(places))


def dp_peer(place, k, sign):
    z, x, y, a, c = place
    k = (k * 13) % 32
    sign = sign * (1 - 2 * c)
    dz, dx, dy = k // 8, (k // 2) % 4, k % 2
    return ((z + sign * dz + 4) % 4, (x + sign * dx + 4) % 4, (y + sign * dy + 2) % 2, a, c)


def ring_gather_start(copies, me, axis, part):
    own = me[axis]
    up, down = moved(me, axis, 1), moved(me, axis, -1)
    first_up = copies.start(part(own, 0), part(own, 0), up)
    first_down = copies.start(part(own, 1), part(own, 1), down)
    second_up = copies.start(part(own, 1), part(own, 1), up)
    second_down = copies.start(part(own, 0), part(own, 0), down)
    return first_up, first_down, second_up, second_down


def ring_gather_forward(copies, me, axis, part, sent):
    up, down = moved(me, axis, 1), moved(me, axis, -1)
    below, above = down[axis], up[axis]
    sent[0].wait_recv()
    third_up = copies.start(part(below, 0), part(below, 0), up)
    sent[1].wait_recv()
    third_down = copies.start(part(above, 1), part(above, 1), down)
    return sent[2], sent[3], third_up, third_down


CHUNKS = 4
HEADS = 3
QKV = HEADS * 3 * HD
OUT = HEADS * HD
SLABS = HEADS + 1
EXP2_SCALE = math.log2(math.e) / math.sqrt(HD)


def nt(left, right):
    return lax.dot_general(left, right, (((1,), (1,)), ((), ())), preferred_element_type=jnp.float32)


def tn(left, right):
    return lax.dot_general(left, right, (((0,), (0,)), ((), ())), preferred_element_type=jnp.float32)


def nn(left, right):
    return jnp.dot(left, right, preferred_element_type=jnp.float32)


MOVES = 3


def forward_kernel(
    plan, shard_qkv, shard_out, segments, levels, own_rows, own_target,
    d_full, x_out, w_out, q_out, k_out, v_out, factors_out, inverse_out, mixed_out,
    w_full, x_full, packed, received, received_target, labels, labels_there, pack, chosen,
    q_marked, k_marked, v_half, v_turned, factors, inverse, mixed,
    partial, target, from_core, from_chip, d_own,
    a2a_send, a2a_recv, send_sem, recv_sem, local_sem,
):
    me = my_place()
    z, x, y, a, c = me
    dp = lax.axis_index("dp")
    rows, width = own_target.shape
    group_rows = x_full.shape[0]
    other_chip, other_core = chip_partner(me), moved(me, C, 1)
    barrier = pltpu.get_barrier_semaphore()

    @pl.loop(1, 32)
    def _(k):
        pl.semaphore_signal(barrier, inc=1, device_id=device(dp_peer(me, k, 1)), device_id_type=MESH)

    for place in (other_chip, other_core):
        pl.semaphore_signal(barrier, inc=1, device_id=device(place), device_id_type=MESH)

    locals_started = []

    def local_copy(src, dst):
        copy = pltpu.make_async_copy(src, dst, local_sem.at[len(locals_started)])
        copy.start()
        locals_started.append(copy)
        return copy

    shards = [
        local_copy(shard_qkv.at[:, :, h * 3 * HD:(h + 1) * 3 * HD], w_full.at[h, z, x, y]) for h in range(HEADS)
    ] + [local_copy(shard_out, w_full.at[HEADS, z, x, y])]
    tile = width // MOVES

    def iota(shape, axis):
        return lax.broadcasted_iota(jnp.int32, shape, axis)

    def one_where(condition):
        return jnp.where(condition, 1.0, 0.0).astype(jnp.bfloat16)

    shards_of, groups = 4, 32
    group = dp + a * (1 - 2 * y)
    plan_half = plan[...].astype(jnp.float32).astype(jnp.bfloat16)
    before = one_where(iota((groups, groups), 0) < iota((groups, groups), 1))
    counts = nn(one_where(iota((8, groups * shards_of), 1) == dp * shards_of + a * 2 + c), plan_half).astype(jnp.bfloat16)
    starts = nn(counts, before).astype(jnp.bfloat16)
    to_group = iota((rows * CAP, groups), 1)
    to_group = to_group + a * (1 - 2 * (to_group & 1))
    here = one_where((iota((rows * CAP, groups), 0) >> 4) == to_group)
    of_row = iota((rows * CAP, 1), 0)
    which = ((of_row >> 3) & 1).astype(jnp.float32)
    source = (nt(here, starts)[:, 0:1] + which) * 8.0 + (of_row & 7).astype(jnp.float32)
    source = jnp.where(which < nt(here, counts)[:, 0:1], source, -1.0)
    pack[...] = one_where(iota((rows * CAP, rows), 1).astype(jnp.float32) == source)
    labels[:, 0:group_rows] = jnp.broadcast_to(segments[...], (8, group_rows))
    lane = iota((8, HD), 1)
    labels[:, group_rows:group_rows + HD] = jnp.where(lane == 0, levels[0:1, 0:1], jnp.where(lane == 1, levels[0:1, 1:2], 0))

    def fill(src, chunk):
        for low in range(chunk * tile, (chunk + 1) * tile, 512):
            blocks = nn(pack[...], src[:, low:low + 512]).astype(jnp.bfloat16)
            packed[:, :, low:low + 512] = blocks.reshape(packed.shape[0], packed.shape[1], 512)

    def block_copy(chunk, k):
        to = dp_peer(me, k, 1)
        dst = received_target if chunk == MOVES else received
        columns = slice(None) if chunk == MOVES else slice(chunk * tile, (chunk + 1) * tile)
        return pltpu.make_async_remote_copy(
            src_ref=packed.at[device(to)["dp"], :, columns],
            dst_ref=dst.at[dp, :, columns],
            send_sem=a2a_send.at[chunk, k],
            recv_sem=a2a_recv.at[chunk, k],
            device_id=device(to),
            device_id_type=MESH,
        )

    def own_block_copy(chunk):
        dst = received_target if chunk == MOVES else received
        columns = slice(None) if chunk == MOVES else slice(chunk * tile, (chunk + 1) * tile)
        return local_copy(packed.at[dp, :, columns], dst.at[dp, :, columns])

    fill(own_rows, 0)
    for copy in shards:
        copy.wait()
    pl.semaphore_wait(barrier, 33)

    copies = Copies(send_sem, recv_sem)
    across = copies.start(w_full.at[0:HEADS, z, x, y], w_full.at[0:HEADS, z, x, y], moved(me, Y, 1))
    labels_across = copies.start(labels, labels_there, moved(me, Y, 1))

    def near_out(half):
        columns = lambda which: pl.ds(0, 2 * HD) if which == half else pl.ds(2 * HD, HD)
        if half == 0:
            return lambda at, which: w_full.at[HEADS, at, x, y, 0, :, columns(which)]
        return lambda at, which: w_full.at[HEADS, z, at, y, 1, :, columns(which)]

    near_axis, far_axis = (Z, X), (X, Z)
    out_sent = [ring_gather_start(copies, me, near_axis[half], near_out(half)) for half in (0, 1)]
    own_blocks = []
    for chunk in range(MOVES):
        if chunk:
            fill(own_rows, chunk)

        @pl.loop(1, 32)
        def _(k):
            block_copy(chunk, k).start()

        own_blocks.append(own_block_copy(chunk))

    arriving = nn(
        one_where(iota((groups, groups * shards_of), 1) == iota((groups, groups * shards_of), 0) * shards_of + a * 2 + c), plan_half)
    arriving = jnp.where(iota((groups, groups), 1) == group, arriving, 0.0).astype(jnp.bfloat16)
    counts = nt(jnp.ones((8, groups), jnp.bfloat16), arriving).astype(jnp.bfloat16)
    starts = nn(counts, before).astype(jnp.bfloat16)
    there = one_where((iota((groups, rows * CAP), 1) >> 4) == iota((groups, rows * CAP), 0))
    of_column = iota((1, rows * CAP), 1)
    which = ((of_column >> 3) & 1).astype(jnp.float32)
    slot = nn(starts, there)[0:1, :] + which
    slot = jnp.where(which < nn(counts, there)[0:1, :], slot, -1.0)
    place = slot * 8.0 + (of_column & 7).astype(jnp.float32)
    chosen[...] = one_where(iota((rows, rows * CAP), 0).astype(jnp.float32) == place)

    def select(src, dst, at, chunk):
        for low in range(chunk * tile, (chunk + 1) * tile, 512):
            blocks = src[:, :, low:low + 512].reshape(rows * CAP, 512)
            dst[at, low:low + 512] = nn(chosen[...], blocks).astype(jnp.bfloat16)

    def near(half):
        if half == 0:
            return lambda at, which: w_full.at[0:HEADS, at, x, which, 0]
        return lambda at, which: w_full.at[0:HEADS, z, at, which, 1]

    def far(s, half):
        ys = pl.ds(y, 1) if s == HEADS else slice(None)
        if half == 0:
            return lambda at, which: w_full.at[s, pl.ds(2 * which, 2), at, ys, 0]
        return lambda at, which: w_full.at[s, at, pl.ds(2 * which, 2), ys, 1]

    across.wait_recv()
    sent = [ring_gather_start(copies, me, near_axis[half], near(half)) for half in (0, 1)]
    rest = [ring_gather_forward(copies, me, near_axis[half], near(half), sent[half]) for half in (0, 1)]
    for half in (0, 1):
        for copy in rest[half]:
            copy.wait_recv()

    far_sent = {}

    def far_start(s):
        far_sent[s] = [ring_gather_start(copies, me, far_axis[half], far(s, half)) for half in (0, 1)]

    def far_forward(s):
        far_sent[s] = [ring_gather_forward(copies, me, far_axis[half], far(s, half), far_sent[s][half]) for half in (0, 1)]

    def far_wait(s):
        for half in (0, 1):
            for copy in far_sent[s][half]:
                copy.wait_recv()

    out_rest = [ring_gather_forward(copies, me, near_axis[half], near_out(half), out_sent[half]) for half in (0, 1)]
    for half in (0, 1):
        for copy in out_rest[half]:
            copy.wait_recv()
    far_start(HEADS)
    far_start(0)

    def rows_of(place, chunk=0, chunks=1):
        step = rows // chunks
        return pl.ds(pl.multiple_of(device(place)["seq"] * rows + chunk * step, step), step)

    x_chip, x_core, x_passed = [], [], []

    def x_arrive(chunk):
        own_blocks[chunk].wait()

        @pl.loop(1, 32)
        def _(k):
            block_copy(chunk, k).wait_recv()

        at = rows_of(me)
        select(received, x_full, at, chunk)
        part = x_full.at[at, chunk * tile:(chunk + 1) * tile]
        x_chip.append(copies.start(part, part, other_chip))
        x_core.append(copies.start(part, part, other_core))

    def x_pass(chunk):
        x_chip[chunk].wait_recv()
        part = x_full.at[rows_of(other_chip), chunk * tile:(chunk + 1) * tile]
        x_passed.append(copies.start(part, part, other_core))

    x_arrive(0)
    far_start(1)

    labels_across.wait_recv()
    lane = iota((rows, HD), 1)
    for i in range(group_rows // rows):
        at = slice(i * rows, (i + 1) * rows)
        segment = jnp.where(a == 1, labels_there[0:1, at], labels[0:1, at]).astype(jnp.float32)
        sign = jnp.broadcast_to(2.0 * segment - 1.0, (HD, rows)).T
        mark_q = jnp.where(lane == 0, 64.0 * sign, jnp.where(lane == 1, -64.0, 0.0)).astype(jnp.bfloat16)
        mark_k = jnp.where(lane == 0, 32.0 * sign, jnp.where(lane == 1, 32.0, 0.0)).astype(jnp.bfloat16)
        for h in range(HEADS):
            q_marked[h, at, HD:2 * HD] = mark_q
            k_marked[h, at, HD:2 * HD] = mark_k

    def project(h, chip):
        @pl.loop(0, 2)
        def _(i):
            at = pl.ds(pl.multiple_of((chip * 2 + i) * rows, rows), rows)
            raw = nn(x_full[at, :], w_full[h].reshape(width, 3 * HD))
            for part, marked in ((0, q_marked), (1, k_marked)):
                values = raw[:, part * HD:(part + 1) * HD]
                factor = lax.rsqrt(jnp.mean(values * values, axis=-1, keepdims=True) + epsilon)
                marked[h, at, 0:HD] = (values * factor).astype(jnp.bfloat16)
                factors[part, h, at, :] = jnp.broadcast_to(factor, (rows, HD))
            values = raw[:, 2 * HD:3 * HD]
            v_half[h, at, :] = values.astype(jnp.bfloat16)
            v_turned[h, :, at] = values.T.astype(jnp.bfloat16)

    def attend(h, at):
        scores = nt(k_marked[h], q_marked[h, at, :])
        raised = jnp.exp2(scores * EXP2_SCALE)
        inverse_sum = 1.0 / jnp.sum(raised, axis=0, keepdims=True)
        turned = nn(v_turned[h], raised.astype(jnp.bfloat16)) * inverse_sum
        mixed[at, h * HD:(h + 1) * HD] = turned.T.astype(jnp.bfloat16)
        inverse[h, at, :] = jnp.broadcast_to(inverse_sum, (HD, rows)).T

    def attend_all(h):
        @pl.loop(0, group_rows // rows)
        def _(i):
            attend(h, pl.ds(pl.multiple_of(i * rows, rows), rows))

    x_arrive(1)
    x_pass(0)
    far_forward(HEADS)
    far_forward(0)
    far_wait(HEADS)
    traded = [
        copies.start(w_full.at[HEADS, :, :, y, half], w_full.at[HEADS, :, :, y, half], moved(me, Y, 1)) for half in (0, 1)]
    x_arrive(2)
    far_wait(0)
    far_start(2)
    far_forward(1)
    x_pass(1)
    for copy in x_core:
        copy.wait_recv()
    project(0, a)
    far_wait(1)
    project(1, a)
    far_forward(2)
    x_pass(2)
    for copy in x_passed:
        copy.wait_recv()
    outs = [local_copy(x_full, x_out)]
    project(0, 1 - a)
    attend_all(0)
    for chunk in range(MOVES):
        @pl.loop(1, 32)
        def _(k):
            block_copy(chunk, k).wait_send()

    for chunk in range(MOVES):
        fill(own_target, chunk)

    @pl.loop(1, 32)
    def _(k):
        block_copy(MOVES, k).start()

    own_block = own_block_copy(MOVES)
    project(1, 1 - a)
    attend_all(1)
    far_wait(2)
    project(2, a)
    project(2, 1 - a)
    for src, dst in ((q_marked, q_out), (k_marked, k_out), (v_half, v_out), (factors, factors_out)):
        outs.append(local_copy(src, dst))
    for copy in traded:
        copy.wait_recv()
    outs.append(local_copy(w_full.at[HEADS], w_out))

    def block(place):
        at = rows_of(place)
        attend(HEADS - 1, at)

        @pl.loop(0, 8)
        def _(t):
            weights = w_full[HEADS, t // 2, pl.ds(t % 2 * 2, 2)].reshape(3 * HD, OUT)
            columns = pl.ds(pl.multiple_of(t * 3 * HD, 3 * HD), 3 * HD)
            partial[at, columns] = nt(mixed[at, :], weights).astype(jnp.bfloat16)

    core_first, core_second, chip_sums = [], [], []
    step = rows // CHUNKS
    far_core = moved(other_chip, C, 1)
    block(far_core)
    for chunk in range(CHUNKS):
        core_first.append(copies.start(
            partial.at[rows_of(far_core, chunk, CHUNKS)], from_core.at[0, pl.ds(chunk * step, step)], other_core))
    block(other_chip)
    for chunk in range(CHUNKS):
        core_first[chunk].wait_recv()
        at = pl.ds(chunk * step, step)
        from_core[0, at] = (
            partial[rows_of(other_chip, chunk, CHUNKS)].astype(jnp.float32) + from_core[0, at].astype(jnp.float32)
        ).astype(jnp.bfloat16)
        chip_sums.append(copies.start(from_core.at[0, at], from_chip.at[at], other_chip))
    block(other_core)
    for chunk in range(CHUNKS):
        core_second.append(copies.start(
            partial.at[rows_of(other_core, chunk, CHUNKS)], from_core.at[1, pl.ds(chunk * step, step)], other_core))
    block(me)
    for src, dst in ((inverse, inverse_out), (mixed, mixed_out)):
        outs.append(local_copy(src, dst))

    own_block.wait()

    @pl.loop(1, 32)
    def _(k):
        block_copy(MOVES, k).wait_recv()

    for chunk in range(MOVES):
        select(received_target, target, slice(None), chunk)
    own_lanes = rows_of(me)
    segment = jnp.where(a == 1, labels_there[0:1, own_lanes], labels[0:1, own_lanes]).astype(jnp.float32)
    first, second = (
        jnp.where(a == 1, labels_there[0:1, at:at + 1], labels[0:1, at:at + 1]).astype(jnp.float32)
        for at in (group_rows, group_rows + 1))
    loss_scale = 1.0 / math.sqrt(group_rows * 32)
    weight = (jnp.where(segment == 0.0, first, second) / 8.0) * loss_scale
    weight = jnp.broadcast_to(weight, (HD, rows)).T[:, 0:1]

    to_chip, to_core, passed = [], [], []
    for chunk in range(CHUNKS):
        core_second[chunk].wait_recv()
        chip_sums[chunk].wait_recv()
        at = slice(chunk * step, (chunk + 1) * step)
        mine = rows_of(me, chunk, CHUNKS)
        prediction = (
            x_full[mine].astype(jnp.float32)
            + (partial[mine].astype(jnp.float32) + from_core[1, at].astype(jnp.float32) + from_chip[at].astype(jnp.float32))
        )
        d_own[at] = (weight[at] * (prediction - target[at].astype(jnp.float32))).astype(jnp.bfloat16)
        to_chip.append(copies.start(d_own.at[at], d_full.at[mine], other_chip))
        to_core.append(copies.start(d_own.at[at], d_full.at[mine], other_core))
    outs.append(local_copy(d_own, d_full.at[rows_of(me)]))
    for chunk in range(CHUNKS):
        to_chip[chunk].wait_recv()
        theirs = rows_of(other_chip, chunk, CHUNKS)
        passed.append(copies.start(d_full.at[theirs], d_full.at[theirs], other_core))
    for chunk in range(CHUNKS):
        to_core[chunk].wait_recv()
        passed[chunk].wait_recv()

    @pl.loop(1, 32)
    def _(k):
        block_copy(MOVES, k).wait_send()

    for copy in outs:
        copy.wait()
    copies.finish()


def forward(plan, shard_qkv, shard_out, segments, levels, own_rows, own_target):
    rows, width = own_target.shape
    group_rows = rows * 4
    blocks = (32, CAP * 8, width)
    vmem = pl.BlockSpec(memory_space=pltpu.VMEM)
    hbm = pl.BlockSpec(memory_space=pl.ANY)
    half, full = jnp.bfloat16, jnp.float32
    saved = [
        ((HEADS, group_rows, 2 * HD), half),
        ((HEADS, group_rows, 2 * HD), half),
        ((HEADS, group_rows, HD), half),
        ((2, HEADS, group_rows, HD), full),
        ((HEADS, group_rows, HD), full),
        ((group_rows, OUT), half),
    ]
    q_shape, k_shape, v_shape, factors_shape, inverse_shape, mixed_shape = saved
    scratch = [
        ((SLABS, 4, 4, 2, 2, 48, 3 * HD), half),
        ((group_rows, width), half),
        (blocks, half),
        (blocks, half),
        (blocks, half),
        ((8, group_rows + HD), jnp.int32),
        ((8, group_rows + HD), jnp.int32),
        ((rows * CAP, rows), half),
        ((rows, rows * CAP), half),
        q_shape,
        k_shape,
        v_shape,
        ((HEADS, HD, group_rows), half),
        factors_shape,
        inverse_shape,
        mixed_shape,
        ((group_rows, width), half),
        ((rows, width), half),
        ((2, rows, width), half),
        ((rows, width), half),
        ((rows, width), half),
    ]
    sems = 2 + 24 + 12 * SLABS + 2 + 3 * MOVES + 6 * CHUNKS
    return pl.pallas_call(
        forward_kernel,
        out_shape=tuple(
            jax.ShapeDtypeStruct(*shape)
            for shape in [((group_rows, width), half), ((group_rows, width), half), ((4, 4, 2, 2, 48, OUT), half)] + saved
        ),
        in_specs=[vmem] + [hbm] * 2 + [vmem] * 4,
        out_specs=(hbm,) * 9,
        scratch_shapes=[pltpu.VMEM(*shape) for shape in scratch] + [
            pltpu.SemaphoreType.DMA((MOVES + 1, 32)),
            pltpu.SemaphoreType.DMA((MOVES + 1, 32)),
            pltpu.SemaphoreType.DMA((sems,)),
            pltpu.SemaphoreType.DMA((sems,)),
            pltpu.SemaphoreType.DMA((20,)),
        ],
        compiler_params=pltpu.CompilerParams(collective_id=2, has_side_effects=True, vmem_limit_bytes=VMEM_LIMIT),
        name="forward_residual_gradient",
    )(
        plan.reshape(-1, plan.shape[2]), shard_qkv.reshape(2, 48, QKV), shard_out.reshape(2, 48, OUT),
        segments, levels, own_rows, own_target)


def added(*values):
    total = values[0].astype(jnp.float32)
    for value in values[1:]:
        total = total + value.astype(jnp.float32)
    return total


def reduce_start(copies, me, axis, block, got):
    up, down = moved(me, axis, 1), moved(me, axis, -1)
    opposite = moved(me, axis, 2)[axis]
    far_up = copies.start(block(opposite, 0), got(0), up)
    far_down = copies.start(block(opposite, 1), got(1), down)
    near_up = copies.start(block(up[axis], 1), got(2), up)
    near_down = copies.start(block(down[axis], 0), got(3), down)
    return far_up, far_down, near_up, near_down


def reduce_pass(copies, me, axis, block, got, sums, sent, add):
    up, down = moved(me, axis, 1), moved(me, axis, -1)
    sent[0].wait_recv()
    add(sums(0), [block(up[axis], 0), got(0)])
    sum_up = copies.start(sums(0), got(4), up)
    sent[1].wait_recv()
    add(sums(1), [block(down[axis], 1), got(1)])
    sum_down = copies.start(sums(1), got(5), down)
    return sent[2], sent[3], sum_up, sum_down


def reduce_end(me, axis, block, got, out, sent, add):
    sent[1].wait_recv()
    sent[2].wait_recv()
    add(out(0), [block(me[axis], 0), got(3), got(4)])
    sent[0].wait_recv()
    sent[3].wait_recv()
    add(out(1), [block(me[axis], 1), got(2), got(5)])


def add_rows(out, parts):
    lead = out.shape[:-2]
    count = math.prod(lead)

    @pl.loop(0, count)
    def _(i):
        index, rest = [], i
        for size in reversed(lead):
            index.insert(0, rest % size)
            rest = rest // size
        index = tuple(index)
        out[index] = added(*[part[index] for part in parts]).astype(out.dtype)


def backward_kernel(*refs):
    inputs, (qkv_sums, out_sums), held = refs[:9], refs[9:11], refs[11:20]
    d_full, x_full, w_out, q_marked, k_marked, v_half, factors, inverse, mixed = held
    (
        d_out, k_turned, dq, dk, dv, d_proj,
        grads, got_far, sum_far, half_far, got_near, sum_near, half_near, got_last, send_sem, recv_sem, local_sem,
    ) = refs[20:]
    loads = [pltpu.make_async_copy(inputs[i], held[i], local_sem.at[i]) for i in range(9)]
    for i in (0, 8, 2, 7, 4, 3, 5, 1, 6):
        loads[i].start()
    me = my_place()
    z, x, y, a, c = me
    greet([moved(me, Z, 1), moved(me, Z, -1), moved(me, X, 1), moved(me, X, -1), moved(me, Y, 1)])
    copies = Copies(send_sem, recv_sem)
    far_axis, near_axis = (X, Z), (Z, X)
    group_rows, width = x_full.shape
    rows = group_rows // 4
    scale = 1.0 / math.sqrt(HD)

    class Slab:
        def __init__(self, s):
            self.s = s

        def far_block(self, half):
            if half == 0:
                return lambda at, which: grads.at[self.s, pl.ds(2 * which, 2), at, :, 0]
            return lambda at, which: grads.at[self.s, at, pl.ds(2 * which, 2), :, 1]

        def near_block(self, half):
            return lambda at, which: half_far.at[self.s, half, at, which]

        def slots(self, ref, half):
            return lambda j: ref.at[self.s, half, j]

        def far_out(self, half):
            return lambda which: half_far.at[self.s, half, pl.ds(2 * which, 2)]

        def near_out(self, half):
            return lambda which: half_near.at[self.s, half, pl.ds(which, 1)]

        def far_start(self):
            self.sent = [
                reduce_start(copies, me, far_axis[h], self.far_block(h), self.slots(got_far, h)) for h in (0, 1)]

        def far_pass(self):
            self.sent = [
                reduce_pass(copies, me, far_axis[h], self.far_block(h), self.slots(got_far, h),
                            self.slots(sum_far, h), self.sent[h], add_rows)
                for h in (0, 1)]

        def near_start(self):
            for h in (0, 1):
                reduce_end(me, far_axis[h], self.far_block(h), self.slots(got_far, h), self.far_out(h), self.sent[h], add_rows)
            self.sent = [
                reduce_start(copies, me, near_axis[h], self.near_block(h), self.slots(got_near, h)) for h in (0, 1)]

        def near_pass(self):
            self.sent = [
                reduce_pass(copies, me, near_axis[h], self.near_block(h), self.slots(got_near, h),
                            self.slots(sum_near, h), self.sent[h], near_add)
                for h in (0, 1)]

        def last_start(self):
            for h in (0, 1):
                reduce_end(me, near_axis[h], self.near_block(h), self.slots(got_near, h), self.near_out(h), self.sent[h], near_add)
            self.sent = [
                copies.start(half_near.at[self.s, h, 1 - y], got_last.at[self.s, h], moved(me, Y, 1)) for h in (0, 1)]

        def end(self):
            for h in (0, 1):
                self.sent[h].wait_recv()
                total = added(half_near[self.s, h, y], got_last[self.s, h])
                if self.s == HEADS:
                    out_sums[h] = total
                else:
                    qkv_sums[h, :, self.s * 3 * HD:(self.s + 1) * 3 * HD] = total

    def near_add(out, parts):
        out[...] = added(*[part[...] for part in parts]).astype(out.dtype).reshape(out.shape)

    def weight_grads(s, left, right):
        @pl.loop(0, 8)
        def _(t):
            columns = pl.ds(pl.multiple_of(t * 384, 384), 384)
            term = tn(left[:, columns], right[...]).astype(jnp.bfloat16)
            grads[s, t // 2, pl.ds(t % 2 * 2, 2)] = term.reshape(2, 2, 2, 48, 384)

    def head(h):
        head_columns = slice(h * HD, (h + 1) * HD)

        @pl.loop(0, 4)
        def _(i):
            at = pl.ds(pl.multiple_of(i * rows, rows), rows)
            k_turned[:, at] = k_marked[h, at, 0:HD].astype(jnp.float32).T.astype(jnp.bfloat16)

        dk[...] = jnp.zeros_like(dk)
        dv[...] = jnp.zeros_like(dv)

        @pl.loop(0, 4)
        def _(i):
            at = pl.ds(pl.multiple_of(i * rows, rows), rows)
            raised = jnp.exp2(nt(k_marked[h], q_marked[h, at, :]) * EXP2_SCALE)
            d_here = d_out[at, head_columns]
            delta = jnp.sum((d_here.astype(jnp.float32) * mixed[at, head_columns].astype(jnp.float32)).T, axis=0, keepdims=True)
            d_scores = (raised * (nt(v_half[h], d_here) - delta)).astype(jnp.bfloat16)
            dv[...] += nn(raised.astype(jnp.bfloat16), d_here)
            dk[...] += nn(d_scores, q_marked[h, at, 0:HD])
            dq[at, :] = nn(k_turned[...], d_scores).T

        @pl.loop(0, 4)
        def _(i):
            at = pl.ds(pl.multiple_of(i * rows, rows), rows)
            for part, grad, marked in ((0, dq, q_marked), (1, dk, k_marked)):
                normed = marked[h, at, 0:HD].astype(jnp.float32)
                got = grad[at, :]
                inner = jnp.mean(got * normed, axis=-1, keepdims=True)
                d_proj[at, part * HD:(part + 1) * HD] = (
                    (factors[part, h, at, :] * scale) * (got - normed * inner)).astype(jnp.bfloat16)
            d_proj[at, 2 * HD:3 * HD] = dv[at, :].astype(jnp.bfloat16)

    out_slab = Slab(HEADS)
    slabs = [Slab(h) for h in range(HEADS)]
    loads[0].wait()
    loads[8].wait()
    weight_grads(HEADS, d_full, mixed)
    out_slab.far_start()
    for i in range(1, 8):
        loads[i].wait()

    @pl.loop(0, 4)
    def _(i):
        at = pl.ds(pl.multiple_of(i * rows, rows), rows)
        got = nn(d_full[at, :], w_out[...])
        for h in range(HEADS):
            d_out[at, h * HD:(h + 1) * HD] = (got[:, h * HD:(h + 1) * HD] * inverse[h, at, :]).astype(jnp.bfloat16)

    head(0)
    out_slab.far_pass()
    weight_grads(0, x_full, d_proj)
    slabs[0].far_start()
    out_slab.near_start()
    head(1)
    slabs[0].far_pass()
    out_slab.near_pass()
    weight_grads(1, x_full, d_proj)
    slabs[1].far_start()
    slabs[0].near_start()
    out_slab.last_start()
    head(2)
    slabs[1].far_pass()
    slabs[0].near_pass()
    out_slab.end()
    weight_grads(2, x_full, d_proj)
    slabs[2].far_start()
    slabs[1].near_start()
    slabs[0].last_start()
    slabs[2].far_pass()
    slabs[1].near_pass()
    slabs[0].end()
    slabs[2].near_start()
    slabs[1].last_start()
    slabs[2].near_pass()
    slabs[1].end()
    slabs[2].last_start()
    slabs[2].end()
    copies.finish()


def backward(d_full, x_full, w_out, q_marked, k_marked, v_half, factors, inverse, mixed):
    group_rows, width = x_full.shape
    inputs = (d_full, x_full, w_out.reshape(width, OUT), q_marked, k_marked, v_half, factors, inverse, mixed)
    half = lambda *lead: pltpu.VMEM((SLABS, 2, *lead, 48, 3 * HD), jnp.bfloat16)
    vmem = pl.BlockSpec(memory_space=pltpu.VMEM)
    qkv_sums, out_sums = pl.pallas_call(
        backward_kernel,
        out_shape=(
            jax.ShapeDtypeStruct((2, 48, QKV), jnp.float32),
            jax.ShapeDtypeStruct((2, 48, OUT), jnp.float32),
        ),
        in_specs=[pl.BlockSpec(memory_space=pl.ANY)] * 9,
        out_specs=(vmem, vmem),
        scratch_shapes=[pltpu.VMEM(value.shape, value.dtype) for value in inputs] + [
            pltpu.VMEM((group_rows, OUT), jnp.bfloat16),
            pltpu.VMEM((HD, group_rows), jnp.bfloat16),
            pltpu.VMEM((group_rows, HD), jnp.float32),
            pltpu.VMEM((group_rows, HD), jnp.float32),
            pltpu.VMEM((group_rows, HD), jnp.float32),
            pltpu.VMEM((group_rows, 3 * HD), jnp.bfloat16),
            pltpu.VMEM((SLABS, 4, 4, 2, 2, 48, 3 * HD), jnp.bfloat16),
            half(6, 2, 2),
            half(2, 2, 2),
            half(4, 2),
            half(6),
            half(2),
            half(2),
            half(),
            pltpu.SemaphoreType.DMA((26 * SLABS,)),
            pltpu.SemaphoreType.DMA((26 * SLABS,)),
            pltpu.SemaphoreType.DMA((9,)),
        ],
        compiler_params=pltpu.CompilerParams(collective_id=3, has_side_effects=True, vmem_limit_bytes=VMEM_LIMIT),
        name="backward_scatter",
    )(*inputs)
    return qkv_sums.reshape(96, QKV), out_sums.reshape(96, OUT)


def per_device(clip_rows, velocity_target, plan, segment_ids, reward_levels, w_qkv, w_out):
    return backward(*forward(plan, w_qkv, w_out, segment_ids, reward_levels, clip_rows, velocity_target))


def solution(mesh):
    return jax.shard_map(
        per_device,
        mesh=mesh,
        in_specs=(
            P(("dp", "seq"), None),
            P(("dp", "seq"), None),
            P(),
            P("dp", None),
            P("dp", None),
            P("dp", "seq"),
            P("dp", "seq"),
        ),
        out_specs=(P("dp", "seq"), P("dp", "seq")),
        check_vma=False,
    )
```

```python
import math

import jax
import jax.numpy as jnp
from jax import lax
from jax.experimental import pallas as pl
from jax.experimental.pallas import tpu as pltpu
from jax.sharding import PartitionSpec as P

HD = 128
CAP = 2
MESH = pl.DeviceIdType.MESH
VMEM_LIMIT = 60 * 1024 * 1024

epsilon = 1e-06


def my_place():
    dp = lax.axis_index("dp")
    seq = lax.axis_index("seq")
    return (dp // 8, (dp // 2) % 4, dp % 2, seq // 2, seq % 2)


def device(place):
    z, x, y, a, c = place
    return {"dp": z * 8 + x * 2 + y, "seq": a * 2 + c}


def moved(place, axis, by):
    place = list(place)
    size = (4, 4, 2, 2, 2)[axis]
    place[axis] = (place[axis] + by + size) % size
    return tuple(place)


Z, X, Y, A, C = range(5)


def chip_partner(place):
    return moved(moved(place, Y, 1), A, 1)


class Copies:
    def __init__(self, send_sem, recv_sem):
        self.send_sem, self.recv_sem, self.used = send_sem, recv_sem, 0
        self.started = []

    def start(self, src, dst, to):
        copy = pltpu.make_async_remote_copy(
            src_ref=src,
            dst_ref=dst,
            send_sem=self.send_sem.at[self.used],
            recv_sem=self.recv_sem.at[self.used],
            device_id=device(to),
            device_id_type=MESH,
        )
        self.used += 1
        copy.start()
        self.started.append(copy)
        return copy

    def finish(self):
        for copy in self.started:
            copy.wait_send()


def greet(places):
    barrier = pltpu.get_barrier_semaphore()
    for place in places:
        pl.semaphore_signal(barrier, inc=1, device_id=device(place), device_id_type=MESH)
    return lambda: pl.semaphore_wait(barrier, len(places))


def dp_peer(place, k, sign):
    z, x, y, a, c = place
    k = (k * 13) % 32
    sign = sign * (1 - 2 * c)
    dz, dx, dy = k // 8, (k // 2) % 4, k % 2
    return ((z + sign * dz + 4) % 4, (x + sign * dx + 4) % 4, (y + sign * dy + 2) % 2, a, c)


def ring_gather_start(copies, me, axis, part):
    own = me[axis]
    up, down = moved(me, axis, 1), moved(me, axis, -1)
    first_up = copies.start(part(own, 0), part(own, 0), up)
    first_down = copies.start(part(own, 1), part(own, 1), down)
    second_up = copies.start(part(own, 1), part(own, 1), up)
    second_down = copies.start(part(own, 0), part(own, 0), down)
    return first_up, first_down, second_up, second_down


def ring_gather_forward(copies, me, axis, part, sent):
    up, down = moved(me, axis, 1), moved(me, axis, -1)
    below, above = down[axis], up[axis]
    sent[0].wait_recv()
    third_up = copies.start(part(below, 0), part(below, 0), up)
    sent[1].wait_recv()
    third_down = copies.start(part(above, 1), part(above, 1), down)
    return sent[2], sent[3], third_up, third_down


CHUNKS = 4
HEADS = 3
QKV = HEADS * 3 * HD
OUT = HEADS * HD
SLABS = HEADS + 1
EXP2_SCALE = math.log2(math.e) / math.sqrt(HD)


def nt(left, right):
    return lax.dot_general(left, right, (((1,), (1,)), ((), ())), preferred_element_type=jnp.float32)


def tn(left, right):
    return lax.dot_general(left, right, (((0,), (0,)), ((), ())), preferred_element_type=jnp.float32)


def nn(left, right):
    return jnp.dot(left, right, preferred_element_type=jnp.float32)


MOVES = 3


def forward_kernel(
    plan, shard_qkv, shard_out, segments, levels, own_rows, own_target,
    d_full, x_out, w_out, q_out, k_out, v_out, factors_out, inverse_out, mixed_out,
    w_full, x_full, packed, received, received_target, labels, labels_there, pack, chosen,
    q_marked, k_marked, v_half, v_turned, factors, inverse, mixed,
    partial, target, from_core, from_chip, d_own,
    a2a_send, a2a_recv, send_sem, recv_sem, local_sem,
):
    me = my_place()
    z, x, y, a, c = me
    dp = lax.axis_index("dp")
    rows, width = own_target.shape
    group_rows = x_full.shape[0]
    other_chip, other_core = chip_partner(me), moved(me, C, 1)
    barrier = pltpu.get_barrier_semaphore()

    @pl.loop(1, 32)
    def _(k):
        pl.semaphore_signal(barrier, inc=1, device_id=device(dp_peer(me, k, 1)), device_id_type=MESH)

    for place in (other_chip, other_core):
        pl.semaphore_signal(barrier, inc=1, device_id=device(place), device_id_type=MESH)

    locals_started = []

    def local_copy(src, dst):
        copy = pltpu.make_async_copy(src, dst, local_sem.at[len(locals_started)])
        copy.start()
        locals_started.append(copy)
        return copy

    shards = [
        local_copy(shard_qkv.at[:, :, h * 3 * HD:(h + 1) * 3 * HD], w_full.at[h, z, x, y]) for h in range(HEADS)
    ] + [local_copy(shard_out, w_full.at[HEADS, z, x, y])]
    tile = width // MOVES

    def iota(shape, axis):
        return lax.broadcasted_iota(jnp.int32, shape, axis)

    def one_where(condition):
        return jnp.where(condition, 1.0, 0.0).astype(jnp.bfloat16)

    shards_of, groups = 4, 32
    group = dp + a * (1 - 2 * y)
    plan_half = plan[...].astype(jnp.float32).astype(jnp.bfloat16)
    before = one_where(iota((groups, groups), 0) < iota((groups, groups), 1))
    counts = nn(one_where(iota((8, groups * shards_of), 1) == dp * shards_of + a * 2 + c), plan_half).astype(jnp.bfloat16)
    starts = nn(counts, before).astype(jnp.bfloat16)
    to_group = iota((rows * CAP, groups), 1)
    to_group = to_group + a * (1 - 2 * (to_group & 1))
    here = one_where((iota((rows * CAP, groups), 0) >> 4) == to_group)
    of_row = iota((rows * CAP, 1), 0)
    which = ((of_row >> 3) & 1).astype(jnp.float32)
    source = (nt(here, starts)[:, 0:1] + which) * 8.0 + (of_row & 7).astype(jnp.float32)
    source = jnp.where(which < nt(here, counts)[:, 0:1], source, -1.0)
    pack[...] = one_where(iota((rows * CAP, rows), 1).astype(jnp.float32) == source)
    labels[:, 0:group_rows] = jnp.broadcast_to(segments[...], (8, group_rows))
    lane = iota((8, HD), 1)
    labels[:, group_rows:group_rows + HD] = jnp.where(lane == 0, levels[0:1, 0:1], jnp.where(lane == 1, levels[0:1, 1:2], 0))

    def fill(src, chunk):
        for low in range(chunk * tile, (chunk + 1) * tile, 512):
            blocks = nn(pack[...], src[:, low:low + 512]).astype(jnp.bfloat16)
            packed[:, :, low:low + 512] = blocks.reshape(packed.shape[0], packed.shape[1], 512)

    def block_copy(chunk, k):
        to = dp_peer(me, k, 1)
        dst = received_target if chunk == MOVES else received
        columns = slice(None) if chunk == MOVES else slice(chunk * tile, (chunk + 1) * tile)
        return pltpu.make_async_remote_copy(
            src_ref=packed.at[device(to)["dp"], :, columns],
            dst_ref=dst.at[dp, :, columns],
            send_sem=a2a_send.at[chunk, k],
            recv_sem=a2a_recv.at[chunk, k],
            device_id=device(to),
            device_id_type=MESH,
        )

    def own_block_copy(chunk):
        dst = received_target if chunk == MOVES else received
        columns = slice(None) if chunk == MOVES else slice(chunk * tile, (chunk + 1) * tile)
        return local_copy(packed.at[dp, :, columns], dst.at[dp, :, columns])

    fill(own_rows, 0)
    for copy in shards:
        copy.wait()
    pl.semaphore_wait(barrier, 33)

    copies = Copies(send_sem, recv_sem)
    across = copies.start(w_full.at[0:HEADS, z, x, y], w_full.at[0:HEADS, z, x, y], moved(me, Y, 1))
    labels_across = copies.start(labels, labels_there, moved(me, Y, 1))

    def near_out(half):
        columns = lambda which: pl.ds(0, 2 * HD) if which == half else pl.ds(2 * HD, HD)
        if half == 0:
            return lambda at, which: w_full.at[HEADS, at, x, y, 0, :, columns(which)]
        return lambda at, which: w_full.at[HEADS, z, at, y, 1, :, columns(which)]

    near_axis, far_axis = (Z, X), (X, Z)
    out_sent = [ring_gather_start(copies, me, near_axis[half], near_out(half)) for half in (0, 1)]
    own_blocks = []
    for chunk in range(MOVES):
        if chunk:
            fill(own_rows, chunk)

        @pl.loop(1, 32)
        def _(k):
            block_copy(chunk, k).start()

        own_blocks.append(own_block_copy(chunk))

    arriving = nn(
        one_where(iota((groups, groups * shards_of), 1) == iota((groups, groups * shards_of), 0) * shards_of + a * 2 + c), plan_half)
    arriving = jnp.where(iota((groups, groups), 1) == group, arriving, 0.0).astype(jnp.bfloat16)
    counts = nt(jnp.ones((8, groups), jnp.bfloat16), arriving).astype(jnp.bfloat16)
    starts = nn(counts, before).astype(jnp.bfloat16)
    there = one_where((iota((groups, rows * CAP), 1) >> 4) == iota((groups, rows * CAP), 0))
    of_column = iota((1, rows * CAP), 1)
    which = ((of_column >> 3) & 1).astype(jnp.float32)
    slot = nn(starts, there)[0:1, :] + which
    slot = jnp.where(which < nn(counts, there)[0:1, :], slot, -1.0)
    place = slot * 8.0 + (of_column & 7).astype(jnp.float32)
    chosen[...] = one_where(iota((rows, rows * CAP), 0).astype(jnp.float32) == place)

    def select(src, dst, at, chunk):
        for low in range(chunk * tile, (chunk + 1) * tile, 512):
            blocks = src[:, :, low:low + 512].reshape(rows * CAP, 512)
            dst[at, low:low + 512] = nn(chosen[...], blocks).astype(jnp.bfloat16)

    def near(half):
        if half == 0:
            return lambda at, which: w_full.at[0:HEADS, at, x, which, 0]
        return lambda at, which: w_full.at[0:HEADS, z, at, which, 1]

    def far(s, half):
        ys = pl.ds(y, 1) if s == HEADS else slice(None)
        if half == 0:
            return lambda at, which: w_full.at[s, pl.ds(2 * which, 2), at, ys, 0]
        return lambda at, which: w_full.at[s, at, pl.ds(2 * which, 2), ys, 1]

    across.wait_recv()
    sent = [ring_gather_start(copies, me, near_axis[half], near(half)) for half in (0, 1)]
    rest = [ring_gather_forward(copies, me, near_axis[half], near(half), sent[half]) for half in (0, 1)]
    for half in (0, 1):
        for copy in rest[half]:
            copy.wait_recv()

    far_sent = {}

    def far_start(s):
        far_sent[s] = [ring_gather_start(copies, me, far_axis[half], far(s, half)) for half in (0, 1)]

    def far_forward(s):
        far_sent[s] = [ring_gather_forward(copies, me, far_axis[half], far(s, half), far_sent[s][half]) for half in (0, 1)]

    def far_wait(s):
        for half in (0, 1):
            for copy in far_sent[s][half]:
                copy.wait_recv()

    out_rest = [ring_gather_forward(copies, me, near_axis[half], near_out(half), out_sent[half]) for half in (0, 1)]
    for half in (0, 1):
        for copy in out_rest[half]:
            copy.wait_recv()
    far_start(HEADS)
    far_start(0)

    def rows_of(place, chunk=0, chunks=1):
        step = rows // chunks
        return pl.ds(pl.multiple_of(device(place)["seq"] * rows + chunk * step, step), step)

    x_chip, x_core, x_passed = [], [], []

    def x_arrive(chunk):
        own_blocks[chunk].wait()

        @pl.loop(1, 32)
        def _(k):
            block_copy(chunk, k).wait_recv()

        at = rows_of(me)
        select(received, x_full, at, chunk)
        part = x_full.at[at, chunk * tile:(chunk + 1) * tile]
        x_chip.append(copies.start(part, part, other_chip))
        x_core.append(copies.start(part, part, other_core))

    def x_pass(chunk):
        x_chip[chunk].wait_recv()
        part = x_full.at[rows_of(other_chip), chunk * tile:(chunk + 1) * tile]
        x_passed.append(copies.start(part, part, other_core))

    x_arrive(0)
    far_start(1)

    labels_across.wait_recv()
    lane = iota((rows, HD), 1)
    for i in range(group_rows // rows):
        at = slice(i * rows, (i + 1) * rows)
        segment = jnp.where(a == 1, labels_there[0:1, at], labels[0:1, at]).astype(jnp.float32)
        sign = jnp.broadcast_to(2.0 * segment - 1.0, (HD, rows)).T
        mark_q = jnp.where(lane == 0, 64.0 * sign, jnp.where(lane == 1, -64.0, 0.0)).astype(jnp.bfloat16)
        mark_k = jnp.where(lane == 0, 32.0 * sign, jnp.where(lane == 1, 32.0, 0.0)).astype(jnp.bfloat16)
        for h in range(HEADS):
            q_marked[h, at, HD:2 * HD] = mark_q
            k_marked[h, at, HD:2 * HD] = mark_k

    def project(h, chip):
        @pl.loop(0, 2)
        def _(i):
            at = pl.ds(pl.multiple_of((chip * 2 + i) * rows, rows), rows)
            raw = nn(x_full[at, :], w_full[h].reshape(width, 3 * HD))
            for part, marked in ((0, q_marked), (1, k_marked)):
                values = raw[:, part * HD:(part + 1) * HD]
                factor = lax.rsqrt(jnp.mean(values * values, axis=-1, keepdims=True) + epsilon)
                marked[h, at, 0:HD] = (values * factor).astype(jnp.bfloat16)
                factors[part, h, at, :] = jnp.broadcast_to(factor, (rows, HD))
            values = raw[:, 2 * HD:3 * HD]
            v_half[h, at, :] = values.astype(jnp.bfloat16)
            v_turned[h, :, at] = values.T.astype(jnp.bfloat16)

    def attend(h, at):
        scores = nt(k_marked[h], q_marked[h, at, :])
        raised = jnp.exp2(scores * EXP2_SCALE)
        inverse_sum = 1.0 / jnp.sum(raised, axis=0, keepdims=True)
        turned = nn(v_turned[h], raised.astype(jnp.bfloat16)) * inverse_sum
        mixed[at, h * HD:(h + 1) * HD] = turned.T.astype(jnp.bfloat16)
        inverse[h, at, :] = jnp.broadcast_to(inverse_sum, (HD, rows)).T

    def attend_all(h):
        @pl.loop(0, group_rows // rows)
        def _(i):
            attend(h, pl.ds(pl.multiple_of(i * rows, rows), rows))

    x_arrive(1)
    x_pass(0)
    far_forward(HEADS)
    far_forward(0)
    far_wait(HEADS)
    traded = [
        copies.start(w_full.at[HEADS, :, :, y, half], w_full.at[HEADS, :, :, y, half], moved(me, Y, 1)) for half in (0, 1)]
    x_arrive(2)
    far_wait(0)
    far_start(2)
    far_forward(1)
    x_pass(1)
    for copy in x_core:
        copy.wait_recv()
    project(0, a)
    far_wait(1)
    project(1, a)
    far_forward(2)
    x_pass(2)
    for copy in x_passed:
        copy.wait_recv()
    outs = [local_copy(x_full, x_out)]
    project(0, 1 - a)
    attend_all(0)
    for chunk in range(MOVES):
        @pl.loop(1, 32)
        def _(k):
            block_copy(chunk, k).wait_send()

    for chunk in range(MOVES):
        fill(own_target, chunk)

    @pl.loop(1, 32)
    def _(k):
        block_copy(MOVES, k).start()

    own_block = own_block_copy(MOVES)
    project(1, 1 - a)
    attend_all(1)
    far_wait(2)
    project(2, a)
    project(2, 1 - a)
    for src, dst in ((q_marked, q_out), (k_marked, k_out), (v_half, v_out), (factors, factors_out)):
        outs.append(local_copy(src, dst))
    for copy in traded:
        copy.wait_recv()
    outs.append(local_copy(w_full.at[HEADS], w_out))

    def block(place):
        at = rows_of(place)
        attend(HEADS - 1, at)

        @pl.loop(0, 8)
        def _(t):
            weights = w_full[HEADS, t // 2, pl.ds(t % 2 * 2, 2)].reshape(3 * HD, OUT)
            columns = pl.ds(pl.multiple_of(t * 3 * HD, 3 * HD), 3 * HD)
            partial[at, columns] = nt(mixed[at, :], weights).astype(jnp.bfloat16)

    core_first, core_second, chip_sums = [], [], []
    step = rows // CHUNKS
    far_core = moved(other_chip, C, 1)
    block(far_core)
    for chunk in range(CHUNKS):
        core_first.append(copies.start(
            partial.at[rows_of(far_core, chunk, CHUNKS)], from_core.at[0, pl.ds(chunk * step, step)], other_core))
    block(other_chip)
    for chunk in range(CHUNKS):
        core_first[chunk].wait_recv()
        at = pl.ds(chunk * step, step)
        from_core[0, at] = (
            partial[rows_of(other_chip, chunk, CHUNKS)].astype(jnp.float32) + from_core[0, at].astype(jnp.float32)
        ).astype(jnp.bfloat16)
        chip_sums.append(copies.start(from_core.at[0, at], from_chip.at[at], other_chip))
    block(other_core)
    for chunk in range(CHUNKS):
        core_second.append(copies.start(
            partial.at[rows_of(other_core, chunk, CHUNKS)], from_core.at[1, pl.ds(chunk * step, step)], other_core))
    block(me)
    for src, dst in ((inverse, inverse_out), (mixed, mixed_out)):
        outs.append(local_copy(src, dst))

    own_block.wait()

    @pl.loop(1, 32)
    def _(k):
        block_copy(MOVES, k).wait_recv()

    for chunk in range(MOVES):
        select(received_target, target, slice(None), chunk)
    own_lanes = rows_of(me)
    segment = jnp.where(a == 1, labels_there[0:1, own_lanes], labels[0:1, own_lanes]).astype(jnp.float32)
    first, second = (
        jnp.where(a == 1, labels_there[0:1, at:at + 1], labels[0:1, at:at + 1]).astype(jnp.float32)
        for at in (group_rows, group_rows + 1))
    loss_scale = 1.0 / math.sqrt(group_rows * 32)
    weight = (jnp.where(segment == 0.0, first, second) / 8.0) * loss_scale
    weight = jnp.broadcast_to(weight, (HD, rows)).T[:, 0:1]

    to_chip, to_core, passed = [], [], []
    for chunk in range(CHUNKS):
        core_second[chunk].wait_recv()
        chip_sums[chunk].wait_recv()
        at = slice(chunk * step, (chunk + 1) * step)
        mine = rows_of(me, chunk, CHUNKS)
        prediction = (
            x_full[mine].astype(jnp.float32)
            + (partial[mine].astype(jnp.float32) + from_core[1, at].astype(jnp.float32) + from_chip[at].astype(jnp.float32))
        )
        d_own[at] = (weight[at] * (prediction - target[at].astype(jnp.float32))).astype(jnp.bfloat16)
        to_chip.append(copies.start(d_own.at[at], d_full.at[mine], other_chip))
        to_core.append(copies.start(d_own.at[at], d_full.at[mine], other_core))
    outs.append(local_copy(d_own, d_full.at[rows_of(me)]))
    for chunk in range(CHUNKS):
        to_chip[chunk].wait_recv()
        theirs = rows_of(other_chip, chunk, CHUNKS)
        passed.append(copies.start(d_full.at[theirs], d_full.at[theirs], other_core))
    for chunk in range(CHUNKS):
        to_core[chunk].wait_recv()
        passed[chunk].wait_recv()

    @pl.loop(1, 32)
    def _(k):
        block_copy(MOVES, k).wait_send()

    for copy in outs:
        copy.wait()
    copies.finish()


def forward(plan, shard_qkv, shard_out, segments, levels, own_rows, own_target):
    rows, width = own_target.shape
    group_rows = rows * 4
    blocks = (32, CAP * 8, width)
    vmem = pl.BlockSpec(memory_space=pltpu.VMEM)
    hbm = pl.BlockSpec(memory_space=pl.ANY)
    half, full = jnp.bfloat16, jnp.float32
    saved = [
        ((HEADS, group_rows, 2 * HD), half),
        ((HEADS, group_rows, 2 * HD), half),
        ((HEADS, group_rows, HD), half),
        ((2, HEADS, group_rows, HD), full),
        ((HEADS, group_rows, HD), full),
        ((group_rows, OUT), half),
    ]
    q_shape, k_shape, v_shape, factors_shape, inverse_shape, mixed_shape = saved
    scratch = [
        ((SLABS, 4, 4, 2, 2, 48, 3 * HD), half),
        ((group_rows, width), half),
        (blocks, half),
        (blocks, half),
        (blocks, half),
        ((8, group_rows + HD), jnp.int32),
        ((8, group_rows + HD), jnp.int32),
        ((rows * CAP, rows), half),
        ((rows, rows * CAP), half),
        q_shape,
        k_shape,
        v_shape,
        ((HEADS, HD, group_rows), half),
        factors_shape,
        inverse_shape,
        mixed_shape,
        ((group_rows, width), half),
        ((rows, width), half),
        ((2, rows, width), half),
        ((rows, width), half),
        ((rows, width), half),
    ]
    sems = 2 + 24 + 12 * SLABS + 2 + 3 * MOVES + 6 * CHUNKS
    return pl.pallas_call(
        forward_kernel,
        out_shape=tuple(
            jax.ShapeDtypeStruct(*shape)
            for shape in [((group_rows, width), half), ((group_rows, width), half), ((4, 4, 2, 2, 48, OUT), half)] + saved
        ),
        in_specs=[vmem] + [hbm] * 2 + [vmem] * 4,
        out_specs=(hbm,) * 9,
        scratch_shapes=[pltpu.VMEM(*shape) for shape in scratch] + [
            pltpu.SemaphoreType.DMA((MOVES + 1, 32)),
            pltpu.SemaphoreType.DMA((MOVES + 1, 32)),
            pltpu.SemaphoreType.DMA((sems,)),
            pltpu.SemaphoreType.DMA((sems,)),
            pltpu.SemaphoreType.DMA((20,)),
        ],
        compiler_params=pltpu.CompilerParams(collective_id=2, has_side_effects=True, vmem_limit_bytes=VMEM_LIMIT),
        name="forward_residual_gradient",
    )(
        plan.reshape(-1, plan.shape[2]), shard_qkv.reshape(2, 48, QKV), shard_out.reshape(2, 48, OUT),
        segments, levels, own_rows, own_target)


def added(*values):
    total = values[0].astype(jnp.float32)
    for value in values[1:]:
        total = total + value.astype(jnp.float32)
    return total


def reduce_start(copies, me, axis, block, got):
    up, down = moved(me, axis, 1), moved(me, axis, -1)
    opposite = moved(me, axis, 2)[axis]
    far_up = copies.start(block(opposite, 0), got(0), up)
    far_down = copies.start(block(opposite, 1), got(1), down)
    near_up = copies.start(block(up[axis], 1), got(2), up)
    near_down = copies.start(block(down[axis], 0), got(3), down)
    return far_up, far_down, near_up, near_down


def reduce_pass(copies, me, axis, block, got, sums, sent, add):
    up, down = moved(me, axis, 1), moved(me, axis, -1)
    sent[0].wait_recv()
    add(sums(0), [block(up[axis], 0), got(0)])
    sum_up = copies.start(sums(0), got(4), up)
    sent[1].wait_recv()
    add(sums(1), [block(down[axis], 1), got(1)])
    sum_down = copies.start(sums(1), got(5), down)
    return sent[2], sent[3], sum_up, sum_down


def reduce_end(me, axis, block, got, out, sent, add):
    sent[1].wait_recv()
    sent[2].wait_recv()
    add(out(0), [block(me[axis], 0), got(3), got(4)])
    sent[0].wait_recv()
    sent[3].wait_recv()
    add(out(1), [block(me[axis], 1), got(2), got(5)])


def add_rows(out, parts):
    lead = out.shape[:-2]
    count = math.prod(lead)

    @pl.loop(0, count)
    def _(i):
        index, rest = [], i
        for size in reversed(lead):
            index.insert(0, rest % size)
            rest = rest // size
        index = tuple(index)
        out[index] = added(*[part[index] for part in parts]).astype(out.dtype)


def backward_kernel(*refs):
    inputs, (qkv_sums, out_sums), held = refs[:9], refs[9:11], refs[11:20]
    d_full, x_full, w_out, q_marked, k_marked, v_half, factors, inverse, mixed = held
    (
        d_out, k_turned, dq, dk, dv, d_proj,
        grads, got_far, sum_far, half_far, got_near, sum_near, half_near, got_last, send_sem, recv_sem, local_sem,
    ) = refs[20:]
    loads = [pltpu.make_async_copy(inputs[i], held[i], local_sem.at[i]) for i in range(9)]
    for i in (0, 8, 2, 7, 4, 3, 5, 1, 6):
        loads[i].start()
    me = my_place()
    z, x, y, a, c = me
    greeted = greet([moved(me, Z, 1), moved(me, Z, -1), moved(me, X, 1), moved(me, X, -1), moved(me, Y, 1)])
    copies = Copies(send_sem, recv_sem)
    far_axis, near_axis = (X, Z), (Z, X)
    group_rows, width = x_full.shape
    rows = group_rows // 4
    scale = 1.0 / math.sqrt(HD)

    class Slab:
        def __init__(self, s):
            self.s = s

        def far_block(self, half):
            if half == 0:
                return lambda at, which: grads.at[self.s, pl.ds(2 * which, 2), at, :, 0]
            return lambda at, which: grads.at[self.s, at, pl.ds(2 * which, 2), :, 1]

        def near_block(self, half):
            return lambda at, which: half_far.at[self.s, half, at, which]

        def slots(self, ref, half):
            return lambda j: ref.at[self.s, half, j]

        def far_out(self, half):
            return lambda which: half_far.at[self.s, half, pl.ds(2 * which, 2)]

        def near_out(self, half):
            return lambda which: half_near.at[self.s, half, pl.ds(which, 1)]

        def far_start(self):
            self.sent = [
                reduce_start(copies, me, far_axis[h], self.far_block(h), self.slots(got_far, h)) for h in (0, 1)]

        def far_pass(self):
            self.sent = [
                reduce_pass(copies, me, far_axis[h], self.far_block(h), self.slots(got_far, h),
                            self.slots(sum_far, h), self.sent[h], add_rows)
                for h in (0, 1)]

        def near_start(self):
            for h in (0, 1):
                reduce_end(me, far_axis[h], self.far_block(h), self.slots(got_far, h), self.far_out(h), self.sent[h], add_rows)
            self.sent = [
                reduce_start(copies, me, near_axis[h], self.near_block(h), self.slots(got_near, h)) for h in (0, 1)]

        def near_pass(self):
            self.sent = [
                reduce_pass(copies, me, near_axis[h], self.near_block(h), self.slots(got_near, h),
                            self.slots(sum_near, h), self.sent[h], near_add)
                for h in (0, 1)]

        def last_start(self):
            for h in (0, 1):
                reduce_end(me, near_axis[h], self.near_block(h), self.slots(got_near, h), self.near_out(h), self.sent[h], near_add)
            self.sent = [
                copies.start(half_near.at[self.s, h, 1 - y], got_last.at[self.s, h], moved(me, Y, 1)) for h in (0, 1)]

        def end(self):
            for h in (0, 1):
                self.sent[h].wait_recv()
                total = added(half_near[self.s, h, y], got_last[self.s, h])
                if self.s == HEADS:
                    out_sums[h] = total
                else:
                    qkv_sums[h, :, self.s * 3 * HD:(self.s + 1) * 3 * HD] = total

    def near_add(out, parts):
        out[...] = added(*[part[...] for part in parts]).astype(out.dtype).reshape(out.shape)

    def weight_grads(s, left, right):
        @pl.loop(0, 8)
        def _(t):
            columns = pl.ds(pl.multiple_of(t * 384, 384), 384)
            term = tn(left[:, columns], right[...]).astype(jnp.bfloat16)
            grads[s, t // 2, pl.ds(t % 2 * 2, 2)] = term.reshape(2, 2, 2, 48, 384)

    def head(h):
        head_columns = slice(h * HD, (h + 1) * HD)

        @pl.loop(0, 4)
        def _(i):
            at = pl.ds(pl.multiple_of(i * rows, rows), rows)
            k_turned[:, at] = k_marked[h, at, 0:HD].astype(jnp.float32).T.astype(jnp.bfloat16)

        dk[...] = jnp.zeros_like(dk)
        dv[...] = jnp.zeros_like(dv)

        @pl.loop(0, 4)
        def _(i):
            at = pl.ds(pl.multiple_of(i * rows, rows), rows)
            raised = jnp.exp2(nt(k_marked[h], q_marked[h, at, :]) * EXP2_SCALE)
            d_here = d_out[at, head_columns]
            delta = jnp.sum((d_here.astype(jnp.float32) * mixed[at, head_columns].astype(jnp.float32)).T, axis=0, keepdims=True)
            d_scores = (raised * (nt(v_half[h], d_here) - delta)).astype(jnp.bfloat16)
            dv[...] += nn(raised.astype(jnp.bfloat16), d_here)
            dk[...] += nn(d_scores, q_marked[h, at, 0:HD])
            dq[at, :] = nn(k_turned[...], d_scores).T

        @pl.loop(0, 4)
        def _(i):
            at = pl.ds(pl.multiple_of(i * rows, rows), rows)
            for part, grad, marked in ((0, dq, q_marked), (1, dk, k_marked)):
                normed = marked[h, at, 0:HD].astype(jnp.float32)
                got = grad[at, :]
                inner = jnp.mean(got * normed, axis=-1, keepdims=True)
                d_proj[at, part * HD:(part + 1) * HD] = (
                    (factors[part, h, at, :] * scale) * (got - normed * inner)).astype(jnp.bfloat16)
            d_proj[at, 2 * HD:3 * HD] = dv[at, :].astype(jnp.bfloat16)

    out_slab = Slab(HEADS)
    slabs = [Slab(h) for h in range(HEADS)]
    loads[0].wait()
    loads[8].wait()
    weight_grads(HEADS, d_full, mixed)
    greeted()
    out_slab.far_start()
    for i in range(1, 8):
        loads[i].wait()

    @pl.loop(0, 4)
    def _(i):
        at = pl.ds(pl.multiple_of(i * rows, rows), rows)
        got = nn(d_full[at, :], w_out[...])
        for h in range(HEADS):
            d_out[at, h * HD:(h + 1) * HD] = (got[:, h * HD:(h + 1) * HD] * inverse[h, at, :]).astype(jnp.bfloat16)

    head(0)
    out_slab.far_pass()
    weight_grads(0, x_full, d_proj)
    slabs[0].far_start()
    out_slab.near_start()
    head(1)
    slabs[0].far_pass()
    out_slab.near_pass()
    weight_grads(1, x_full, d_proj)
    slabs[1].far_start()
    slabs[0].near_start()
    out_slab.last_start()
    head(2)
    slabs[1].far_pass()
    slabs[0].near_pass()
    out_slab.end()
    weight_grads(2, x_full, d_proj)
    slabs[2].far_start()
    slabs[1].near_start()
    slabs[0].last_start()
    slabs[2].far_pass()
    slabs[1].near_pass()
    slabs[0].end()
    slabs[2].near_start()
    slabs[1].last_start()
    slabs[2].near_pass()
    slabs[1].end()
    slabs[2].last_start()
    slabs[2].end()
    copies.finish()


def backward(d_full, x_full, w_out, q_marked, k_marked, v_half, factors, inverse, mixed):
    group_rows, width = x_full.shape
    inputs = (d_full, x_full, w_out.reshape(width, OUT), q_marked, k_marked, v_half, factors, inverse, mixed)
    half = lambda *lead: pltpu.VMEM((SLABS, 2, *lead, 48, 3 * HD), jnp.bfloat16)
    vmem = pl.BlockSpec(memory_space=pltpu.VMEM)
    qkv_sums, out_sums = pl.pallas_call(
        backward_kernel,
        out_shape=(
            jax.ShapeDtypeStruct((2, 48, QKV), jnp.float32),
            jax.ShapeDtypeStruct((2, 48, OUT), jnp.float32),
        ),
        in_specs=[pl.BlockSpec(memory_space=pl.ANY)] * 9,
        out_specs=(vmem, vmem),
        scratch_shapes=[pltpu.VMEM(value.shape, value.dtype) for value in inputs] + [
            pltpu.VMEM((group_rows, OUT), jnp.bfloat16),
            pltpu.VMEM((HD, group_rows), jnp.bfloat16),
            pltpu.VMEM((group_rows, HD), jnp.float32),
            pltpu.VMEM((group_rows, HD), jnp.float32),
            pltpu.VMEM((group_rows, HD), jnp.float32),
            pltpu.VMEM((group_rows, 3 * HD), jnp.bfloat16),
            pltpu.VMEM((SLABS, 4, 4, 2, 2, 48, 3 * HD), jnp.bfloat16),
            half(6, 2, 2),
            half(2, 2, 2),
            half(4, 2),
            half(6),
            half(2),
            half(2),
            half(),
            pltpu.SemaphoreType.DMA((26 * SLABS,)),
            pltpu.SemaphoreType.DMA((26 * SLABS,)),
            pltpu.SemaphoreType.DMA((9,)),
        ],
        compiler_params=pltpu.CompilerParams(collective_id=3, has_side_effects=True, vmem_limit_bytes=VMEM_LIMIT),
        name="backward_scatter",
    )(*inputs)
    return qkv_sums.reshape(96, QKV), out_sums.reshape(96, OUT)


def per_device(clip_rows, velocity_target, plan, segment_ids, reward_levels, w_qkv, w_out):
    return backward(*forward(plan, w_qkv, w_out, segment_ids, reward_levels, clip_rows, velocity_target))


def solution(mesh):
    return jax.shard_map(
        per_device,
        mesh=mesh,
        in_specs=(
            P(("dp", "seq"), None),
            P(("dp", "seq"), None),
            P(),
            P("dp", None),
            P("dp", None),
            P("dp", "seq"),
            P("dp", "seq"),
        ),
        out_specs=(P("dp", "seq"), P("dp", "seq")),
        check_vma=False,
    )
```
